128 devices in a mesh: site: 64 (over x, z, y_lo, core), row: 2 (over y_hi).
Axes of the slice: x: 4, y: 4 (y_hi: 2, y_lo: 2; y = y_hi * 2 + y_lo), z: 4, core: 2. Of those that a mesh axis runs over, the one named last changes fastest.
Arguments:
- tensors: bfloat16 [128, 128, 128, 2, 128], P('site', 'row'), may hold values from -40 to 40
- neighbours: int32 [128, 3], replicated, may hold values from -1 to 127, as said below
- edge_ranks: int32 [128], replicated, may hold values from 64 to 128, as said below
- gate_matrix: float32 [4, 4], replicated, may hold values from -1.2 to 1.2
- probes: float32 [512, 128], replicated, may hold values from -6 to 6
Outputs:
- new_tensors: bfloat16 [128, 128, 128, 2, 128], P('site', 'row')
- messages: float32 [128, 3, 128], P('site')
- new_bonds: float32 [128, 128], P('site')
The draws below stay inside these ranges and needn't reach their ends.
Inputs may be any that keep to these rules, and one draw needn't show every extreme that they name: neighbours[i, 0] = i - 1 and neighbours[i, 1] = i + 1, -1 past the ends; neighbours[i, 2] is the partner of site i under this layer's gates or -1; partners are mutual, and sites 4q and 4q + 1 pair only with sites 4q + 2 or 4q + 3. `edge_ranks`: the two sites of a gated pair carry the same rank.
All inputs are finite; a program needn't handle non-finite values.
Results may differ from the reference program's by a relative error of at most 0.0085.
Values may be sent and summed in bfloat16 or wider, within the bound.
No kernel may reach another device: no remote copies, remote signals or barrier semaphores. Data moves between devices by JAX's collectives and lax.ppermute only.
A program may use at most 192 MiB of HBM per device.

```python
import math
import jax
import jax.numpy as jnp
from jax import lax

BOND = 128
PHYS = 2
ROUNDS = 4
SWEEPS = 8
RANK_MIN = 64
SITES = 128


def graph_partners(key):
    local_key = jax.random.fold_in(key, 101)
    blocks = SITES // 4
    pattern = jax.random.randint(local_key, (blocks,), 0, 5)
    pattern = pattern.at[0].set(0)
    table = jnp.array([[2, 3, 0, 1], [3, -1, -1, 0], [2, -1, 0, -1], [-1, 3, -1, 1], [-1, -1, -1, -1]], jnp.int32)
    offsets = table[pattern]
    starts = (jnp.arange(blocks, dtype=jnp.int32) * 4)[:, None]
    return jnp.where(offsets >= 0, starts + offsets, -1).reshape(SITES).astype(jnp.int32)


def draw_neighbours(key, part):
    partner = graph_partners(key)
    site_ids = jnp.arange(SITES, dtype=jnp.int32)
    before = jnp.where(site_ids > 0, site_ids - 1, -1)
    beyond = jnp.where(site_ids < SITES - 1, site_ids + 1, -1)
    return jnp.stack([before, beyond, partner], axis=1).astype(jnp.int32)


def draw_edge_ranks(key, part):
    partner = graph_partners(key)
    site_ids = jnp.arange(SITES, dtype=jnp.int32)
    levels = jax.random.randint(jax.random.fold_in(key, 202), (SITES,), RANK_MIN, BOND + 1)
    levels = levels.at[0].set(BOND).at[1].set(RANK_MIN)
    left_ids = jnp.where(partner >= 0, jnp.minimum(site_ids, partner), site_ids)
    return levels[left_ids].astype(jnp.int32)


def draw_tensors(key, part):
    shape = (SITES, BOND, BOND, PHYS, BOND)
    spread = math.log(10.0) / 6.0
    coupling = 1.5
    core = jnp.clip(jax.random.normal(jax.random.fold_in(key, 303), shape, jnp.float32), -6.0, 6.0)
    bond_axis = jax.random.uniform(jax.random.fold_in(key, 304), (SITES + 1, BOND), jnp.float32, -1.0, 1.0)
    first_axis = bond_axis[:SITES]
    second_axis = bond_axis[1:]
    joint = jnp.exp(coupling * first_axis[:, :, None] * second_axis[:, None, :])
    joint = joint[:, :, :, None, None]
    third_scale = jnp.exp(jax.random.uniform(jax.random.fold_in(key, 306), (SITES, 1, 1, 1, BOND), jnp.float32, -spread, spread))
    leg_pair = jnp.exp(jax.random.uniform(jax.random.fold_in(key, 307), (SITES, 1, BOND, 1, BOND), jnp.float32, -2.3, 2.3))
    return jnp.clip(core * joint * third_scale * leg_pair, -40.0, 40.0).astype(jnp.bfloat16)


def draw_gate_matrix(key, part):
    diagonal = jax.random.uniform(jax.random.fold_in(key, 401), (4,), jnp.float32, 0.8, 1.2)
    offdiag = jax.random.uniform(jax.random.fold_in(key, 402), (4, 4), jnp.float32, -0.25, 0.25)
    return jnp.where(jnp.eye(4, dtype=bool), diagonal[None, :], offdiag).astype(jnp.float32)


def bell_draw(key, shape, deviation, bound, kind=jnp.bfloat16):
    drawn = jax.random.normal(key, shape, jnp.float32) * deviation
    return jnp.minimum(jnp.maximum(drawn, -bound), bound).astype(kind)


def setup_inputs(seed: int = 0) -> dict:
    keys = jax.random.split(jax.random.key(seed), 6)
    return {
        "tensors": draw_tensors(jax.random.fold_in(keys[5], 71), 0),
        "neighbours": draw_neighbours(jax.random.fold_in(keys[5], 71), 0),
        "edge_ranks": draw_edge_ranks(jax.random.fold_in(keys[5], 71), 0),
        "gate_matrix": draw_gate_matrix(jax.random.fold_in(keys[5], 71), 0),
        "probes": bell_draw(keys[4], (4 * BOND, BOND), 1.0, 6.0, jnp.float32),
    }


highest = lax.Precision.HIGHEST

def incoming(messages, neighbours, site_ids):
    bond_dim = messages.shape[-1]
    linked = neighbours[site_ids]
    safe_ids = jnp.maximum(linked, 0)
    backward = neighbours[safe_ids]
    select = (backward == site_ids[:, None, None]).astype(jnp.float32)
    picked = jnp.einsum('kij,kijb->kib', select, messages[safe_ids], precision=highest)
    return jnp.where(linked[:, :, None] < 0, jnp.float32(1.0) / bond_dim, picked)

def site_messages(squares, first_w, second_w, third_w):
    row_count, bond_dim = (squares.shape[0], squares.shape[1])
    third_b = third_w.astype(jnp.bfloat16)
    paired = (first_w[:, None] * second_w[None, :]).astype(jnp.bfloat16)
    flat_rows = squares.reshape(row_count * bond_dim, bond_dim)
    mixed_rows = jnp.dot(flat_rows, third_b, preferred_element_type=jnp.float32).reshape(row_count, bond_dim)
    toward_first = jnp.dot(mixed_rows, second_w, precision=highest)
    toward_second = jnp.dot(first_w, mixed_rows, precision=highest)
    toward_third = jnp.dot(paired.reshape(row_count * bond_dim), flat_rows, preferred_element_type=jnp.float32)
    return (toward_first, toward_second, toward_third)

def weight_rows(tensor, first_w, second_w):
    row_scale = jnp.sqrt(first_w[:, None] * second_w[None, :])
    return (tensor.astype(jnp.float32) * row_scale[:, :, None, None]).astype(jnp.bfloat16)

def gram_of(weighted):
    row_count, bond_dim = (weighted.shape[0], weighted.shape[1])
    flat_rows = weighted.reshape(row_count * bond_dim, 2 * bond_dim)
    return lax.dot_general(flat_rows, flat_rows, (((0,), (0,)), ((), ())), preferred_element_type=jnp.float32)

def root_pair(matrix):
    size = matrix.shape[0]
    ident = jnp.eye(size, dtype=jnp.float32)
    scale = jnp.sum(jnp.diagonal(matrix))
    current = matrix / scale
    partner_z = ident
    for sweep in range(SWEEPS):
        poly = 1.5 * ident - 0.5 * jnp.dot(partner_z, current, precision=highest)
        current = jnp.dot(current, poly, precision=highest)
        partner_z = jnp.dot(poly, partner_z, precision=highest)
    root_scale = jnp.sqrt(scale)
    return (current * root_scale, partner_z / root_scale)

def truncate(r_left, r_right, strength, kept_mask, gate_matrix, probes):
    wide_dim = r_left.shape[0]
    bond_dim = strength.shape[0]
    left_rows = r_left.reshape(2 * wide_dim, bond_dim) * strength[None, :]
    right_rows = r_right.reshape(2 * wide_dim, bond_dim)
    joined = jnp.dot(left_rows, right_rows.T, precision=highest).reshape(wide_dim, 2, wide_dim, 2)
    theta_mat = jnp.einsum('xyst,asbt->axby', gate_matrix.reshape(2, 2, 2, 2), joined, precision=highest)
    theta_mat = theta_mat.reshape(2 * wide_dim, 2 * wide_dim)
    sampled = jnp.dot(theta_mat, probes * kept_mask[None, :], precision=highest)
    inner_gram = jnp.dot(sampled.T, sampled, precision=highest) + jnp.diag(1.0 - kept_mask)
    inner_root, inner_inverse = root_pair(inner_gram)
    basis_cols = jnp.dot(sampled, inner_inverse, precision=highest)
    coeffs = jnp.dot(basis_cols.T, theta_mat, precision=highest)
    new_bond = jnp.sqrt(lax.optimization_barrier(jnp.mean(coeffs * coeffs, axis=1)) + 1e-06)
    right_new = coeffs / new_bond[:, None]
    left_target = basis_cols.reshape(wide_dim, 2 * bond_dim)
    right_target = right_new.reshape(bond_dim, wide_dim, 2).transpose(1, 2, 0).reshape(wide_dim, 2 * bond_dim)
    return (left_target, right_target, new_bond)

def apply_update(tensor, own_inverse, target):
    row_count, bond_dim = (tensor.shape[0], tensor.shape[1])
    change = jnp.dot(own_inverse, target, precision=highest)
    flat_rows = tensor.reshape(row_count * bond_dim, 2 * bond_dim)
    result = jnp.dot(flat_rows, change.astype(jnp.bfloat16), preferred_element_type=jnp.float32)
    return result.astype(jnp.bfloat16).reshape(tensor.shape)

def reference(tensors, neighbours, edge_ranks, gate_matrix, probes):
    site_count, bond_dim = (tensors.shape[0], tensors.shape[1])
    site_ids = jnp.arange(site_count, dtype=jnp.int32)

    def square_site(tensor):
        return lax.optimization_barrier(jnp.sum(jnp.square(tensor.astype(jnp.float32)), axis=2)).astype(jnp.bfloat16)
    squares = lax.map(square_site, tensors)
    messages = jnp.full((site_count, 3, bond_dim), 1.0 / bond_dim, jnp.float32)
    for round_index in range(ROUNDS):
        weights = incoming(messages, neighbours, site_ids)

        def one_site(operands):
            square_block, weight_set = operands
            return jnp.stack(site_messages(square_block, weight_set[0], weight_set[1], weight_set[2]))
        totals = lax.map(one_site, (squares, weights))
        messages = totals / lax.optimization_barrier(jnp.sum(totals, axis=-1, keepdims=True))
    weights = incoming(messages, neighbours, site_ids)

    def factor_site(operands):
        return root_pair(gram_of(weight_rows(operands[0], operands[1], operands[2])))
    uppers, inverses = lax.map(factor_site, (tensors, weights[:, 0], weights[:, 1]))

    def one_update(site):
        partner = neighbours[site, 2]
        safe_partner = jnp.where(partner < 0, site, partner)
        own_upper = uppers[site]
        other_upper = uppers[safe_partner]
        swapped = site > safe_partner
        r_left = jnp.where(swapped, other_upper, own_upper)
        r_right = jnp.where(swapped, own_upper, other_upper)
        left_id = jnp.minimum(site, safe_partner)
        right_id = jnp.maximum(site, safe_partner)
        strength = bond_dim * jnp.sqrt(messages[left_id, 2] * messages[right_id, 2])
        kept_mask = (jnp.arange(bond_dim, dtype=jnp.int32) < edge_ranks[left_id]).astype(jnp.float32)
        left_target, right_target, new_bond = truncate(r_left, r_right, strength, kept_mask, gate_matrix, probes)
        target = jnp.where(site < safe_partner, left_target, right_target)
        updated = apply_update(tensors[site], inverses[site], target)
        is_gated = partner >= 0
        return (jnp.where(is_gated, updated, tensors[site]), jnp.where(is_gated, new_bond, jnp.float32(0.0)))
    new_tensors, new_bonds = lax.map(one_update, site_ids)
    return (new_tensors, messages, new_bonds)
```

```python
import functools

import jax
import jax.numpy as jnp
from jax import lax
from jax.experimental import pallas as pl
from jax.experimental.pallas import tpu as pltpu
from jax.sharding import PartitionSpec as P

ROUNDS = 4
SWEEPS = 8
F32 = jnp.float32
BF16 = jnp.bfloat16
MB = 1 << 20
highest = lax.Precision.HIGHEST

CORE, ROW, MATE0, MATE1, FIRST, LAST, KEPT, RANK, GATED = range(9)


def smem():
    return pl.BlockSpec(memory_space=pltpu.SMEM)


def vmem():
    return pl.BlockSpec(memory_space=pltpu.VMEM)


def params(mib):
    return pltpu.CompilerParams(vmem_limit_bytes=mib * MB)


def cost(flops, moved):
    return pl.CostEstimate(flops=int(flops), bytes_accessed=int(moved), transcendentals=0)


def halves(value):
    high = value.astype(BF16)
    low = (value - high.astype(F32)).astype(BF16)
    return (high, low)


def dot_of(left, right, dims=((1,), (0,))):
    return lax.dot_general(left, right, (dims, ((), ())), preferred_element_type=F32)


def dot3(left, right, dims=((1,), (0,))):
    return dot_of(left[0], right[0], dims) + (
        dot_of(left[0], right[1], dims) + dot_of(left[1], right[0], dims)
    )


def dot_high(left, right, dims=((1,), (0,))):
    return lax.dot_general(left, right, (dims, ((), ())), preferred_element_type=F32, precision=highest)


def down(row):
    size = row.shape[-1]
    return jnp.transpose(jnp.broadcast_to(row, (size, size)))


def normalized(ref):
    rows = ref[...]
    return rows / jnp.sum(rows, axis=1, keepdims=True)


def incoming(info, own, mate, side):
    bond = own.shape[-1]
    flat = jnp.full((1, bond), 1.0 / bond, F32)
    zero = jnp.zeros((1, bond), F32)
    odd = info[CORE] == 1

    def row(rows, member, leg):
        return rows[3 * member + leg : 3 * member + leg + 1]

    def from_mate(place):
        return jnp.where(place == 0, row(mate, 0, 2), row(mate, 1, 2))

    mate0, mate1 = (info[MATE0], info[MATE1])
    up0 = row(mate, 1, 1) + jnp.where(mate0 == 1, row(mate, 1, 2), zero)
    first0 = jnp.where(odd, up0, jnp.where(info[FIRST] == 1, flat, row(side, 1, 1)))
    second0 = row(own, 1, 0)
    third0 = from_mate(mate0) + jnp.where(jnp.logical_and(odd, mate0 == 1), row(mate, 1, 1), zero)
    third0 = jnp.where(mate0 < 0, flat, third0)
    first1 = row(own, 0, 1)
    down1 = row(mate, 0, 0) + jnp.where(mate1 == 0, row(mate, 0, 2), zero)
    second1 = jnp.where(odd, jnp.where(info[LAST] == 1, flat, row(side, 0, 0)), down1)
    third1 = from_mate(mate1) + jnp.where(
        jnp.logical_and(jnp.logical_not(odd), mate1 == 0), row(mate, 0, 0), zero
    )
    third1 = jnp.where(mate1 < 0, flat, third1)
    return ((first0, second0, third0), (first1, second1, third1))


def split_kernel(x_ref, d_ref, s_ref, scratch):
    rows = x_ref.shape[1]
    bond = x_ref.shape[3]

    def body(index, carry):
        slot = scratch.at[index % 2]
        slot[...] = x_ref[0, index].astype(F32)
        even = slot[pl.ds(0, bond, 2), :]
        odd = slot[pl.ds(1, bond, 2), :]
        d_ref[0, index] = jnp.concatenate([even, odd], axis=1).astype(BF16)
        s_ref[0, index] = (even * even + odd * odd).astype(BF16)
        return carry

    lax.fori_loop(0, rows, body, 0, unroll=4)


def split_call(x):
    members, rows, wide, bond = x.shape
    block = 16
    return pl.pallas_call(
        split_kernel,
        grid=(members, rows // block),
        in_specs=[pl.BlockSpec((1, block, wide, bond), lambda m, i: (m, i, 0, 0))],
        out_specs=[
            pl.BlockSpec((1, block, bond, wide), lambda m, i: (m, i, 0, 0)),
            pl.BlockSpec((1, block, bond, bond), lambda m, i: (m, i, 0, 0)),
        ],
        out_shape=[
            jax.ShapeDtypeStruct((members, rows, bond, wide), BF16),
            jax.ShapeDtypeStruct((members, rows, bond, bond), BF16),
        ],
        scratch_shapes=[pltpu.VMEM((2, wide, bond), F32)],
        compiler_params=params(16),
        cost_estimate=cost(4 * x.size, 5 * x.size),
        name="split",
    )(x)


def round_kernel(info, own_ref, mate_ref, side_ref, s_ref, out_ref, first_ref, sums_ref):
    members, rows, bond = s_ref.shape[:3]
    weights = incoming(info, normalized(own_ref), normalized(mate_ref), normalized(side_ref))
    start = info[ROW] * rows
    out_ref[...] = jnp.ones(out_ref.shape, F32)
    for member in range(members):
        first, second, third = weights[member]
        third = third.astype(BF16).astype(F32)
        first_ref[...] = down(first)
        second_down = down(second)
        outer = second_down * third

        def body(index, total):
            block = s_ref[member, index].astype(F32)
            total = total + first_ref[pl.ds(start + index, 1), :] * block
            sums_ref[index] = jnp.sum((block * outer).reshape(bond // 8, 8, bond), axis=0)
            return total

        total = lax.fori_loop(0, rows, body, jnp.zeros((bond, bond), F32), unroll=4)
        ones = jnp.ones((8, bond), F32)
        half = dot_high(ones, jnp.sum(sums_ref[...], axis=1), ((1,), (1,)))[:1]
        empty = jnp.zeros_like(half)
        toward_first = jnp.where(
            info[ROW] == 0,
            jnp.concatenate([half, empty], axis=1),
            jnp.concatenate([empty, half], axis=1),
        )
        toward_second = dot_high(jnp.broadcast_to(third, (8, bond)), total, ((1,), (1,)))[:1]
        toward_third = jnp.sum(total * second_down, axis=0, keepdims=True)
        out_ref[pl.ds(3 * member, 1), :] = toward_first
        out_ref[pl.ds(3 * member + 1, 1), :] = toward_second
        out_ref[pl.ds(3 * member + 2, 1), :] = toward_third


def round_call(info, own, mate, side, squares):
    members, rows, bond = squares.shape[:3]
    return pl.pallas_call(
        round_kernel,
        in_specs=[smem(), vmem(), vmem(), vmem(), vmem()],
        out_specs=vmem(),
        out_shape=jax.ShapeDtypeStruct((8, bond), F32),
        scratch_shapes=[pltpu.VMEM((bond, bond), F32), pltpu.VMEM((rows, 8, bond), F32)],
        compiler_params=params(12),
        cost_estimate=cost(4 * squares.size, 2 * squares.size),
        name="message_round",
    )(info, own, mate, side, squares)


def gram_kernel(info, own_ref, mate_ref, side_ref, d_ref, keep_ref, send_ref, msg_ref, first_ref, second_ref, gram):
    member, step = (pl.program_id(0), pl.program_id(1))
    block, bond = d_ref.shape[1:3]
    rows = block * pl.num_programs(1)

    @pl.when(jnp.logical_and(member == 0, step == 0))
    def prepare():
        own = normalized(own_ref)
        weights = incoming(info, own, normalized(mate_ref), normalized(side_ref))
        for place in range(2):
            first_ref[place] = jnp.sqrt(down(weights[place][0]))
            second_ref[place] = jnp.sqrt(down(weights[place][1]))
            msg_ref[place] = own[3 * place : 3 * place + 3]

    start = info[ROW] * rows + step * block
    second = second_ref[member]
    parts = []
    for index in range(block):
        scale = first_ref[member, pl.ds(start + index, 1), :] * second
        piece = d_ref[0, index].astype(F32) * jnp.concatenate([scale, scale], axis=1)
        parts.append(piece.astype(BF16))
    weighted = jnp.concatenate(parts, axis=0)
    product = dot_of(weighted, weighted, ((0,), (0,)))

    @pl.when(step == 0)
    def begin():
        gram[...] = product

    @pl.when(step != 0)
    def add():
        gram[...] += product

    def put(ref):
        ref[0] = gram[:bond, :bond]
        ref[1] = gram[:bond, bond:]
        ref[2] = gram[bond:, bond:]

    last = step == pl.num_programs(1) - 1

    @pl.when(jnp.logical_and(last, member == info[KEPT]))
    def put_keep():
        put(keep_ref)

    @pl.when(jnp.logical_and(last, member != info[KEPT]))
    def put_send():
        put(send_ref)


def gram_call(info, own, mate, side, flat):
    members, rows, bond, wide = flat.shape
    block = 8
    upper = jax.ShapeDtypeStruct((3, bond, bond), F32)
    return pl.pallas_call(
        gram_kernel,
        grid=(members, rows // block),
        in_specs=[
            smem(),
            vmem(),
            vmem(),
            vmem(),
            pl.BlockSpec((1, block, bond, wide), lambda m, i: (m, i, 0, 0)),
        ],
        out_specs=[vmem(), vmem(), vmem()],
        out_shape=[upper, upper, jax.ShapeDtypeStruct((members, 3, bond), F32)],
        scratch_shapes=[
            pltpu.VMEM((members, bond, bond), F32),
            pltpu.VMEM((members, bond, bond), F32),
            pltpu.VMEM((wide, wide), F32),
        ],
        compiler_params=params(16),
        cost_estimate=cost(2 * wide * flat.size, 2 * flat.size),
        name="gram",
    )(info, own, mate, side, flat)


def eye_mask(size):
    down_index = lax.broadcasted_iota(jnp.int32, (size, size), 0)
    across_index = lax.broadcasted_iota(jnp.int32, (size, size), 1)
    return down_index == across_index


def root_pair(matrix):
    size = matrix.shape[0]
    diagonal = eye_mask(size)
    lift = jnp.where(diagonal, 1.5, 0.0).astype(F32)
    scale = jnp.sum(jnp.where(diagonal, matrix, 0.0), keepdims=True)
    current = matrix / scale
    poly = lift - 0.5 * current
    poly_parts = halves(poly)
    current = dot3(halves(current), poly_parts)
    partner = poly
    for _ in range(SWEEPS - 1):
        current_parts, partner_parts = (halves(current), halves(partner))
        poly_parts = halves(lift - 0.5 * dot3(partner_parts, current_parts))
        current = dot3(current_parts, poly_parts)
        partner = dot3(poly_parts, partner_parts)
    root_scale = jnp.sqrt(scale)
    return (current * root_scale, partner / root_scale)


def root_kernel(keep_ref, got_ref, upper_ref, inverse_ref):
    corner = keep_ref[0] + got_ref[0]
    above = keep_ref[1] + got_ref[1]
    below = keep_ref[2] + got_ref[2]
    matrix = jnp.concatenate(
        [
            jnp.concatenate([corner, above], axis=1),
            jnp.concatenate([jnp.transpose(above), below], axis=1),
        ],
        axis=0,
    )
    upper_ref[...], inverse_ref[...] = root_pair(matrix)


def root_call(keep, got):
    wide = 2 * keep.shape[1]
    full = jax.ShapeDtypeStruct((wide, wide), F32)
    return pl.pallas_call(
        root_kernel,
        in_specs=[vmem(), vmem()],
        out_specs=[vmem(), vmem()],
        out_shape=[full, full],
        compiler_params=params(16),
        cost_estimate=cost(66 * 2 * wide**3, 16 * wide * wide),
        name="root",
    )(keep, got)


def truncate_kernel(info, gate, own_ref, mate_ref, upper_ref, inverse_ref, other_ref, probes_ref, out_ref):
    wide, bond = (upper_ref.shape[0], probes_ref.shape[1])
    odd = info[CORE] == 1
    kept = info[KEPT]
    mate_place = jnp.maximum(jnp.where(kept == 0, info[MATE0], info[MATE1]), 0)
    own_msg = own_ref[pl.ds(3 * kept + 2, 1), :]
    mate_msg = mate_ref[pl.ds(3 * mate_place + 2, 1), :]
    own_msg = own_msg / jnp.sum(own_msg, axis=1, keepdims=True)
    mate_msg = mate_msg / jnp.sum(mate_msg, axis=1, keepdims=True)
    strength = bond * jnp.sqrt(own_msg * mate_msg)
    own_upper, other_upper = (upper_ref[...], other_ref[...])
    left = jnp.where(odd, other_upper, own_upper)
    right = jnp.where(odd, own_upper, other_upper)
    left_parts = halves(
        jnp.concatenate([left[:, :bond] * strength, left[:, bond:] * strength], axis=0)
    )
    right_parts = halves(jnp.concatenate([right[:, :bond], right[:, bond:]], axis=0))
    joined = dot3(left_parts, right_parts, ((1,), (1,)))
    joined_t = dot3(right_parts, left_parts, ((1,), (1,)))

    def quarter(value, down_half, across_half):
        return value[
            down_half * wide : (down_half + 1) * wide, across_half * wide : (across_half + 1) * wide
        ]

    def mixed(value, flipped):
        block_rows = []
        for out_down in range(2):
            blocks = []
            for out_across in range(2):
                out_first, out_second = (out_across, out_down) if flipped else (out_down, out_across)
                total = None
                for first in range(2):
                    for second in range(2):
                        piece = quarter(value, second, first) if flipped else quarter(value, first, second)
                        term = gate[2 * out_first + out_second, 2 * first + second] * piece
                        total = term if total is None else total + term
                blocks.append(total)
            block_rows.append(jnp.concatenate(blocks, axis=1))
        return jnp.concatenate(block_rows, axis=0)

    theta_parts = halves(mixed(joined, False))
    theta_t_parts = halves(mixed(joined_t, True))
    across = lax.broadcasted_iota(jnp.int32, (1, bond), 1)
    mask = (across < info[RANK]).astype(F32)
    probes = jnp.concatenate(
        [probes_ref[pl.ds(0, wide, 2), :], probes_ref[pl.ds(1, wide, 2), :]], axis=0
    )
    sampled_parts = halves(dot3(theta_parts, halves(probes * mask)))
    inner = dot3(sampled_parts, sampled_parts, ((0,), (0,)))
    inner = inner + jnp.where(eye_mask(bond), 1.0 - mask, 0.0)
    _, inner_inverse = root_pair(inner)
    basis = dot3(sampled_parts, halves(inner_inverse))
    coeffs_t = dot3(theta_t_parts, halves(basis))
    new_bond = jnp.sqrt(jnp.mean(coeffs_t * coeffs_t, axis=0, keepdims=True) + 1e-06)
    target = jnp.where(odd, coeffs_t / new_bond, basis)
    target = jnp.concatenate([target[:wide], target[wide:]], axis=1)
    change = dot3(halves(inverse_ref[...]), halves(target))
    gated = info[GATED] == 1
    identity = eye_mask(wide).astype(F32)
    out_ref[:wide] = jnp.where(gated, change, identity).astype(BF16)
    bond_parts = halves(jnp.where(gated, new_bond, 0.0))
    out_ref[wide:] = jnp.broadcast_to(jnp.concatenate(bond_parts, axis=1), (16, wide))


def truncate_call(info, gate, own, mate, upper, inverse, other, probes):
    wide = upper.shape[0]
    return pl.pallas_call(
        truncate_kernel,
        in_specs=[smem(), smem()] + [vmem()] * 6,
        out_specs=vmem(),
        out_shape=jax.ShapeDtypeStruct((wide + 16, wide), BF16),
        compiler_params=params(32),
        cost_estimate=cost(40 * 2 * wide**3, 24 * wide * wide),
        name="truncate",
    )(info, gate, own, mate, upper, inverse, other, probes)


def update_kernel(info, pack_ref, got_ref, d_ref, out_ref, bond_ref, scratch):
    member, step = (pl.program_id(0), pl.program_id(1))
    block, bond, wide = d_ref.shape[1:]
    kept = info[KEPT]

    @pl.when(jnp.logical_and(member == 0, step == 0))
    def bonds():
        tail = pack_ref[wide:].astype(F32)
        got = got_ref[wide:].astype(F32)
        mine = tail[:1, :bond] + tail[:1, bond:]
        other = got[:1, :bond] + got[:1, bond:]
        bond_ref[pl.ds(0, 1), :] = jnp.where(kept == 0, mine, other)
        bond_ref[pl.ds(1, 1), :] = jnp.where(kept == 0, other, mine)

    change = jnp.where(member == kept, pack_ref[:wide].astype(F32), got_ref[:wide].astype(F32)).astype(BF16)
    for index in range(block):
        result = dot_of(d_ref[0, index], change)
        slot = scratch.at[index % 2]
        slot[pl.ds(0, bond, 2), :] = result[:, :bond]
        slot[pl.ds(1, bond, 2), :] = result[:, bond:]
        out_ref[0, index] = slot[...].astype(BF16)


def update_call(info, pack, got, flat):
    members, rows, bond, wide = flat.shape
    block = 8
    return pl.pallas_call(
        update_kernel,
        grid=(members, rows // block),
        in_specs=[
            smem(),
            vmem(),
            vmem(),
            pl.BlockSpec((1, block, bond, wide), lambda m, i: (m, i, 0, 0)),
        ],
        out_specs=[pl.BlockSpec((1, block, wide, bond), lambda m, i: (m, i, 0, 0)), vmem()],
        out_shape=[
            jax.ShapeDtypeStruct((members, rows, wide, bond), BF16),
            jax.ShapeDtypeStruct((members, bond), F32),
        ],
        scratch_shapes=[pltpu.VMEM((2, wide, bond), F32)],
        compiler_params=params(16),
        cost_estimate=cost(2 * wide * flat.size, 4 * flat.size),
        name="update",
    )(info, pack, got, flat)


def scalars(neighbours, edge_ranks):
    device = lax.axis_index("site")
    row = lax.axis_index("row")
    core = device % 2
    base = device // 2 * 4
    block = lax.dynamic_slice(neighbours[:, 2], (base,), (4,))
    local = jnp.where(block < 0, -1, block - base)
    even0, even1 = (local[0], local[1])
    mate0 = jnp.where(core == 1, local[2], jnp.where(even0 < 0, -1, even0 - 2))
    mate1 = jnp.where(core == 1, local[3], jnp.where(even1 < 0, -1, even1 - 2))
    swap = jnp.logical_or(even0 == 3, even1 == 2).astype(jnp.int32)
    kept = jnp.where(core == 1, row ^ swap, row)
    rank = lax.dynamic_index_in_dim(edge_ranks, 2 * device + kept, keepdims=False)
    gated = jnp.where(kept == 0, mate0, mate1) >= 0
    first = device == 0
    last = device == lax.axis_size("site") - 1
    values = [core, row, mate0, mate1, first, last, kept, rank, gated]
    return jnp.stack([value.astype(jnp.int32) for value in values])


def shards(tensors, neighbours, edge_ranks, gate_matrix, probes):
    members, rows, bond, phys = tensors.shape[:4]
    sites = lax.axis_size("site")
    row_swap = [(0, 1), (1, 0)]
    core_swap = [(i, i ^ 1) for i in range(sites)]
    side_swap = [(i, i + 1) for i in range(1, sites - 1, 2)]
    side_swap += [(j, i) for i, j in side_swap]
    info = scalars(neighbours, edge_ranks)
    flat, squares = split_call(tensors.reshape(members, rows, bond * phys, bond))
    own = mate = side = jnp.ones((8, bond), F32)
    for _ in range(ROUNDS):
        part = round_call(info, own, mate, side, squares)
        own = part + lax.ppermute(part, "row", row_swap)
        side = lax.ppermute(own, "site", side_swap)
        mate = lax.ppermute(own, "site", core_swap)
    keep, send, messages = gram_call(info, own, mate, side, flat)
    got = lax.ppermute(send, "row", row_swap)
    upper, inverse = root_call(keep, got)
    other = lax.ppermute(upper, "site", core_swap)
    pack = truncate_call(info, gate_matrix, own, mate, upper, inverse, other, probes)
    got_pack = lax.ppermute(pack, "row", row_swap)
    updated, bonds = update_call(info, pack, got_pack, flat)
    return (updated.reshape(tensors.shape), messages, bonds)


def solution(mesh):
    return jax.shard_map(
        shards,
        mesh=mesh,
        in_specs=(P("site", "row", None, None, None), P(), P(), P(), P()),
        out_specs=(P("site", "row", None, None, None), P("site", None, None), P("site", None)),
        check_vma=False,
    )
```

```python
import functools

import jax
import jax.numpy as jnp
from jax import lax
from jax.experimental import pallas as pl
from jax.experimental.pallas import tpu as pltpu
from jax.sharding import PartitionSpec as P

ROUNDS = 4
SWEEPS = 8
F32 = jnp.float32
BF16 = jnp.bfloat16
MB = 1 << 20
highest = lax.Precision.HIGHEST

CORE, ROW, MATE0, MATE1, FIRST, LAST, KEPT, RANK, GATED = range(9)


def smem():
    return pl.BlockSpec(memory_space=pltpu.SMEM)


def vmem():
    return pl.BlockSpec(memory_space=pltpu.VMEM)


def params(mib):
    return pltpu.CompilerParams(vmem_limit_bytes=mib * MB)


def cost(flops, moved):
    return pl.CostEstimate(flops=int(flops), bytes_accessed=int(moved), transcendentals=0)


def halves(value):
    high = value.astype(BF16)
    low = (value - high.astype(F32)).astype(BF16)
    return (high, low)


def dot_of(left, right, dims=((1,), (0,))):
    return lax.dot_general(left, right, (dims, ((), ())), preferred_element_type=F32)


def dot3(left, right, dims=((1,), (0,))):
    return dot_of(left[0], right[0], dims) + (
        dot_of(left[0], right[1], dims) + dot_of(left[1], right[0], dims)
    )


def dot_high(left, right, dims=((1,), (0,))):
    return lax.dot_general(left, right, (dims, ((), ())), preferred_element_type=F32, precision=highest)


def down(row):
    size = row.shape[-1]
    return jnp.transpose(jnp.broadcast_to(row, (size, size)))


def normalized(ref):
    rows = ref[...]
    return rows / jnp.sum(rows, axis=1, keepdims=True)


def incoming(info, own, mate, side):
    bond = own.shape[-1]
    flat = jnp.full((1, bond), 1.0 / bond, F32)
    zero = jnp.zeros((1, bond), F32)
    odd = info[CORE] == 1

    def row(rows, member, leg):
        return rows[3 * member + leg : 3 * member + leg + 1]

    def from_mate(place):
        return jnp.where(place == 0, row(mate, 0, 2), row(mate, 1, 2))

    mate0, mate1 = (info[MATE0], info[MATE1])
    up0 = row(mate, 1, 1) + jnp.where(mate0 == 1, row(mate, 1, 2), zero)
    first0 = jnp.where(odd, up0, jnp.where(info[FIRST] == 1, flat, row(side, 1, 1)))
    second0 = row(own, 1, 0)
    third0 = from_mate(mate0) + jnp.where(jnp.logical_and(odd, mate0 == 1), row(mate, 1, 1), zero)
    third0 = jnp.where(mate0 < 0, flat, third0)
    first1 = row(own, 0, 1)
    down1 = row(mate, 0, 0) + jnp.where(mate1 == 0, row(mate, 0, 2), zero)
    second1 = jnp.where(odd, jnp.where(info[LAST] == 1, flat, row(side, 0, 0)), down1)
    third1 = from_mate(mate1) + jnp.where(
        jnp.logical_and(jnp.logical_not(odd), mate1 == 0), row(mate, 0, 0), zero
    )
    third1 = jnp.where(mate1 < 0, flat, third1)
    return ((first0, second0, third0), (first1, second1, third1))


def hbm():
    return pl.BlockSpec(memory_space=pltpu.HBM)


def write_scalars(near, ranks, info):
    device, row = (lax.axis_index("site"), lax.axis_index("row"))
    core = lax.rem(device, 2)
    base = 2 * (device - core)
    even0, even1 = (near[2, base] - base, near[2, base + 1] - base)
    odd0, odd1 = (near[2, base + 2], near[2, base + 3])
    odd = core == 1
    info[MATE0] = jnp.where(odd, jnp.where(odd0 < 0, -1, odd0 - base), jnp.maximum(even0 - 2, -1))
    info[MATE1] = jnp.where(odd, jnp.where(odd1 < 0, -1, odd1 - base), jnp.maximum(even1 - 2, -1))
    crossed = jnp.logical_or(even0 == 3, even1 == 2)
    kept = jnp.where(jnp.logical_and(odd, crossed), 1 - row, row)
    site = 2 * device + kept
    info[CORE] = core
    info[ROW] = row
    info[FIRST] = (device == 0).astype(jnp.int32)
    info[LAST] = (device == lax.axis_size("site") - 1).astype(jnp.int32)
    info[KEPT] = kept
    info[RANK] = ranks[site]
    info[GATED] = (near[2, site] >= 0).astype(jnp.int32)


def open_kernel(x_hbm, x_ref, s_ref, out_ref, scratch, sums_ref, total_ref, sems):
    members, rows, wide, bond = x_hbm.shape
    steps = sems.shape[0]
    per = steps // members
    block = rows // per

    def fetch(step):
        place = (step // per, pl.ds(lax.rem(step, per) * block, block))
        return pltpu.make_async_copy(x_hbm.at[place], x_ref.at[place], sems.at[step])

    for step in range(steps):
        fetch(step).start()
    total_ref[...] = jnp.zeros(total_ref.shape, F32)

    def body(step, carry):
        fetch(step).wait()
        member, start = (step // per, lax.rem(step, per) * block)
        total = total_ref[member]
        for index in range(block):
            lane = scratch.at[index % scratch.shape[0]]
            lane[...] = x_ref[member, start + index].astype(F32)
            even = lane[pl.ds(0, bond, 2), :]
            odd = lane[pl.ds(1, bond, 2), :]
            square = even * even + odd * odd
            s_ref[member, start + index] = square.astype(BF16)
            sums_ref[member, start + index] = jnp.sum(square.reshape(bond // 8, 8, bond), axis=0)
            total = total + square
        total_ref[member] = total
        return carry

    lax.fori_loop(0, steps, body, 0)
    row = lax.axis_index("row")
    flat_weight = jnp.ones((1, bond), F32)
    out_ref[...] = jnp.ones(out_ref.shape, F32)
    for member in range(members):
        finish(row, out_ref, member, sums_ref[member], total_ref[member], flat_weight, None)


def open_call(x):
    members, rows, wide, bond = x.shape
    block = 8
    steps = members * rows // block
    return pl.pallas_call(
        open_kernel,
        in_specs=[hbm()],
        out_specs=[vmem(), vmem(), vmem()],
        out_shape=[
            jax.ShapeDtypeStruct(x.shape, BF16),
            jax.ShapeDtypeStruct((members, rows, bond, bond), BF16),
            jax.ShapeDtypeStruct((8, bond), F32),
        ],
        scratch_shapes=[
            pltpu.VMEM((4, wide, bond), F32),
            pltpu.VMEM((members, rows, 8, bond), F32),
            pltpu.VMEM((members, bond, bond), F32),
            pltpu.SemaphoreType.DMA((steps,)),
        ],
        compiler_params=params(38),
        cost_estimate=cost(4 * x.size, 5 * x.size),
        name="open",
    )(x)


def flatten_kernel(after, x_ref, *refs, member):
    flat_ref, scratch = refs[-2:]
    rows, bond = flat_ref.shape[:2]
    if member == 0:
        write_scalars(*refs[:3])

    def body(index, carry):
        lane = scratch.at[lax.rem(index, scratch.shape[0])]
        lane[...] = x_ref[member, index].astype(F32)
        parts = [lane[pl.ds(place, bond, 2), :] for place in range(2)]
        flat_ref[index] = jnp.concatenate(parts, axis=1).astype(BF16)
        return carry

    lax.fori_loop(0, rows, body, 0, unroll=8)


def flatten_call(after, x, member, *tables):
    members, rows, wide, bond = x.shape
    flat = jax.ShapeDtypeStruct((rows, bond, wide), BF16)
    info = jax.ShapeDtypeStruct((16,), jnp.int32)
    return pl.pallas_call(
        functools.partial(flatten_kernel, member=member),
        in_specs=[pl.BlockSpec(memory_space=pl.ANY), vmem()] + [smem()] * len(tables),
        out_specs=[smem(), vmem()] if tables else [vmem()],
        out_shape=[info, flat] if tables else [flat],
        scratch_shapes=[pltpu.VMEM((8, wide, bond), F32)],
        compiler_params=params(8),
        cost_estimate=cost(x.size, 2 * x.size),
        name="flatten",
    )(after, x, *tables)


def finish(row_index, out_ref, member, sums, total, third, second_down):
    bond = total.shape[0]
    half = dot_high(jnp.ones((8, bond), F32), jnp.sum(sums, axis=1), ((1,), (1,)))[:1]
    empty = jnp.zeros_like(half)
    toward_first = jnp.where(
        row_index == 0,
        jnp.concatenate([half, empty], axis=1),
        jnp.concatenate([empty, half], axis=1),
    )
    toward_second = dot_high(jnp.broadcast_to(third, (8, bond)), total, ((1,), (1,)))[:1]
    weighted = total if second_down is None else total * second_down
    toward_third = jnp.sum(weighted, axis=0, keepdims=True)
    for leg, row in enumerate((toward_first, toward_second, toward_third)):
        out_ref[pl.ds(3 * member + leg, 1), :] = row


def round_kernel(info, own_ref, mate_ref, side_ref, s_ref, after, out_ref, first_ref, sums_ref):
    members, rows, bond = s_ref.shape[:3]
    group = 4
    weights = incoming(info, normalized(own_ref), normalized(mate_ref), normalized(side_ref))
    start = info[ROW] * rows
    out_ref[...] = jnp.ones(out_ref.shape, F32)
    heads = []
    for member in range(members):
        first, second, third = weights[member]
        third = third.astype(BF16).astype(F32)
        first_ref[member] = down(first)
        second_down = down(second)
        heads.append((third, second_down, (second_down * third).astype(BF16)))
    totals = []
    for member in range(members):
        outer = heads[member][2]

        def body(step, total):
            joined = None
            for place in range(group):
                index = step * group + place
                block = s_ref[member, index]
                scale = jnp.broadcast_to(first_ref[member, pl.ds(start + index, 1), :], (16, bond))
                scale = jnp.concatenate([scale.astype(BF16)] * (bond // 16), axis=0)
                term = scale * block
                joined = term if joined is None else joined + term
                piece = block * outer
                piece = piece[:64] + piece[64:]
                piece = (piece[:32] + piece[32:]).astype(F32)
                sums_ref[member, index] = (piece[:8] + piece[8:16]) + (piece[16:24] + piece[24:])
            return total + joined.astype(F32)

        totals.append(lax.fori_loop(0, rows // group, body, jnp.zeros((bond, bond), F32), unroll=2))
    for member in range(members):
        third, second_down, _ = heads[member]
        finish(info[ROW], out_ref, member, sums_ref[member], totals[member], third, second_down)


def round_call(info, own, mate, side, squares, after):
    members, rows, bond = squares.shape[:3]
    return pl.pallas_call(
        round_kernel,
        in_specs=[smem(), vmem(), vmem(), vmem(), vmem(), pl.BlockSpec(memory_space=pl.ANY)],
        out_specs=vmem(),
        out_shape=jax.ShapeDtypeStruct((8, bond), F32),
        scratch_shapes=[
            pltpu.VMEM((members, bond, bond), F32),
            pltpu.VMEM((members, rows, 8, bond), F32),
        ],
        compiler_params=params(12),
        cost_estimate=cost(4 * squares.size, 2 * squares.size),
        name="message_round",
    )(info, own, mate, side, squares, after)


def gram_kernel(info, own_ref, mate_ref, side_ref, d0_ref, d1_ref, keep_ref, send_ref, msg_ref, first_ref, second_ref, gram):
    members = 2
    rows, bond, wide = d0_ref.shape
    block = 32
    own = normalized(own_ref)
    weights = incoming(info, own, normalized(mate_ref), normalized(side_ref))
    for member in range(members):
        first_ref[member] = jnp.sqrt(down(weights[member][0]))
        second_ref[member] = jnp.sqrt(down(weights[member][1]))
        for leg in range(3):
            msg_ref[leg, pl.ds(member, 1), :] = own[3 * member + leg : 3 * member + leg + 1]
    gram[...] = jnp.zeros(gram.shape, F32)
    for member, d_ref in enumerate((d0_ref, d1_ref)):

        def body(step, carry):
            start = step * block
            second = second_ref[member]
            parts = []
            for index in range(block):
                scale = first_ref[member, pl.ds(info[ROW] * rows + start + index, 1), :] * second
                piece = d_ref[start + index].astype(F32) * jnp.concatenate([scale, scale], axis=1)
                parts.append(piece.astype(BF16))
            weighted = jnp.concatenate(parts, axis=0)
            gram[member] += dot_of(weighted, weighted, ((0,), (0,)))
            return carry

        lax.fori_loop(0, rows // block, body, 0)

    def put(ref, member):
        ref[0] = gram[member, :bond, :bond]
        ref[1] = gram[member, :bond, bond:]
        ref[2] = gram[member, bond:, bond:]

    put(keep_ref, info[KEPT])
    put(send_ref, 1 - info[KEPT])


def gram_call(info, own, mate, side, flats):
    members = len(flats)
    rows, bond, wide = flats[0].shape
    upper = jax.ShapeDtypeStruct((3, bond, bond), F32)
    return pl.pallas_call(
        gram_kernel,
        in_specs=[smem()] + [vmem()] * 5,
        out_specs=[vmem(), vmem(), vmem()],
        out_shape=[upper, upper, jax.ShapeDtypeStruct((3, members, bond), F32)],
        scratch_shapes=[
            pltpu.VMEM((members, bond, bond), F32),
            pltpu.VMEM((members, bond, bond), F32),
            pltpu.VMEM((members, wide, wide), F32),
        ],
        compiler_params=params(24),
        cost_estimate=cost(4 * wide * flats[0].size, 4 * flats[0].size),
        name="gram",
    )(info, own, mate, side, *flats)


def eye_mask(size):
    down_index = lax.broadcasted_iota(jnp.int32, (size, size), 0)
    across_index = lax.broadcasted_iota(jnp.int32, (size, size), 1)
    return down_index == across_index


def root_pair(matrix):
    size = matrix.shape[0]
    diagonal = eye_mask(size)
    lift = jnp.where(diagonal, 1.5, 0.0).astype(F32)
    scale = jnp.sum(jnp.where(diagonal, matrix, 0.0), keepdims=True)
    current = matrix / scale
    poly = lift - 0.5 * current
    poly_parts = halves(poly)
    current = dot3(halves(current), poly_parts)
    partner = poly
    for _ in range(SWEEPS - 1):
        current_parts, partner_parts = (halves(current), halves(partner))
        poly_parts = halves(lift - 0.5 * dot3(partner_parts, current_parts))
        current = dot3(current_parts, poly_parts)
        partner = dot3(poly_parts, partner_parts)
    root_scale = jnp.sqrt(scale)
    return (current * root_scale, partner / root_scale)


def root_kernel(keep_ref, got_ref, upper_ref, inverse_ref):
    corner = keep_ref[0] + got_ref[0]
    above = keep_ref[1] + got_ref[1]
    below = keep_ref[2] + got_ref[2]
    matrix = jnp.concatenate(
        [
            jnp.concatenate([corner, above], axis=1),
            jnp.concatenate([jnp.transpose(above), below], axis=1),
        ],
        axis=0,
    )
    upper_ref[...], inverse_ref[...] = root_pair(matrix)


def root_call(keep, got):
    wide = 2 * keep.shape[1]
    full = jax.ShapeDtypeStruct((wide, wide), F32)
    return pl.pallas_call(
        root_kernel,
        in_specs=[vmem(), vmem()],
        out_specs=[vmem(), vmem()],
        out_shape=[full, full],
        compiler_params=params(16),
        cost_estimate=cost(66 * 2 * wide**3, 16 * wide * wide),
        name="root",
    )(keep, got)


def truncate_kernel(info, gate, own_ref, mate_ref, upper_ref, inverse_ref, other_ref, probes_ref, out_ref):
    wide, bond = (upper_ref.shape[0], probes_ref.shape[1])
    odd = info[CORE] == 1
    kept = info[KEPT]
    mate_place = jnp.maximum(jnp.where(kept == 0, info[MATE0], info[MATE1]), 0)
    own_msg = own_ref[pl.ds(3 * kept + 2, 1), :]
    mate_msg = mate_ref[pl.ds(3 * mate_place + 2, 1), :]
    own_msg = own_msg / jnp.sum(own_msg, axis=1, keepdims=True)
    mate_msg = mate_msg / jnp.sum(mate_msg, axis=1, keepdims=True)
    strength = bond * jnp.sqrt(own_msg * mate_msg)
    own_upper, other_upper = (upper_ref[...], other_ref[...])
    left = jnp.where(odd, other_upper, own_upper)
    right = jnp.where(odd, own_upper, other_upper)
    left_parts = halves(
        jnp.concatenate([left[:, :bond] * strength, left[:, bond:] * strength], axis=0)
    )
    right_parts = halves(jnp.concatenate([right[:, :bond], right[:, bond:]], axis=0))
    joined = dot3(left_parts, right_parts, ((1,), (1,)))
    joined_t = dot3(right_parts, left_parts, ((1,), (1,)))

    def quarter(value, down_half, across_half):
        return value[
            down_half * wide : (down_half + 1) * wide, across_half * wide : (across_half + 1) * wide
        ]

    def mixed(value, flipped):
        block_rows = []
        for out_down in range(2):
            blocks = []
            for out_across in range(2):
                out_first, out_second = (out_across, out_down) if flipped else (out_down, out_across)
                total = None
                for first in range(2):
                    for second in range(2):
                        piece = quarter(value, second, first) if flipped else quarter(value, first, second)
                        term = gate[2 * out_first + out_second, 2 * first + second] * piece
                        total = term if total is None else total + term
                blocks.append(total)
            block_rows.append(jnp.concatenate(blocks, axis=1))
        return jnp.concatenate(block_rows, axis=0)

    theta_parts = halves(mixed(joined, False))
    theta_t_parts = halves(mixed(joined_t, True))
    across = lax.broadcasted_iota(jnp.int32, (1, bond), 1)
    mask = (across < info[RANK]).astype(F32)
    probes = jnp.concatenate(
        [probes_ref[pl.ds(0, wide, 2), :], probes_ref[pl.ds(1, wide, 2), :]], axis=0
    )
    sampled_parts = halves(dot3(theta_parts, halves(probes * mask)))
    inner = dot3(sampled_parts, sampled_parts, ((0,), (0,)))
    inner = inner + jnp.where(eye_mask(bond), 1.0 - mask, 0.0)
    _, inner_inverse = root_pair(inner)
    basis = dot3(sampled_parts, halves(inner_inverse))
    coeffs_t = dot3(theta_t_parts, halves(basis))
    new_bond = jnp.sqrt(jnp.mean(coeffs_t * coeffs_t, axis=0, keepdims=True) + 1e-06)
    target = jnp.where(odd, coeffs_t / new_bond, basis)
    target = jnp.concatenate([target[:wide], target[wide:]], axis=1)
    change = dot3(halves(inverse_ref[...]), halves(target))
    gated = info[GATED] == 1
    identity = eye_mask(wide).astype(F32)
    out_ref[:wide] = jnp.where(gated, change, identity).astype(BF16)
    bond_parts = halves(jnp.where(gated, new_bond, 0.0))
    out_ref[wide:] = jnp.broadcast_to(jnp.concatenate(bond_parts, axis=1), (16, wide))


def truncate_call(info, gate, own, mate, upper, inverse, other, probes):
    wide = upper.shape[0]
    return pl.pallas_call(
        truncate_kernel,
        in_specs=[smem(), smem()] + [vmem()] * 6,
        out_specs=vmem(),
        out_shape=jax.ShapeDtypeStruct((wide + 16, wide), BF16),
        compiler_params=params(32),
        cost_estimate=cost(40 * 2 * wide**3, 24 * wide * wide),
        name="truncate",
    )(info, gate, own, mate, upper, inverse, other, probes)


def update_kernel(info, pack_ref, got_ref, d0_ref, d1_ref, out_hbm, bond_ref, held, scratch, sems):
    rows, bond, wide = d0_ref.shape
    slots, block = held.shape[:2]
    per = rows // block
    kept = info[KEPT]
    tail = pack_ref[wide:].astype(F32)
    got = got_ref[wide:].astype(F32)
    mine = tail[:1, :bond] + tail[:1, bond:]
    other = got[:1, :bond] + got[:1, bond:]
    bond_ref[pl.ds(0, 1), :] = jnp.where(kept == 0, mine, other)
    bond_ref[pl.ds(1, 1), :] = jnp.where(kept == 0, other, mine)

    def put(member, step):
        slot = lax.rem(member * per + step, slots)
        target = out_hbm.at[member, pl.ds(step * block, block)]
        return pltpu.make_async_copy(held.at[slot], target, sems.at[slot])

    for member, d_ref in enumerate((d0_ref, d1_ref)):
        change = jnp.where(member == kept, pack_ref[:wide].astype(F32), got_ref[:wide].astype(F32)).astype(BF16)

        def body(step, carry):
            start = step * block
            slot = lax.rem(member * per + step, slots)

            @pl.when(member * per + step >= slots)
            def free():
                put(member, step).wait()

            result = dot_of(d_ref[pl.ds(start, block)].reshape(block * bond, wide), change)
            for index in range(block):
                lane = scratch.at[index % scratch.shape[0]]
                piece = result[index * bond : (index + 1) * bond]
                lane[pl.ds(0, bond, 2), :] = piece[:, :bond]
                lane[pl.ds(1, bond, 2), :] = piece[:, bond:]
                held[slot, index] = lane[...].astype(BF16)
            put(member, step).start()
            return carry

        lax.fori_loop(0, per, body, 0)
    for step in range(per - slots, per):
        put(1, step).wait()


def update_call(info, pack, got, flats):
    members = len(flats)
    rows, bond, wide = flats[0].shape
    block, slots = (16, 4)
    return pl.pallas_call(
        update_kernel,
        in_specs=[smem()] + [vmem()] * 4,
        out_specs=[hbm(), vmem()],
        out_shape=[
            jax.ShapeDtypeStruct((members, rows, wide, bond), BF16),
            jax.ShapeDtypeStruct((members, bond), F32),
        ],
        scratch_shapes=[
            pltpu.VMEM((slots, block, wide, bond), BF16),
            pltpu.VMEM((4, wide, bond), F32),
            pltpu.SemaphoreType.DMA((slots,)),
        ],
        compiler_params=params(24),
        cost_estimate=cost(4 * wide * flats[0].size, 8 * flats[0].size),
        name="update",
    )(info, pack, got, *flats)


def shards(tensors, neighbours, edge_ranks, gate_matrix, probes):
    members, rows, bond, phys = tensors.shape[:4]
    sites = lax.axis_size("site")
    row_swap = [(0, 1), (1, 0)]
    core_swap = [(i, i ^ 1) for i in range(sites)]
    side_swap = [(i, i + 1) for i in range(1, sites - 1, 2)]
    side_swap += [(j, i) for i, j in side_swap]
    x = tensors.reshape(members, rows, bond * phys, bond)
    x, squares, part = open_call(x)
    for index in range(ROUNDS):
        if index > 0:
            part = round_call(info, own, mate, side, squares, flats[-1])
        if index == 0:
            info, *flats = flatten_call(part, x, index, neighbours.T, edge_ranks)
        elif index < members:
            flats += flatten_call(part, x, index)
        own = part + lax.ppermute(part, "row", row_swap)
        side = lax.ppermute(own, "site", side_swap)
        mate = lax.ppermute(own, "site", core_swap)
    keep, send, messages = gram_call(info, own, mate, side, flats)
    got = lax.ppermute(send, "row", row_swap)
    upper, inverse = root_call(keep, got)
    other = lax.ppermute(upper, "site", core_swap)
    pack = truncate_call(info, gate_matrix, own, mate, upper, inverse, other, probes)
    got_pack = lax.ppermute(pack, "row", row_swap)
    updated, bonds = update_call(info, pack, got_pack, flats)
    return (updated.reshape(tensors.shape), messages.transpose(1, 0, 2), bonds)


def solution(mesh):
    return jax.shard_map(
        shards,
        mesh=mesh,
        in_specs=(P("site", "row", None, None, None), P(), P(), P(), P()),
        out_specs=(P("site", "row", None, None, None), P("site", None, None), P("site", None)),
        check_vma=False,
    )
```

```python
import functools

import jax
import jax.numpy as jnp
from jax import lax
from jax.experimental import pallas as pl
from jax.experimental.pallas import tpu as pltpu
from jax.sharding import PartitionSpec as P

ROUNDS = 4
SWEEPS = 8
F32 = jnp.float32
BF16 = jnp.bfloat16
MB = 1 << 20
highest = lax.Precision.HIGHEST

CORE, ROW, MATE0, MATE1, FIRST, LAST, KEPT, RANK, GATED = range(9)


def smem():
    return pl.BlockSpec(memory_space=pltpu.SMEM)


def vmem():
    return pl.BlockSpec(memory_space=pltpu.VMEM)


def params(mib):
    return pltpu.CompilerParams(vmem_limit_bytes=mib * MB)


def cost(flops, moved):
    return pl.CostEstimate(flops=int(flops), bytes_accessed=int(moved), transcendentals=0)


def halves(value):
    high = value.astype(BF16)
    low = (value - high.astype(F32)).astype(BF16)
    return (high, low)


def dot_of(left, right, dims=((1,), (0,))):
    return lax.dot_general(left, right, (dims, ((), ())), preferred_element_type=F32)


def dot3(left, right, dims=((1,), (0,))):
    return dot_of(left[0], right[0], dims) + (
        dot_of(left[0], right[1], dims) + dot_of(left[1], right[0], dims)
    )


def dot_high(left, right, dims=((1,), (0,))):
    return lax.dot_general(left, right, (dims, ((), ())), preferred_element_type=F32, precision=highest)


def down(row):
    size = row.shape[-1]
    return jnp.transpose(jnp.broadcast_to(row, (size, size)))


def normalized(ref):
    rows = ref[...]
    return rows / jnp.sum(rows, axis=1, keepdims=True)


def pick(rows, member, leg):
    return rows[3 * member + leg : 3 * member + leg + 1]


def level(rows):
    return jnp.full((1, rows.shape[-1]), 1.0 / rows.shape[-1], F32)


def from_mate(mate, place):
    return jnp.where(place == 0, pick(mate, 0, 2), pick(mate, 1, 2))


def inner_incoming(info, own, mate):
    odd = info[CORE] == 1
    place = jnp.where(odd, info[MATE0], info[MATE1])
    joined = place == info[CORE]
    chain = jnp.where(odd, pick(mate, 1, 1), pick(mate, 0, 0))
    gated = jnp.where(odd, pick(mate, 1, 2), pick(mate, 0, 2))
    near = chain + jnp.where(joined, gated, 0.0)
    home = jnp.where(odd, pick(own, 1, 0), pick(own, 0, 1))
    third = from_mate(mate, place) + jnp.where(joined, chain, 0.0)
    return (
        jnp.where(odd, near, home),
        jnp.where(odd, home, near),
        jnp.where(place < 0, level(own), third),
    )


def outer_known(info, own, mate):
    odd = info[CORE] == 1
    place = jnp.where(odd, info[MATE1], info[MATE0])
    home = jnp.where(odd, pick(own, 0, 1), pick(own, 1, 0))
    return (home, jnp.where(place < 0, level(own), from_mate(mate, place)))


def outer_far(info, side):
    far = jnp.where(info[CORE] == 1, pick(side, 0, 0), pick(side, 1, 1))
    return jnp.where(info[FIRST] + info[LAST] > 0, level(side), far)


def outer_incoming(info, own, mate, side):
    odd = info[CORE] == 1
    home, third = outer_known(info, own, mate)
    far = outer_far(info, side)
    return (jnp.where(odd, home, far), jnp.where(odd, far, home), third)


def hbm():
    return pl.BlockSpec(memory_space=pltpu.HBM)


def anywhere():
    return pl.BlockSpec(memory_space=pl.ANY)


def write_scalars(near, ranks, info):
    device, row = (lax.axis_index("site"), lax.axis_index("row"))
    core = lax.rem(device, 2)
    base = 2 * (device - core)
    even0, even1 = (near[2, base] - base, near[2, base + 1] - base)
    odd0, odd1 = (near[2, base + 2], near[2, base + 3])
    odd = core == 1
    info[MATE0] = jnp.where(odd, jnp.where(odd0 < 0, -1, odd0 - base), jnp.maximum(even0 - 2, -1))
    info[MATE1] = jnp.where(odd, jnp.where(odd1 < 0, -1, odd1 - base), jnp.maximum(even1 - 2, -1))
    crossed = jnp.logical_or(even0 == 3, even1 == 2)
    kept = jnp.where(jnp.logical_and(odd, crossed), 1 - row, row)
    site = 2 * device + kept
    info[CORE] = core
    info[ROW] = row
    info[FIRST] = (device == 0).astype(jnp.int32)
    info[LAST] = (device == lax.axis_size("site") - 1).astype(jnp.int32)
    info[KEPT] = kept
    info[RANK] = ranks[site]
    info[GATED] = (near[2, site] >= 0).astype(jnp.int32)


def open_kernel(x_hbm, x_ref, s_ref, out_ref, scratch, sums_ref, total_ref, sems):
    members, rows, wide, bond = x_hbm.shape
    steps = sems.shape[0]
    per = steps // members
    block = rows // per

    def fetch(step):
        place = (step // per, pl.ds(lax.rem(step, per) * block, block))
        return pltpu.make_async_copy(x_hbm.at[place], x_ref.at[place], sems.at[step])

    for step in range(steps):
        fetch(step).start()
    total_ref[...] = jnp.zeros(total_ref.shape, F32)

    def body(step, carry):
        fetch(step).wait()
        member, start = (step // per, lax.rem(step, per) * block)
        total = total_ref[member]
        for index in range(block):
            lane = scratch.at[index % scratch.shape[0]]
            lane[...] = x_ref[member, start + index].astype(F32)
            even = lane[pl.ds(0, bond, 2), :]
            odd = lane[pl.ds(1, bond, 2), :]
            square = even * even + odd * odd
            s_ref[member, start + index] = square.astype(BF16)
            sums_ref[member, start + index] = jnp.sum(square.reshape(bond // 8, 8, bond), axis=0)
            total = total + square
        total_ref[member] = total
        return carry

    lax.fori_loop(0, steps, body, 0)
    row = lax.axis_index("row")
    flat_weight = jnp.ones((1, bond), F32)
    out_ref[...] = jnp.ones(out_ref.shape, F32)
    for member in range(members):
        finish(row, out_ref, member, sums_ref[member], total_ref[member], flat_weight, None)


def open_call(x):
    members, rows, wide, bond = x.shape
    block = 8
    steps = members * rows // block
    return pl.pallas_call(
        open_kernel,
        in_specs=[hbm()],
        out_specs=[vmem(), vmem(), vmem()],
        out_shape=[
            jax.ShapeDtypeStruct(x.shape, BF16),
            jax.ShapeDtypeStruct((members, rows, bond, bond), BF16),
            jax.ShapeDtypeStruct((8, bond), F32),
        ],
        scratch_shapes=[
            pltpu.VMEM((4, wide, bond), F32),
            pltpu.VMEM((members, rows, 8, bond), F32),
            pltpu.VMEM((members, bond, bond), F32),
            pltpu.SemaphoreType.DMA((steps,)),
        ],
        compiler_params=params(38),
        cost_estimate=cost(4 * x.size, 5 * x.size),
        name="open",
    )(x)


def flatten_kernel(after, x_ref, *refs, member):
    flat_ref, scratch = refs[-2:]
    rows, bond = flat_ref.shape[1:3]
    if member == 0:
        write_scalars(*refs[:3])

    def body(index, carry):
        lane = scratch.at[lax.rem(index, scratch.shape[0])]
        lane[...] = x_ref[member, index].astype(F32)
        parts = [lane[pl.ds(place, bond, 2), :] for place in range(2)]
        flat_ref[member, index] = jnp.concatenate(parts, axis=1).astype(BF16)
        return carry

    lax.fori_loop(0, rows, body, 0, unroll=8)


def flatten_call(after, x, member, *more):
    members, rows, wide, bond = x.shape
    flat = jax.ShapeDtypeStruct((members, rows, bond, wide), BF16)
    info = jax.ShapeDtypeStruct((16,), jnp.int32)
    first = member == 0
    return pl.pallas_call(
        functools.partial(flatten_kernel, member=member),
        in_specs=[anywhere(), vmem()] + ([smem(), smem()] if first else [vmem()]),
        out_specs=[smem(), vmem()] if first else vmem(),
        out_shape=[info, flat] if first else flat,
        input_output_aliases={} if first else {2: 0},
        scratch_shapes=[pltpu.VMEM((8, wide, bond), F32)],
        compiler_params=params(8),
        cost_estimate=cost(x.size, 2 * x.size),
        name="flatten",
    )(after, x, *more)


def halved(row_index, row):
    half = row.shape[1] // 2
    return jnp.where(row_index == 0, row[:, :half], row[:, half:])


def placed(row_index, half):
    empty = jnp.zeros_like(half)
    return jnp.where(
        row_index == 0,
        jnp.concatenate([half, empty], axis=1),
        jnp.concatenate([empty, half], axis=1),
    )


def by_row(row, matrix):
    return dot_high(jnp.broadcast_to(row, (8, row.shape[1])), matrix)[:1]


def by_column(row, matrix):
    return dot_high(jnp.broadcast_to(row, (8, row.shape[1])), matrix, ((1,), (1,)))[:1]


def put_leg(out_ref, member, leg, row):
    out_ref[pl.ds(3 * member + leg, 1), :] = row


def finish(row_index, out_ref, member, sums, total, third, second_down):
    bond = total.shape[0]
    half = by_column(jnp.ones((1, bond), F32), jnp.sum(sums, axis=1))
    weighted = total if second_down is None else total * second_down
    put_leg(out_ref, member, 0, placed(row_index, half))
    put_leg(out_ref, member, 1, by_column(third, total))
    put_leg(out_ref, member, 2, jnp.sum(weighted, axis=0, keepdims=True))


GROUP = 4


def scaled_sum(s_ref, member, step, first_ref, start):
    bond = s_ref.shape[2]
    joined = None
    for place in range(GROUP):
        index = step * GROUP + place
        scale = jnp.broadcast_to(first_ref[pl.ds(start + index, 1), :], (16, bond)).astype(BF16)
        term = jnp.concatenate([scale] * (bond // 16), axis=0) * s_ref[member, index]
        joined = term if joined is None else joined + term
    return joined.astype(F32)


def contract_inner(info, weights, s_ref, out_ref, first_ref, sums_ref):
    rows, bond = s_ref.shape[1:3]
    member = 1 - info[CORE]
    start = info[ROW] * rows
    first, second, third = weights
    third = third.astype(BF16).astype(F32)
    first_ref[...] = down(first)
    second_down = down(second)
    outer = (second_down * third).astype(BF16)

    def body(step, total):
        for place in range(GROUP):
            index = step * GROUP + place
            piece = s_ref[member, index] * outer
            piece = piece[:64] + piece[64:]
            piece = (piece[:32] + piece[32:]).astype(F32)
            sums_ref[index] = (piece[:8] + piece[8:16]) + (piece[16:24] + piece[24:])
        return total + scaled_sum(s_ref, member, step, first_ref, start)

    total = lax.fori_loop(0, rows // GROUP, body, jnp.zeros((bond, bond), F32), unroll=2)
    finish(info[ROW], out_ref, member, sums_ref[...], total, third, second_down)


def contract_outer(info, home, third, s_ref, out_ref, mixed_ref, other_ref, first_ref):
    rows, bond = s_ref.shape[1:3]
    member = info[CORE]
    odd = info[CORE] == 1
    start = info[ROW] * rows
    third_rows = jnp.broadcast_to(third.astype(BF16), (8, bond))

    def mix(step, carry):
        pair = s_ref[member, pl.ds(2 * step, 2)].reshape(2 * bond, bond)
        product = dot_of(third_rows, pair, ((1,), (1,)))
        mixed_ref[pl.ds(2 * step, 1), :] = product[:1, :bond]
        mixed_ref[pl.ds(2 * step + 1, 1), :] = product[:1, bond:]
        return carry

    lax.fori_loop(0, rows // 2, mix, 0, unroll=8)

    @pl.when(odd)
    def over_first():
        first_ref[...] = down(home)

        def body(step, total):
            return total + scaled_sum(s_ref, member, step, first_ref, start)

        zero = jnp.zeros((bond, bond), F32)
        other_ref[...] = lax.fori_loop(0, rows // GROUP, body, zero, unroll=2)
        put_leg(out_ref, member, 1, by_row(halved(info[ROW], home), mixed_ref[...]))

    @pl.when(jnp.logical_not(odd))
    def over_second():
        second_rows = jnp.concatenate(halves(home) + (jnp.zeros((6, bond), BF16),), axis=0)

        def body(step, carry):
            pair = jnp.concatenate([s_ref[member, 2 * step], s_ref[member, 2 * step + 1]], axis=1)
            product = dot_of(second_rows, pair)
            product = product[:1] + product[1:2]
            other_ref[pl.ds(2 * step, 1), :] = product[:, :bond]
            other_ref[pl.ds(2 * step + 1, 1), :] = product[:, bond:]
            return carry

        lax.fori_loop(0, rows // 2, body, 0, unroll=8)
        put_leg(out_ref, member, 0, placed(info[ROW], by_column(home, mixed_ref[...])))


def inner_kernel(info, own_ref, mate_ref, s_ref, after, out_ref, mixed_ref, other_ref, first_ref, sums_ref):
    own, mate = (normalized(own_ref), normalized(mate_ref))
    out_ref[...] = jnp.ones(out_ref.shape, F32)
    contract_inner(info, inner_incoming(info, own, mate), s_ref, out_ref, first_ref, sums_ref)
    home, third = outer_known(info, own, mate)
    contract_outer(info, home, third, s_ref, out_ref, mixed_ref, other_ref, first_ref)


def outer_kernel(info, side_ref, part_ref, mixed_ref, other_ref, out_ref):
    rows = mixed_ref.shape[0]
    far = outer_far(info, normalized(side_ref))
    out_ref[...] = part_ref[...]

    @pl.when(info[CORE] == 1)
    def as_second():
        put_leg(out_ref, 1, 0, placed(info[ROW], by_column(far, mixed_ref[...])))
        put_leg(out_ref, 1, 2, by_row(far, other_ref[...]))

    @pl.when(info[CORE] == 0)
    def as_first():
        half = halved(info[ROW], far)
        put_leg(out_ref, 0, 1, by_row(half, mixed_ref[...]))
        put_leg(out_ref, 0, 2, by_row(half, other_ref[:rows]))


def inner_call(info, own, mate, squares, after):
    rows, bond = squares.shape[1:3]
    return pl.pallas_call(
        inner_kernel,
        in_specs=[smem(), vmem(), vmem(), vmem(), anywhere()],
        out_specs=[vmem(), vmem(), vmem()],
        out_shape=[
            jax.ShapeDtypeStruct((8, bond), F32),
            jax.ShapeDtypeStruct((rows, bond), F32),
            jax.ShapeDtypeStruct((bond, bond), F32),
        ],
        scratch_shapes=[pltpu.VMEM((bond, bond), F32), pltpu.VMEM((rows, 8, bond), F32)],
        compiler_params=params(8),
        cost_estimate=cost(4 * squares.size, 2 * squares.size),
        name="inner_round",
    )(info, own, mate, squares, after)


def outer_call(info, side, part, mixed, other):
    return pl.pallas_call(
        outer_kernel,
        in_specs=[smem(), vmem(), vmem(), vmem(), vmem()],
        out_specs=vmem(),
        out_shape=jax.ShapeDtypeStruct(part.shape, F32),
        compiler_params=params(8),
        cost_estimate=cost(8 * mixed.size, 8 * mixed.size),
        name="outer_round",
    )(info, side, part, mixed, other)


def add_gram(info, member, weights, d_ref, out_ref, first_ref, gram):
    rows, bond = d_ref.shape[1:3]
    block = 32
    start = info[ROW] * rows
    first_ref[...] = jnp.sqrt(down(weights[0]))
    second = jnp.sqrt(down(weights[1]))
    gram[...] = jnp.zeros(gram.shape, F32)

    def body(step, carry):
        parts = []
        for place in range(block):
            index = step * block + place
            scale = first_ref[pl.ds(start + index, 1), :] * second
            piece = d_ref[member, index].astype(F32) * jnp.concatenate([scale, scale], axis=1)
            parts.append(piece.astype(BF16))
        weighted = jnp.concatenate(parts, axis=0)
        gram[...] += dot_of(weighted, weighted, ((0,), (0,)))
        return carry

    lax.fori_loop(0, rows // block, body, 0)
    out_ref[0] = gram[:bond, :bond]
    out_ref[1] = gram[:bond, bond:]
    out_ref[2] = gram[bond:, bond:]


def gram_weights(info, member, own_ref, mate_ref, side_ref):
    own, mate, side = (normalized(own_ref), normalized(mate_ref), normalized(side_ref))
    inner = inner_incoming(info, own, mate)
    outer = outer_incoming(info, own, mate, side)
    return [jnp.where(member == info[CORE], outer[leg], inner[leg]) for leg in range(2)]


def send_kernel(info, own_ref, mate_ref, side_ref, d_ref, out_ref, msg_ref, first_ref, gram):
    member = 1 - info[KEPT]
    weights = gram_weights(info, member, own_ref, mate_ref, side_ref)
    own = normalized(own_ref)
    for place in range(2):
        for leg in range(3):
            msg_ref[leg, pl.ds(place, 1), :] = pick(own, place, leg)
    add_gram(info, member, weights, d_ref, out_ref, first_ref, gram)


def keep_kernel(info, own_ref, mate_ref, side_ref, d_ref, after, out_ref, first_ref, gram):
    member = info[KEPT]
    weights = gram_weights(info, member, own_ref, mate_ref, side_ref)
    add_gram(info, member, weights, d_ref, out_ref, first_ref, gram)


def gram_call(kernel, name, extra_specs, out_specs, out_shape, flat, operands):
    rows, bond, wide = flat.shape[1:]
    return pl.pallas_call(
        kernel,
        in_specs=[smem()] + [vmem()] * 4 + extra_specs,
        out_specs=out_specs,
        out_shape=out_shape,
        scratch_shapes=[pltpu.VMEM((bond, bond), F32), pltpu.VMEM((wide, wide), F32)],
        compiler_params=params(20),
        cost_estimate=cost(wide * flat.size, flat.size),
        name=name,
    )(*operands)


def send_call(info, own, mate, side, flat):
    members, _, bond, _ = flat.shape
    shapes = [
        jax.ShapeDtypeStruct((3, bond, bond), F32),
        jax.ShapeDtypeStruct((3, members, bond), F32),
    ]
    operands = (info, own, mate, side, flat)
    return gram_call(send_kernel, "gram_to_send", [], [vmem(), vmem()], shapes, flat, operands)


def keep_call(info, own, mate, side, flat, after):
    bond = flat.shape[2]
    shape = jax.ShapeDtypeStruct((3, bond, bond), F32)
    operands = (info, own, mate, side, flat, after)
    return gram_call(keep_kernel, "gram_to_keep", [anywhere()], vmem(), shape, flat, operands)


def eye_mask(size):
    down_index = lax.broadcasted_iota(jnp.int32, (size, size), 0)
    across_index = lax.broadcasted_iota(jnp.int32, (size, size), 1)
    return down_index == across_index


def root_pair(matrix):
    size = matrix.shape[0]
    diagonal = eye_mask(size)
    lift = jnp.where(diagonal, 1.5, 0.0).astype(F32)
    scale = jnp.sum(jnp.where(diagonal, matrix, 0.0), keepdims=True)
    current = matrix / scale
    poly = lift - 0.5 * current
    poly_parts = halves(poly)
    current = dot3(halves(current), poly_parts)
    partner = poly
    for _ in range(SWEEPS - 1):
        current_parts, partner_parts = (halves(current), halves(partner))
        poly_parts = halves(lift - 0.5 * dot3(partner_parts, current_parts))
        current = dot3(current_parts, poly_parts)
        partner = dot3(poly_parts, partner_parts)
    root_scale = jnp.sqrt(scale)
    return (current * root_scale, partner / root_scale)


def root_kernel(keep_ref, got_ref, upper_ref, inverse_ref):
    corner = keep_ref[0] + got_ref[0]
    above = keep_ref[1] + got_ref[1]
    below = keep_ref[2] + got_ref[2]
    matrix = jnp.concatenate(
        [
            jnp.concatenate([corner, above], axis=1),
            jnp.concatenate([jnp.transpose(above), below], axis=1),
        ],
        axis=0,
    )
    upper_ref[...], inverse_ref[...] = root_pair(matrix)


def root_call(keep, got):
    wide = 2 * keep.shape[1]
    full = jax.ShapeDtypeStruct((wide, wide), F32)
    return pl.pallas_call(
        root_kernel,
        in_specs=[vmem(), vmem()],
        out_specs=[vmem(), vmem()],
        out_shape=[full, full],
        compiler_params=params(16),
        cost_estimate=cost(66 * 2 * wide**3, 16 * wide * wide),
        name="root",
    )(keep, got)


def truncate_kernel(info, gate, own_ref, mate_ref, upper_ref, inverse_ref, other_ref, probes_ref, out_ref):
    wide, bond = (upper_ref.shape[0], probes_ref.shape[1])
    odd = info[CORE] == 1
    kept = info[KEPT]
    mate_place = jnp.maximum(jnp.where(kept == 0, info[MATE0], info[MATE1]), 0)
    own_msg = own_ref[pl.ds(3 * kept + 2, 1), :]
    mate_msg = mate_ref[pl.ds(3 * mate_place + 2, 1), :]
    own_msg = own_msg / jnp.sum(own_msg, axis=1, keepdims=True)
    mate_msg = mate_msg / jnp.sum(mate_msg, axis=1, keepdims=True)
    strength = bond * jnp.sqrt(own_msg * mate_msg)
    own_upper, other_upper = (upper_ref[...], other_ref[...])
    left = jnp.where(odd, other_upper, own_upper)
    right = jnp.where(odd, own_upper, other_upper)
    left_parts, right_parts = (halves(left), halves(right))

    def block(value, down_half, across_half):
        return value[
            down_half * bond : (down_half + 1) * bond, across_half * bond : (across_half + 1) * bond
        ]

    def combined(value, entry):
        block_rows = []
        for out_down in range(2):
            blocks = []
            for out_across in range(2):
                total = None
                for first in range(2):
                    for second in range(2):
                        term = entry(out_down, out_across, first, second) * block(value, first, second)
                        total = term if total is None else total + term
                blocks.append(total * strength_down)
            block_rows.append(jnp.concatenate(blocks, axis=1))
        return jnp.concatenate(block_rows, axis=0)

    across = lax.broadcasted_iota(jnp.int32, (1, bond), 1)
    mask = (across < info[RANK]).astype(F32)
    strength_down = down(strength)
    probes = jnp.concatenate(
        [probes_ref[pl.ds(0, wide, 2), :] * mask, probes_ref[pl.ds(1, wide, 2), :] * mask], axis=1
    )
    probed = combined(
        dot3(right_parts, halves(probes)),
        lambda s, s_out, t, t_out: gate[2 * s_out + t_out, 2 * s + t],
    )
    sampled = dot3(left_parts, halves(probed))
    sampled_parts = halves(jnp.concatenate([sampled[:, :bond], sampled[:, bond:]], axis=0))
    inner = dot3(sampled_parts, sampled_parts, ((0,), (0,)))
    inner = inner + jnp.where(eye_mask(bond), 1.0 - mask, 0.0)
    _, inner_inverse = root_pair(inner)
    basis = dot3(sampled_parts, halves(inner_inverse))
    basis = jnp.concatenate([basis[:wide], basis[wide:]], axis=1)
    based = combined(
        dot3(left_parts, halves(basis)),
        lambda t, t_out, s, s_out: gate[2 * s_out + t_out, 2 * s + t],
    )
    coeffs = dot3(right_parts, halves(based))
    squares = jnp.sum(coeffs * coeffs, axis=0, keepdims=True)
    new_bond = jnp.sqrt((squares[:, :bond] + squares[:, bond:]) / (2 * wide) + 1e-06)
    target = jnp.where(odd, coeffs / jnp.concatenate([new_bond, new_bond], axis=1), basis)
    change = dot3(halves(inverse_ref[...]), halves(target))
    gated = info[GATED] == 1
    identity = eye_mask(wide).astype(F32)
    out_ref[:wide] = jnp.where(gated, change, identity).astype(BF16)
    bond_parts = halves(jnp.where(gated, new_bond, 0.0))
    out_ref[wide:] = jnp.broadcast_to(jnp.concatenate(bond_parts, axis=1), (16, wide))


def truncate_call(info, gate, own, mate, upper, inverse, other, probes):
    wide = upper.shape[0]
    return pl.pallas_call(
        truncate_kernel,
        in_specs=[smem(), smem()] + [vmem()] * 6,
        out_specs=vmem(),
        out_shape=jax.ShapeDtypeStruct((wide + 16, wide), BF16),
        compiler_params=params(32),
        cost_estimate=cost(40 * 2 * wide**3, 24 * wide * wide),
        name="truncate",
    )(info, gate, own, mate, upper, inverse, other, probes)


def update_member(member, pack_ref, d_ref, out_hbm, held, scratch, sems):
    rows, bond, wide = d_ref.shape[1:]
    slots, block = held.shape[:2]
    steps = rows // block

    def put(step):
        slot = lax.rem(step, slots)
        target = out_hbm.at[member, pl.ds(step * block, block)]
        return pltpu.make_async_copy(held.at[slot], target, sems.at[slot])

    def body(step, carry):
        start = step * block
        slot = lax.rem(step, slots)

        @pl.when(step >= slots)
        def free():
            put(step).wait()

        rows_in = d_ref[member, pl.ds(start, block)].reshape(block * bond, wide)
        result = dot_of(rows_in, pack_ref[:wide])
        for index in range(block):
            lane = scratch.at[index % scratch.shape[0]]
            piece = result[index * bond : (index + 1) * bond]
            lane[pl.ds(0, bond, 2), :] = piece[:, :bond]
            lane[pl.ds(1, bond, 2), :] = piece[:, bond:]
            held[slot, index] = lane[...].astype(BF16)
        put(step).start()
        return carry

    lax.fori_loop(0, steps, body, 0)
    for step in range(steps - slots, steps):
        put(step).wait()


def own_kernel(info, pack_ref, d_ref, after, out_hbm, held, scratch, sems):
    update_member(info[KEPT], pack_ref, d_ref, out_hbm, held, scratch, sems)


def other_kernel(info, pack_ref, got_ref, d_ref, begun_hbm, out_hbm, bond_ref, held, scratch, sems):
    bond, wide = d_ref.shape[2:]
    kept = info[KEPT]
    tail = pack_ref[wide:].astype(F32)
    got = got_ref[wide:].astype(F32)
    mine = tail[:1, :bond] + tail[:1, bond:]
    other = got[:1, :bond] + got[:1, bond:]
    bond_ref[pl.ds(0, 1), :] = jnp.where(kept == 0, mine, other)
    bond_ref[pl.ds(1, 1), :] = jnp.where(kept == 0, other, mine)
    update_member(1 - kept, got_ref, d_ref, out_hbm, held, scratch, sems)


def update_call(kernel, name, in_specs, aliases, with_bonds, flat, operands):
    members, rows, bond, wide = flat.shape
    block, slots = (16, 4)
    tensor = jax.ShapeDtypeStruct((members, rows, wide, bond), BF16)
    bonds = jax.ShapeDtypeStruct((members, bond), F32)
    return pl.pallas_call(
        kernel,
        in_specs=in_specs,
        out_specs=[hbm(), vmem()] if with_bonds else hbm(),
        out_shape=[tensor, bonds] if with_bonds else tensor,
        input_output_aliases=aliases,
        scratch_shapes=[
            pltpu.VMEM((slots, block, wide, bond), BF16),
            pltpu.VMEM((4, wide, bond), F32),
            pltpu.SemaphoreType.DMA((slots,)),
        ],
        compiler_params=params(24),
        cost_estimate=cost(wide * flat.size, 2 * flat.size),
        name=name,
    )(*operands)


def own_call(info, pack, flat, after):
    specs = [smem(), vmem(), vmem(), anywhere()]
    return update_call(own_kernel, "update_own", specs, {}, False, flat, (info, pack, flat, after))


def other_call(info, pack, got, flat, begun):
    specs = [smem(), vmem(), vmem(), vmem(), hbm()]
    operands = (info, pack, got, flat, begun)
    return update_call(other_kernel, "update_other", specs, {4: 0}, True, flat, operands)


def shards(tensors, neighbours, edge_ranks, gate_matrix, probes):
    members, rows, bond, phys = tensors.shape[:4]
    sites = lax.axis_size("site")
    row_swap = [(0, 1), (1, 0)]
    core_swap = [(i, i ^ 1) for i in range(sites)]
    side_swap = [(i, i + 1) for i in range(1, sites - 1, 2)]
    side_swap += [(j, i) for i, j in side_swap]
    x = tensors.reshape(members, rows, bond * phys, bond)
    x, squares, part = open_call(x)
    info, flat = flatten_call(part, x, 0, neighbours.T, edge_ranks)
    for index in range(ROUNDS):
        if index > 0:
            begun = inner_call(info, own, mate, squares, flat)
            part = outer_call(info, side, *begun)
        if index == 1:
            flat = flatten_call(part, x, 1, flat)
        own = part + lax.ppermute(part, "row", row_swap)
        side = lax.ppermute(own, "site", side_swap)
        mate = lax.ppermute(own, "site", core_swap)
    send, messages = send_call(info, own, mate, side, flat)
    got = lax.ppermute(send, "row", row_swap)
    keep = keep_call(info, own, mate, side, flat, send)
    upper, inverse = root_call(keep, got)
    other = lax.ppermute(upper, "site", core_swap)
    pack = truncate_call(info, gate_matrix, own, mate, upper, inverse, other, probes)
    got_pack = lax.ppermute(pack, "row", row_swap)
    begun = own_call(info, pack, flat, pack)
    updated, bonds = other_call(info, pack, got_pack, flat, begun)
    return (updated.reshape(tensors.shape), messages.transpose(1, 0, 2), bonds)


def solution(mesh):
    return jax.shard_map(
        shards,
        mesh=mesh,
        in_specs=(P("site", "row", None, None, None), P(), P(), P(), P()),
        out_specs=(P("site", "row", None, None, None), P("site", None, None), P("site", None)),
        check_vma=False,
    )
```

```python
import functools

import jax
import jax.numpy as jnp
from jax import lax
from jax.experimental import pallas as pl
from jax.experimental.pallas import tpu as pltpu
from jax.sharding import PartitionSpec as P

ROUNDS = 4
SWEEPS = 8
F32 = jnp.float32
BF16 = jnp.bfloat16
MB = 1 << 20
highest = lax.Precision.HIGHEST

CORE, ROW, MATE0, MATE1, FIRST, LAST, KEPT, RANK, GATED = range(9)


def smem():
    return pl.BlockSpec(memory_space=pltpu.SMEM)


def vmem():
    return pl.BlockSpec(memory_space=pltpu.VMEM)


def params(mib):
    return pltpu.CompilerParams(vmem_limit_bytes=mib * MB)


def cost(flops, moved):
    return pl.CostEstimate(flops=int(flops), bytes_accessed=int(moved), transcendentals=0)


def halves(value):
    high = value.astype(BF16)
    low = (value - high.astype(F32)).astype(BF16)
    return (high, low)


def dot_of(left, right, dims=((1,), (0,))):
    return lax.dot_general(left, right, (dims, ((), ())), preferred_element_type=F32)


def dot3(left, right, dims=((1,), (0,))):
    return dot_of(left[0], right[0], dims) + (
        dot_of(left[0], right[1], dims) + dot_of(left[1], right[0], dims)
    )


def dot_high(left, right, dims=((1,), (0,))):
    return lax.dot_general(left, right, (dims, ((), ())), preferred_element_type=F32, precision=highest)


def down(row):
    size = row.shape[-1]
    return jnp.transpose(jnp.broadcast_to(row, (size, size)))


def normalized(ref):
    rows = ref[...]
    return rows / jnp.sum(rows, axis=1, keepdims=True)


def pick(rows, member, leg):
    return rows[3 * member + leg : 3 * member + leg + 1]


def level(rows):
    return jnp.full((1, rows.shape[-1]), 1.0 / rows.shape[-1], F32)


def from_mate(mate, place):
    return jnp.where(place == 0, pick(mate, 0, 2), pick(mate, 1, 2))


def inner_incoming(info, own, mate):
    odd = info[0, CORE] == 1
    place = jnp.where(odd, info[0, MATE0], info[0, MATE1])
    joined = place == info[0, CORE]
    chain = jnp.where(odd, pick(mate, 1, 1), pick(mate, 0, 0))
    gated = jnp.where(odd, pick(mate, 1, 2), pick(mate, 0, 2))
    near = chain + jnp.where(joined, gated, 0.0)
    home = jnp.where(odd, pick(own, 1, 0), pick(own, 0, 1))
    third = from_mate(mate, place) + jnp.where(joined, chain, 0.0)
    return (
        jnp.where(odd, near, home),
        jnp.where(odd, home, near),
        jnp.where(place < 0, level(own), third),
    )


def outer_known(info, own, mate):
    odd = info[0, CORE] == 1
    place = jnp.where(odd, info[0, MATE1], info[0, MATE0])
    home = jnp.where(odd, pick(own, 0, 1), pick(own, 1, 0))
    return (home, jnp.where(place < 0, level(own), from_mate(mate, place)))


def outer_far(info, side):
    far = jnp.where(info[0, CORE] == 1, pick(side, 0, 0), pick(side, 1, 1))
    return jnp.where(info[0, FIRST] + info[0, LAST] > 0, level(side), far)


def outer_incoming(info, own, mate, side):
    odd = info[0, CORE] == 1
    home, third = outer_known(info, own, mate)
    far = outer_far(info, side)
    return (jnp.where(odd, home, far), jnp.where(odd, far, home), third)


def hbm():
    return pl.BlockSpec(memory_space=pltpu.HBM)


def anywhere():
    return pl.BlockSpec(memory_space=pl.ANY)


def scalars_kernel(after, near, ranks, out_ref):
    device, row = (lax.axis_index("site"), lax.axis_index("row"))
    core = lax.rem(device, 2)
    base = 2 * (device - core)
    even0, even1 = (near[2, base] - base, near[2, base + 1] - base)
    odd0, odd1 = (near[2, base + 2], near[2, base + 3])
    odd = core == 1
    crossed = jnp.logical_or(even0 == 3, even1 == 2)
    kept = jnp.where(jnp.logical_and(odd, crossed), 1 - row, row)
    site = 2 * device + kept
    values = {
        CORE: core,
        ROW: row,
        MATE0: jnp.where(odd, jnp.where(odd0 < 0, -1, odd0 - base), jnp.maximum(even0 - 2, -1)),
        MATE1: jnp.where(odd, jnp.where(odd1 < 0, -1, odd1 - base), jnp.maximum(even1 - 2, -1)),
        FIRST: (device == 0).astype(jnp.int32),
        LAST: (device == lax.axis_size("site") - 1).astype(jnp.int32),
        KEPT: kept,
        RANK: ranks[site],
        GATED: (near[2, site] >= 0).astype(jnp.int32),
    }
    lanes = lax.broadcasted_iota(jnp.int32, out_ref.shape, 1)
    total = jnp.zeros(out_ref.shape, jnp.int32)
    for place, value in values.items():
        total = jnp.where(lanes == place, value, total)
    out_ref[...] = total


def scalars_call(after, near, ranks):
    return pl.pallas_call(
        scalars_kernel,
        in_specs=[anywhere(), smem(), smem()],
        out_specs=vmem(),
        out_shape=jax.ShapeDtypeStruct((8, 128), jnp.int32),
        compiler_params=params(4),
        cost_estimate=cost(1024, 1 << 20),
        name="scalars",
    )(after, near, ranks)


def open_kernel(x_hbm, x_ref, s_ref, out_ref, scratch, sums_ref, total_ref, sems):
    members, rows, wide, bond = x_hbm.shape
    steps = sems.shape[0]
    per = steps // members
    block = rows // per

    def fetch(step):
        place = (step // per, pl.ds(lax.rem(step, per) * block, block))
        return pltpu.make_async_copy(x_hbm.at[place], x_ref.at[place], sems.at[step])

    for step in range(steps):
        fetch(step).start()
    total_ref[...] = jnp.zeros(total_ref.shape, F32)

    def body(step, carry):
        fetch(step).wait()
        member, start = (step // per, lax.rem(step, per) * block)
        total = total_ref[member]
        for index in range(block):
            lane = scratch.at[index % scratch.shape[0]]
            lane[...] = x_ref[member, start + index].astype(F32)
            even = lane[pl.ds(0, bond, 2), :]
            odd = lane[pl.ds(1, bond, 2), :]
            square = even * even + odd * odd
            s_ref[member, start + index] = square.astype(BF16)
            sums_ref[member, start + index] = jnp.sum(square.reshape(bond // 8, 8, bond), axis=0)
            total = total + square
        total_ref[member] = total
        return carry

    lax.fori_loop(0, steps, body, 0)
    row = lax.axis_index("row")
    flat_weight = jnp.ones((1, bond), F32)
    out_ref[...] = jnp.ones(out_ref.shape, F32)
    for member in range(members):
        finish(row, out_ref, member, sums_ref[member], total_ref[member], flat_weight, None)


def open_call(x):
    members, rows, wide, bond = x.shape
    block = 8
    steps = members * rows // block
    return pl.pallas_call(
        open_kernel,
        in_specs=[hbm()],
        out_specs=[vmem(), vmem(), vmem()],
        out_shape=[
            jax.ShapeDtypeStruct(x.shape, BF16),
            jax.ShapeDtypeStruct((members, rows, bond, bond), BF16),
            jax.ShapeDtypeStruct((8, bond), F32),
        ],
        scratch_shapes=[
            pltpu.VMEM((4, wide, bond), F32),
            pltpu.VMEM((members, rows, 8, bond), F32),
            pltpu.VMEM((members, bond, bond), F32),
            pltpu.SemaphoreType.DMA((steps,)),
        ],
        compiler_params=params(38),
        cost_estimate=cost(4 * x.size, 5 * x.size),
        name="open",
    )(x)


def flatten_kernel(after, x_ref, flat_ref, scratch):
    members, rows, bond = flat_ref.shape[:3]
    for member in range(members):

        def body(index, carry):
            lane = scratch.at[lax.rem(index, scratch.shape[0])]
            lane[...] = x_ref[member, index].astype(F32)
            parts = [lane[pl.ds(place, bond, 2), :] for place in range(2)]
            flat_ref[member, index] = jnp.concatenate(parts, axis=1).astype(BF16)
            return carry

        lax.fori_loop(0, rows, body, 0, unroll=8)


def flatten_call(after, x):
    members, rows, wide, bond = x.shape
    return pl.pallas_call(
        flatten_kernel,
        in_specs=[anywhere(), vmem()],
        out_specs=vmem(),
        out_shape=jax.ShapeDtypeStruct((members, rows, bond, wide), BF16),
        scratch_shapes=[pltpu.VMEM((8, wide, bond), F32)],
        compiler_params=params(8),
        cost_estimate=cost(2 * x.size, 4 * x.size),
        name="flatten",
    )(after, x)


def halved(row_index, row):
    half = row.shape[1] // 2
    return jnp.where(row_index == 0, row[:, :half], row[:, half:])


def placed(row_index, half):
    empty = jnp.zeros_like(half)
    return jnp.where(
        row_index == 0,
        jnp.concatenate([half, empty], axis=1),
        jnp.concatenate([empty, half], axis=1),
    )


def by_row(row, matrix):
    return dot_high(jnp.broadcast_to(row, (8, row.shape[1])), matrix)[:1]


def by_column(row, matrix):
    return dot_high(jnp.broadcast_to(row, (8, row.shape[1])), matrix, ((1,), (1,)))[:1]


def put_leg(out_ref, member, leg, row):
    out_ref[pl.ds(3 * member + leg, 1), :] = row


def finish(row_index, out_ref, member, sums, total, third, second_down):
    bond = total.shape[0]
    half = by_column(jnp.ones((1, bond), F32), jnp.sum(sums, axis=1))
    weighted = total if second_down is None else total * second_down
    put_leg(out_ref, member, 0, placed(row_index, half))
    put_leg(out_ref, member, 1, by_column(third, total))
    put_leg(out_ref, member, 2, jnp.sum(weighted, axis=0, keepdims=True))


GROUP = 4


def scaled_sum(s_ref, member, step, first_ref, start):
    bond = s_ref.shape[2]
    joined = None
    for place in range(GROUP):
        index = step * GROUP + place
        scale = jnp.broadcast_to(first_ref[pl.ds(start + index, 1), :], (16, bond)).astype(BF16)
        term = jnp.concatenate([scale] * (bond // 16), axis=0) * s_ref[member, index]
        joined = term if joined is None else joined + term
    return joined.astype(F32)


def contract_inner(info, weights, s_ref, out_ref, first_ref, sums_ref):
    rows, bond = s_ref.shape[1:3]
    member = 1 - info[0, CORE]
    start = info[0, ROW] * rows
    first, second, third = weights
    third = third.astype(BF16).astype(F32)
    first_ref[...] = down(first)
    second_down = down(second)
    outer = (second_down * third).astype(BF16)

    def body(step, total):
        for place in range(GROUP):
            index = step * GROUP + place
            piece = s_ref[member, index] * outer
            piece = piece[:64] + piece[64:]
            piece = (piece[:32] + piece[32:]).astype(F32)
            sums_ref[index] = (piece[:8] + piece[8:16]) + (piece[16:24] + piece[24:])
        return total + scaled_sum(s_ref, member, step, first_ref, start)

    total = lax.fori_loop(0, rows // GROUP, body, jnp.zeros((bond, bond), F32), unroll=2)
    finish(info[0, ROW], out_ref, member, sums_ref[...], total, third, second_down)


def contract_outer(info, home, third, s_ref, out_ref, mixed_ref, other_ref, first_ref):
    rows, bond = s_ref.shape[1:3]
    member = info[0, CORE]
    odd = info[0, CORE] == 1
    start = info[0, ROW] * rows
    third_rows = jnp.broadcast_to(third.astype(BF16), (8, bond))

    def mix(step, carry):
        pair = s_ref[member, pl.ds(2 * step, 2)].reshape(2 * bond, bond)
        product = dot_of(third_rows, pair, ((1,), (1,)))
        mixed_ref[pl.ds(2 * step, 1), :] = product[:1, :bond]
        mixed_ref[pl.ds(2 * step + 1, 1), :] = product[:1, bond:]
        return carry

    lax.fori_loop(0, rows // 2, mix, 0, unroll=8)

    @pl.when(odd)
    def over_first():
        first_ref[...] = down(home)

        def body(step, total):
            return total + scaled_sum(s_ref, member, step, first_ref, start)

        zero = jnp.zeros((bond, bond), F32)
        other_ref[...] = lax.fori_loop(0, rows // GROUP, body, zero, unroll=2)
        put_leg(out_ref, member, 1, by_row(halved(info[0, ROW], home), mixed_ref[...]))

    @pl.when(jnp.logical_not(odd))
    def over_second():
        second_rows = jnp.concatenate(halves(home) + (jnp.zeros((6, bond), BF16),), axis=0)

        def body(step, carry):
            pair = jnp.concatenate([s_ref[member, 2 * step], s_ref[member, 2 * step + 1]], axis=1)
            product = dot_of(second_rows, pair)
            product = product[:1] + product[1:2]
            other_ref[pl.ds(2 * step, 1), :] = product[:, :bond]
            other_ref[pl.ds(2 * step + 1, 1), :] = product[:, bond:]
            return carry

        lax.fori_loop(0, rows // 2, body, 0, unroll=8)
        put_leg(out_ref, member, 0, placed(info[0, ROW], by_column(home, mixed_ref[...])))


def inner_kernel(info, own_ref, mate_ref, s_ref, out_ref, mixed_ref, other_ref, first_ref, sums_ref):
    own, mate = (normalized(own_ref), normalized(mate_ref))
    out_ref[...] = jnp.ones(out_ref.shape, F32)
    contract_inner(info, inner_incoming(info, own, mate), s_ref, out_ref, first_ref, sums_ref)
    home, third = outer_known(info, own, mate)
    contract_outer(info, home, third, s_ref, out_ref, mixed_ref, other_ref, first_ref)


def outer_kernel(info, side_ref, part_ref, mixed_ref, other_ref, out_ref):
    rows = mixed_ref.shape[0]
    far = outer_far(info, normalized(side_ref))
    out_ref[...] = part_ref[...]

    @pl.when(info[0, CORE] == 1)
    def as_second():
        put_leg(out_ref, 1, 0, placed(info[0, ROW], by_column(far, mixed_ref[...])))
        put_leg(out_ref, 1, 2, by_row(far, other_ref[...]))

    @pl.when(info[0, CORE] == 0)
    def as_first():
        half = halved(info[0, ROW], far)
        put_leg(out_ref, 0, 1, by_row(half, mixed_ref[...]))
        put_leg(out_ref, 0, 2, by_row(half, other_ref[:rows]))


def inner_call(info, own, mate, squares):
    rows, bond = squares.shape[1:3]
    return pl.pallas_call(
        inner_kernel,
        in_specs=[vmem(), vmem(), vmem(), vmem()],
        out_specs=[vmem(), vmem(), vmem()],
        out_shape=[
            jax.ShapeDtypeStruct((8, bond), F32),
            jax.ShapeDtypeStruct((rows, bond), F32),
            jax.ShapeDtypeStruct((bond, bond), F32),
        ],
        scratch_shapes=[pltpu.VMEM((bond, bond), F32), pltpu.VMEM((rows, 8, bond), F32)],
        compiler_params=params(8),
        cost_estimate=cost(4 * squares.size, 2 * squares.size),
        name="inner_round",
    )(info, own, mate, squares)


def outer_call(info, side, part, mixed, other):
    return pl.pallas_call(
        outer_kernel,
        in_specs=[vmem(), vmem(), vmem(), vmem(), vmem()],
        out_specs=vmem(),
        out_shape=jax.ShapeDtypeStruct(part.shape, F32),
        compiler_params=params(8),
        cost_estimate=cost(8 * mixed.size, 8 * mixed.size),
        name="outer_round",
    )(info, side, part, mixed, other)


def add_gram(info, member, weights, d_ref, out_ref, first_ref, gram):
    rows, bond = d_ref.shape[1:3]
    block = 32
    start = info[0, ROW] * rows
    first_ref[...] = jnp.sqrt(down(weights[0]))
    second = jnp.sqrt(down(weights[1]))
    gram[...] = jnp.zeros(gram.shape, F32)

    def body(step, carry):
        parts = []
        for place in range(block):
            index = step * block + place
            scale = first_ref[pl.ds(start + index, 1), :] * second
            piece = d_ref[member, index].astype(F32) * jnp.concatenate([scale, scale], axis=1)
            parts.append(piece.astype(BF16))
        weighted = jnp.concatenate(parts, axis=0)
        gram[...] += dot_of(weighted, weighted, ((0,), (0,)))
        return carry

    lax.fori_loop(0, rows // block, body, 0)
    out_ref[0] = gram[:bond, :bond]
    out_ref[1] = gram[:bond, bond:]
    out_ref[2] = gram[bond:, bond:]


def gram_weights(info, member, own_ref, mate_ref, side_ref):
    own, mate, side = (normalized(own_ref), normalized(mate_ref), normalized(side_ref))
    inner = inner_incoming(info, own, mate)
    outer = outer_incoming(info, own, mate, side)
    return [jnp.where(member == info[0, CORE], outer[leg], inner[leg]) for leg in range(2)]


def send_kernel(info, own_ref, mate_ref, side_ref, d_ref, out_ref, first_ref, gram):
    member = 1 - info[0, KEPT]
    weights = gram_weights(info, member, own_ref, mate_ref, side_ref)
    add_gram(info, member, weights, d_ref, out_ref, first_ref, gram)


def keep_kernel(info, own_ref, mate_ref, side_ref, d_ref, after, out_ref, msg_ref, first_ref, gram):
    member = info[0, KEPT]
    weights = gram_weights(info, member, own_ref, mate_ref, side_ref)
    own = normalized(own_ref)
    for place in range(2):
        for leg in range(3):
            msg_ref[leg, pl.ds(place, 1), :] = pick(own, place, leg)
    add_gram(info, member, weights, d_ref, out_ref, first_ref, gram)


def gram_call(kernel, name, extra_specs, out_specs, out_shape, flat, operands):
    rows, bond, wide = flat.shape[1:]
    return pl.pallas_call(
        kernel,
        in_specs=[vmem()] + [vmem()] * 4 + extra_specs,
        out_specs=out_specs,
        out_shape=out_shape,
        scratch_shapes=[pltpu.VMEM((bond, bond), F32), pltpu.VMEM((wide, wide), F32)],
        compiler_params=params(20),
        cost_estimate=cost(wide * flat.size, flat.size),
        name=name,
    )(*operands)


def send_call(info, own, mate, side, flat):
    bond = flat.shape[2]
    shape = jax.ShapeDtypeStruct((3, bond, bond), F32)
    operands = (info, own, mate, side, flat)
    return gram_call(send_kernel, "gram_to_send", [], vmem(), shape, flat, operands)


def keep_call(info, own, mate, side, flat, after):
    members, _, bond, _ = flat.shape
    shapes = [
        jax.ShapeDtypeStruct((3, bond, bond), F32),
        jax.ShapeDtypeStruct((3, members, bond), F32),
    ]
    operands = (info, own, mate, side, flat, after)
    return gram_call(keep_kernel, "gram_to_keep", [anywhere()], [vmem(), vmem()], shapes, flat, operands)


def eye_mask(size):
    down_index = lax.broadcasted_iota(jnp.int32, (size, size), 0)
    across_index = lax.broadcasted_iota(jnp.int32, (size, size), 1)
    return down_index == across_index


def root_pair(matrix):
    size = matrix.shape[0]
    diagonal = eye_mask(size)
    lift = jnp.where(diagonal, 1.5, 0.0).astype(F32)
    scale = jnp.sum(jnp.where(diagonal, matrix, 0.0), keepdims=True)
    current = matrix / scale
    poly = lift - 0.5 * current
    poly_parts = halves(poly)
    current = dot3(halves(current), poly_parts)
    partner = poly
    for _ in range(SWEEPS - 1):
        current_parts, partner_parts = (halves(current), halves(partner))
        poly_parts = halves(lift - 0.5 * dot3(partner_parts, current_parts))
        current = dot3(current_parts, poly_parts)
        partner = dot3(poly_parts, partner_parts)
    root_scale = jnp.sqrt(scale)
    return (current * root_scale, partner / root_scale)


def root_kernel(keep_ref, got_ref, upper_ref, inverse_ref):
    corner = keep_ref[0] + got_ref[0]
    above = keep_ref[1] + got_ref[1]
    below = keep_ref[2] + got_ref[2]
    matrix = jnp.concatenate(
        [
            jnp.concatenate([corner, above], axis=1),
            jnp.concatenate([jnp.transpose(above), below], axis=1),
        ],
        axis=0,
    )
    upper_ref[...], inverse_ref[...] = root_pair(matrix)


def root_call(keep, got):
    wide = 2 * keep.shape[1]
    full = jax.ShapeDtypeStruct((wide, wide), F32)
    return pl.pallas_call(
        root_kernel,
        in_specs=[vmem(), vmem()],
        out_specs=[vmem(), vmem()],
        out_shape=[full, full],
        compiler_params=params(16),
        cost_estimate=cost(66 * 2 * wide**3, 16 * wide * wide),
        name="root",
    )(keep, got)


def truncate_kernel(info, gate, own_ref, mate_ref, upper_ref, inverse_ref, other_ref, probes_ref, out_ref):
    wide, bond = (upper_ref.shape[0], probes_ref.shape[1])
    odd = info[0, CORE] == 1
    kept = info[0, KEPT]
    mate_place = jnp.maximum(jnp.where(kept == 0, info[0, MATE0], info[0, MATE1]), 0)
    own_msg = own_ref[pl.ds(3 * kept + 2, 1), :]
    mate_msg = mate_ref[pl.ds(3 * mate_place + 2, 1), :]
    own_msg = own_msg / jnp.sum(own_msg, axis=1, keepdims=True)
    mate_msg = mate_msg / jnp.sum(mate_msg, axis=1, keepdims=True)
    strength = bond * jnp.sqrt(own_msg * mate_msg)
    own_upper, other_upper = (upper_ref[...], other_ref[...])
    left = jnp.where(odd, other_upper, own_upper)
    right = jnp.where(odd, own_upper, other_upper)
    left_parts, right_parts = (halves(left), halves(right))

    def block(value, down_half, across_half):
        return value[
            down_half * bond : (down_half + 1) * bond, across_half * bond : (across_half + 1) * bond
        ]

    def combined(value, entry):
        block_rows = []
        for out_down in range(2):
            blocks = []
            for out_across in range(2):
                total = None
                for first in range(2):
                    for second in range(2):
                        term = entry(out_down, out_across, first, second) * block(value, first, second)
                        total = term if total is None else total + term
                blocks.append(total * strength_down)
            block_rows.append(jnp.concatenate(blocks, axis=1))
        return jnp.concatenate(block_rows, axis=0)

    across = lax.broadcasted_iota(jnp.int32, (1, bond), 1)
    mask = (across < info[0, RANK]).astype(F32)
    strength_down = down(strength)
    probes = jnp.concatenate(
        [probes_ref[pl.ds(0, wide, 2), :] * mask, probes_ref[pl.ds(1, wide, 2), :] * mask], axis=1
    )
    probed = combined(
        dot3(right_parts, halves(probes)),
        lambda s, s_out, t, t_out: gate[2 * s_out + t_out, 2 * s + t],
    )
    sampled = dot3(left_parts, halves(probed))
    sampled_parts = halves(jnp.concatenate([sampled[:, :bond], sampled[:, bond:]], axis=0))
    inner = dot3(sampled_parts, sampled_parts, ((0,), (0,)))
    inner = inner + jnp.where(eye_mask(bond), 1.0 - mask, 0.0)
    _, inner_inverse = root_pair(inner)
    basis = dot3(sampled_parts, halves(inner_inverse))
    basis = jnp.concatenate([basis[:wide], basis[wide:]], axis=1)
    based = combined(
        dot3(left_parts, halves(basis)),
        lambda t, t_out, s, s_out: gate[2 * s_out + t_out, 2 * s + t],
    )
    coeffs = dot3(right_parts, halves(based))
    squares = jnp.sum(coeffs * coeffs, axis=0, keepdims=True)
    new_bond = jnp.sqrt((squares[:, :bond] + squares[:, bond:]) / (2 * wide) + 1e-06)
    target = jnp.where(odd, coeffs / jnp.concatenate([new_bond, new_bond], axis=1), basis)
    change = dot3(halves(inverse_ref[...]), halves(target))
    gated = info[0, GATED] == 1
    identity = eye_mask(wide).astype(F32)
    out_ref[:wide] = jnp.where(gated, change, identity).astype(BF16)
    bond_parts = halves(jnp.where(gated, new_bond, 0.0))
    out_ref[wide:] = jnp.broadcast_to(jnp.concatenate(bond_parts, axis=1), (16, wide))


def truncate_call(info, gate, own, mate, upper, inverse, other, probes):
    wide = upper.shape[0]
    return pl.pallas_call(
        truncate_kernel,
        in_specs=[vmem()] * 8,
        out_specs=vmem(),
        out_shape=jax.ShapeDtypeStruct((wide + 16, wide), BF16),
        compiler_params=params(32),
        cost_estimate=cost(40 * 2 * wide**3, 24 * wide * wide),
        name="truncate",
    )(info, gate, own, mate, upper, inverse, other, probes)


def update_member(member, pack_ref, d_ref, out_hbm, held, scratch, sems):
    rows, bond, wide = d_ref.shape[1:]
    slots, block = held.shape[:2]
    steps = rows // block

    def put(step):
        slot = lax.rem(step, slots)
        target = out_hbm.at[member, pl.ds(step * block, block)]
        return pltpu.make_async_copy(held.at[slot], target, sems.at[slot])

    def body(step, carry):
        start = step * block
        slot = lax.rem(step, slots)

        @pl.when(step >= slots)
        def free():
            put(step).wait()

        rows_in = d_ref[member, pl.ds(start, block)].reshape(block * bond, wide)
        result = dot_of(rows_in, pack_ref[:wide])
        for index in range(block):
            lane = scratch.at[index % scratch.shape[0]]
            piece = result[index * bond : (index + 1) * bond]
            lane[pl.ds(0, bond, 2), :] = piece[:, :bond]
            lane[pl.ds(1, bond, 2), :] = piece[:, bond:]
            held[slot, index] = lane[...].astype(BF16)
        put(step).start()
        return carry

    lax.fori_loop(0, steps, body, 0)
    for step in range(steps - slots, steps):
        put(step).wait()


def own_kernel(info, pack_ref, d_ref, after, out_hbm, held, scratch, sems):
    update_member(info[0, KEPT], pack_ref, d_ref, out_hbm, held, scratch, sems)


def other_kernel(info, pack_ref, got_ref, d_ref, begun_hbm, out_hbm, bond_hbm, held, scratch, sems, bond_ref, bond_sem):
    bond, wide = d_ref.shape[2:]
    kept = info[0, KEPT]
    tail = pack_ref[wide:].astype(F32)
    got = got_ref[wide:].astype(F32)
    mine = tail[:1, :bond] + tail[:1, bond:]
    other = got[:1, :bond] + got[:1, bond:]
    bond_ref[pl.ds(0, 1), :] = jnp.where(kept == 0, mine, other)
    bond_ref[pl.ds(1, 1), :] = jnp.where(kept == 0, other, mine)
    bond_copy = pltpu.make_async_copy(bond_ref, bond_hbm, bond_sem)
    bond_copy.start()
    update_member(1 - kept, got_ref, d_ref, out_hbm, held, scratch, sems)
    bond_copy.wait()


def update_call(kernel, name, in_specs, aliases, with_bonds, flat, operands):
    members, rows, bond, wide = flat.shape
    block, slots = (16, 4)
    tensor = jax.ShapeDtypeStruct((members, rows, wide, bond), BF16)
    bonds = jax.ShapeDtypeStruct((members, bond), F32)
    return pl.pallas_call(
        kernel,
        in_specs=in_specs,
        out_specs=[hbm(), hbm()] if with_bonds else hbm(),
        out_shape=[tensor, bonds] if with_bonds else tensor,
        input_output_aliases=aliases,
        scratch_shapes=[
            pltpu.VMEM((slots, block, wide, bond), BF16),
            pltpu.VMEM((4, wide, bond), F32),
            pltpu.SemaphoreType.DMA((slots,)),
        ]
        + ([pltpu.VMEM((members, bond), F32), pltpu.SemaphoreType.DMA(())] if with_bonds else []),
        compiler_params=params(24),
        cost_estimate=cost(wide * flat.size, 2 * flat.size),
        name=name,
    )(*operands)


def own_call(info, pack, flat, after):
    specs = [vmem(), vmem(), vmem(), anywhere()]
    return update_call(own_kernel, "update_own", specs, {}, False, flat, (info, pack, flat, after))


def other_call(info, pack, got, flat, begun):
    specs = [vmem(), vmem(), vmem(), vmem(), hbm()]
    operands = (info, pack, got, flat, begun)
    return update_call(other_kernel, "update_other", specs, {4: 0}, True, flat, operands)


def shards(tensors, neighbours, edge_ranks, gate_matrix, probes):
    members, rows, bond, phys = tensors.shape[:4]
    sites = lax.axis_size("site")
    row_swap = [(0, 1), (1, 0)]
    core_swap = [(i, i ^ 1) for i in range(sites)]
    side_swap = [(i, i + 1) for i in range(1, sites - 1, 2)]
    side_swap += [(j, i) for i, j in side_swap]
    x = tensors.reshape(members, rows, bond * phys, bond)
    x, squares, part = open_call(x)
    info = scalars_call(part, neighbours.T, edge_ranks)
    for index in range(ROUNDS):
        if index > 0:
            begun = inner_call(info, own, mate, squares)
            part = outer_call(info, side, *begun)
        own = part + lax.ppermute(part, "row", row_swap)
        side = lax.ppermute(own, "site", side_swap)
        mate = lax.ppermute(own, "site", core_swap)
    flat = flatten_call(own, x)
    send = send_call(info, own, mate, side, flat)
    got = lax.ppermute(send, "row", row_swap)
    keep, messages = keep_call(info, own, mate, side, flat, send)
    upper, inverse = root_call(keep, got)
    other = lax.ppermute(upper, "site", core_swap)
    pack = truncate_call(info, gate_matrix, own, mate, upper, inverse, other, probes)
    got_pack = lax.ppermute(pack, "row", row_swap)
    begun = own_call(info, pack, flat, pack)
    updated, bonds = other_call(info, pack, got_pack, flat, begun)
    return (updated.reshape(tensors.shape), messages.transpose(1, 0, 2), bonds)


def solution(mesh):
    return jax.shard_map(
        shards,
        mesh=mesh,
        in_specs=(P("site", "row", None, None, None), P(), P(), P(), P()),
        out_specs=(P("site", "row", None, None, None), P("site", None, None), P("site", None)),
        check_vma=False,
    )
```

```python
import functools

import jax
import jax.numpy as jnp
from jax import lax
from jax.experimental import pallas as pl
from jax.experimental.pallas import tpu as pltpu
from jax.sharding import PartitionSpec as P

ROUNDS = 4
SWEEPS = 8
F32 = jnp.float32
BF16 = jnp.bfloat16
MB = 1 << 20
highest = lax.Precision.HIGHEST

CORE, ROW, MATE0, MATE1, FIRST, LAST, KEPT, RANK, GATED = range(9)


def smem():
    return pl.BlockSpec(memory_space=pltpu.SMEM)


def vmem():
    return pl.BlockSpec(memory_space=pltpu.VMEM)


def params(mib):
    return pltpu.CompilerParams(vmem_limit_bytes=mib * MB)


def cost(flops, moved):
    return pl.CostEstimate(flops=int(flops), bytes_accessed=int(moved), transcendentals=0)


def halves(value):
    high = value.astype(BF16)
    low = (value - high.astype(F32)).astype(BF16)
    return (high, low)


def dot_of(left, right, dims=((1,), (0,))):
    return lax.dot_general(left, right, (dims, ((), ())), preferred_element_type=F32)


def dot3(left, right, dims=((1,), (0,))):
    return dot_of(left[0], right[0], dims) + (
        dot_of(left[0], right[1], dims) + dot_of(left[1], right[0], dims)
    )


def dot_high(left, right, dims=((1,), (0,))):
    return lax.dot_general(left, right, (dims, ((), ())), preferred_element_type=F32, precision=highest)


def down(row):
    size = row.shape[-1]
    return jnp.transpose(jnp.broadcast_to(row, (size, size)))


def normalized(ref):
    rows = ref[...]
    return rows / jnp.sum(rows, axis=1, keepdims=True)


def pick(rows, member, leg):
    return rows[3 * member + leg : 3 * member + leg + 1]


def level(rows):
    return jnp.full((1, rows.shape[-1]), 1.0 / rows.shape[-1], F32)


def from_mate(mate, place):
    return jnp.where(place == 0, pick(mate, 0, 2), pick(mate, 1, 2))


def inner_incoming(info, own, mate):
    odd = info[0, CORE] == 1
    place = jnp.where(odd, info[0, MATE0], info[0, MATE1])
    joined = place == info[0, CORE]
    chain = jnp.where(odd, pick(mate, 1, 1), pick(mate, 0, 0))
    gated = jnp.where(odd, pick(mate, 1, 2), pick(mate, 0, 2))
    near = chain + jnp.where(joined, gated, 0.0)
    home = jnp.where(odd, pick(own, 1, 0), pick(own, 0, 1))
    third = from_mate(mate, place) + jnp.where(joined, chain, 0.0)
    return (
        jnp.where(odd, near, home),
        jnp.where(odd, home, near),
        jnp.where(place < 0, level(own), third),
    )


def outer_known(info, own, mate):
    odd = info[0, CORE] == 1
    place = jnp.where(odd, info[0, MATE1], info[0, MATE0])
    home = jnp.where(odd, pick(own, 0, 1), pick(own, 1, 0))
    return (home, jnp.where(place < 0, level(own), from_mate(mate, place)))


def outer_far(info, side):
    far = jnp.where(info[0, CORE] == 1, pick(side, 0, 0), pick(side, 1, 1))
    return jnp.where(info[0, FIRST] + info[0, LAST] > 0, level(side), far)


def outer_incoming(info, own, mate, side):
    odd = info[0, CORE] == 1
    home, third = outer_known(info, own, mate)
    far = outer_far(info, side)
    return (jnp.where(odd, home, far), jnp.where(odd, far, home), third)


def hbm():
    return pl.BlockSpec(memory_space=pltpu.HBM)


def anywhere():
    return pl.BlockSpec(memory_space=pl.ANY)


def scalars_kernel(after, near, ranks, out_ref):
    device, row = (lax.axis_index("site"), lax.axis_index("row"))
    core = lax.rem(device, 2)
    base = 2 * (device - core)
    even0, even1 = (near[2, base] - base, near[2, base + 1] - base)
    odd0, odd1 = (near[2, base + 2], near[2, base + 3])
    odd = core == 1
    crossed = jnp.logical_or(even0 == 3, even1 == 2)
    kept = jnp.where(jnp.logical_and(odd, crossed), 1 - row, row)
    site = 2 * device + kept
    values = {
        CORE: core,
        ROW: row,
        MATE0: jnp.where(odd, jnp.where(odd0 < 0, -1, odd0 - base), jnp.maximum(even0 - 2, -1)),
        MATE1: jnp.where(odd, jnp.where(odd1 < 0, -1, odd1 - base), jnp.maximum(even1 - 2, -1)),
        FIRST: (device == 0).astype(jnp.int32),
        LAST: (device == lax.axis_size("site") - 1).astype(jnp.int32),
        KEPT: kept,
        RANK: ranks[site],
        GATED: (near[2, site] >= 0).astype(jnp.int32),
    }
    lanes = lax.broadcasted_iota(jnp.int32, out_ref.shape, 1)
    total = jnp.zeros(out_ref.shape, jnp.int32)
    for place, value in values.items():
        total = jnp.where(lanes == place, value, total)
    out_ref[...] = total


def scalars_call(after, near, ranks):
    return pl.pallas_call(
        scalars_kernel,
        in_specs=[anywhere(), smem(), smem()],
        out_specs=vmem(),
        out_shape=jax.ShapeDtypeStruct((8, 128), jnp.int32),
        compiler_params=params(4),
        cost_estimate=cost(1024, 1 << 20),
        name="scalars",
    )(after, near, ranks)


def add_kernel(one_ref, two_ref, after, out_ref):
    out_ref[...] = one_ref[...] + two_ref[...]


def add_call(one, two, after):
    return pl.pallas_call(
        add_kernel,
        in_specs=[vmem(), vmem(), anywhere()],
        out_specs=vmem(),
        out_shape=jax.ShapeDtypeStruct(one.shape, F32),
        compiler_params=params(4),
        cost_estimate=cost(one.size, 12 * one.size),
        name="add",
    )(one, two, after)


def open_kernel(x_hbm, x_ref, s_ref, out_ref, scratch, sums_ref, total_ref, sems):
    members, rows, wide, bond = x_hbm.shape
    steps = sems.shape[0]
    per = steps // members
    block = rows // per

    def fetch(step):
        place = (step // per, pl.ds(lax.rem(step, per) * block, block))
        return pltpu.make_async_copy(x_hbm.at[place], x_ref.at[place], sems.at[step])

    for step in range(steps):
        fetch(step).start()
    total_ref[...] = jnp.zeros(total_ref.shape, F32)

    def body(step, carry):
        fetch(step).wait()
        member, start = (step // per, lax.rem(step, per) * block)
        total = total_ref[member]
        for index in range(block):
            lane = scratch.at[index % scratch.shape[0]]
            lane[...] = x_ref[member, start + index].astype(F32)
            even = lane[pl.ds(0, bond, 2), :]
            odd = lane[pl.ds(1, bond, 2), :]
            square = even * even + odd * odd
            s_ref[member, start + index] = square.astype(BF16)
            sums_ref[member, start + index] = jnp.sum(square.reshape(bond // 8, 8, bond), axis=0)
            total = total + square
        total_ref[member] = total
        return carry

    lax.fori_loop(0, steps, body, 0)
    row = lax.axis_index("row")
    flat_weight = jnp.ones((1, bond), F32)
    out_ref[...] = jnp.ones(out_ref.shape, F32)
    for member in range(members):
        finish(row, out_ref, member, sums_ref[member], total_ref[member], flat_weight, None)


def open_call(x):
    members, rows, wide, bond = x.shape
    block = 8
    steps = members * rows // block
    return pl.pallas_call(
        open_kernel,
        in_specs=[hbm()],
        out_specs=[vmem(), vmem(), vmem()],
        out_shape=[
            jax.ShapeDtypeStruct(x.shape, BF16),
            jax.ShapeDtypeStruct((members, rows, bond, bond), BF16),
            jax.ShapeDtypeStruct((8, bond), F32),
        ],
        scratch_shapes=[
            pltpu.VMEM((4, wide, bond), F32),
            pltpu.VMEM((members, rows, 8, bond), F32),
            pltpu.VMEM((members, bond, bond), F32),
            pltpu.SemaphoreType.DMA((steps,)),
        ],
        compiler_params=params(38),
        cost_estimate=cost(4 * x.size, 5 * x.size),
        name="open",
    )(x)


def flatten_kernel(after, x_ref, flat_ref, scratch):
    members, rows, bond = flat_ref.shape[:3]
    for member in range(members):

        def body(index, carry):
            lane = scratch.at[lax.rem(index, scratch.shape[0])]
            lane[...] = x_ref[member, index].astype(F32)
            parts = [lane[pl.ds(place, bond, 2), :] for place in range(2)]
            flat_ref[member, index] = jnp.concatenate(parts, axis=1).astype(BF16)
            return carry

        lax.fori_loop(0, rows, body, 0, unroll=8)


def flatten_call(after, x):
    members, rows, wide, bond = x.shape
    return pl.pallas_call(
        flatten_kernel,
        in_specs=[anywhere(), vmem()],
        out_specs=vmem(),
        out_shape=jax.ShapeDtypeStruct((members, rows, bond, wide), BF16),
        scratch_shapes=[pltpu.VMEM((8, wide, bond), F32)],
        compiler_params=params(8),
        cost_estimate=cost(2 * x.size, 4 * x.size),
        name="flatten",
    )(after, x)


def halved(row_index, row):
    half = row.shape[1] // 2
    return jnp.where(row_index == 0, row[:, :half], row[:, half:])


def placed(row_index, half):
    empty = jnp.zeros_like(half)
    return jnp.where(
        row_index == 0,
        jnp.concatenate([half, empty], axis=1),
        jnp.concatenate([empty, half], axis=1),
    )


def by_row(row, matrix):
    return dot_high(jnp.broadcast_to(row, (8, row.shape[1])), matrix)[:1]


def by_column(row, matrix):
    return dot_high(jnp.broadcast_to(row, (8, row.shape[1])), matrix, ((1,), (1,)))[:1]


def put_leg(out_ref, member, leg, row):
    out_ref[pl.ds(3 * member + leg, 1), :] = row


def finish(row_index, out_ref, member, sums, total, third, second_down):
    bond = total.shape[0]
    half = by_column(jnp.ones((1, bond), F32), jnp.sum(sums, axis=1))
    weighted = total if second_down is None else total * second_down
    put_leg(out_ref, member, 0, placed(row_index, half))
    put_leg(out_ref, member, 1, by_column(third, total))
    put_leg(out_ref, member, 2, jnp.sum(weighted, axis=0, keepdims=True))


GROUP = 4


def scaled_sum(s_ref, member, step, first_ref, start):
    bond = s_ref.shape[2]
    joined = None
    for place in range(GROUP):
        index = step * GROUP + place
        scale = jnp.broadcast_to(first_ref[pl.ds(start + index, 1), :], (16, bond)).astype(BF16)
        term = jnp.concatenate([scale] * (bond // 16), axis=0) * s_ref[member, index]
        joined = term if joined is None else joined + term
    return joined.astype(F32)


def contract_inner(info, weights, s_ref, out_ref, first_ref, sums_ref):
    rows, bond = s_ref.shape[1:3]
    member = 1 - info[0, CORE]
    start = info[0, ROW] * rows
    first, second, third = weights
    third = third.astype(BF16).astype(F32)
    first_ref[...] = down(first)
    second_down = down(second)
    outer = (second_down * third).astype(BF16)

    def body(step, total):
        for place in range(GROUP):
            index = step * GROUP + place
            piece = s_ref[member, index] * outer
            piece = piece[:64] + piece[64:]
            piece = (piece[:32] + piece[32:]).astype(F32)
            sums_ref[index] = (piece[:8] + piece[8:16]) + (piece[16:24] + piece[24:])
        return total + scaled_sum(s_ref, member, step, first_ref, start)

    total = lax.fori_loop(0, rows // GROUP, body, jnp.zeros((bond, bond), F32), unroll=2)
    finish(info[0, ROW], out_ref, member, sums_ref[...], total, third, second_down)


def contract_outer(info, home, third, s_ref, out_ref, mixed_ref, other_ref, first_ref):
    rows, bond = s_ref.shape[1:3]
    member = info[0, CORE]
    odd = info[0, CORE] == 1
    start = info[0, ROW] * rows
    third_rows = jnp.broadcast_to(third.astype(BF16), (8, bond))

    def mix(step, carry):
        pair = s_ref[member, pl.ds(2 * step, 2)].reshape(2 * bond, bond)
        product = dot_of(third_rows, pair, ((1,), (1,)))
        mixed_ref[pl.ds(2 * step, 1), :] = product[:1, :bond]
        mixed_ref[pl.ds(2 * step + 1, 1), :] = product[:1, bond:]
        return carry

    lax.fori_loop(0, rows // 2, mix, 0, unroll=8)

    @pl.when(odd)
    def over_first():
        first_ref[...] = down(home)

        def body(step, total):
            return total + scaled_sum(s_ref, member, step, first_ref, start)

        zero = jnp.zeros((bond, bond), F32)
        other_ref[...] = lax.fori_loop(0, rows // GROUP, body, zero, unroll=2)
        put_leg(out_ref, member, 1, by_row(halved(info[0, ROW], home), mixed_ref[...]))

    @pl.when(jnp.logical_not(odd))
    def over_second():
        second_rows = jnp.concatenate(halves(home) + (jnp.zeros((6, bond), BF16),), axis=0)

        def body(step, carry):
            pair = jnp.concatenate([s_ref[member, 2 * step], s_ref[member, 2 * step + 1]], axis=1)
            product = dot_of(second_rows, pair)
            product = product[:1] + product[1:2]
            other_ref[pl.ds(2 * step, 1), :] = product[:, :bond]
            other_ref[pl.ds(2 * step + 1, 1), :] = product[:, bond:]
            return carry

        lax.fori_loop(0, rows // 2, body, 0, unroll=8)
        put_leg(out_ref, member, 0, placed(info[0, ROW], by_column(home, mixed_ref[...])))


def inner_kernel(info, own_ref, mate_ref, s_ref, out_ref, mixed_ref, other_ref, first_ref, sums_ref):
    own, mate = (normalized(own_ref), normalized(mate_ref))
    out_ref[...] = jnp.ones(out_ref.shape, F32)
    contract_inner(info, inner_incoming(info, own, mate), s_ref, out_ref, first_ref, sums_ref)
    home, third = outer_known(info, own, mate)
    contract_outer(info, home, third, s_ref, out_ref, mixed_ref, other_ref, first_ref)


def outer_kernel(info, side_ref, part_ref, mixed_ref, other_ref, out_ref):
    rows = mixed_ref.shape[0]
    far = outer_far(info, normalized(side_ref))
    out_ref[...] = part_ref[...]

    @pl.when(info[0, CORE] == 1)
    def as_second():
        put_leg(out_ref, 1, 0, placed(info[0, ROW], by_column(far, mixed_ref[...])))
        put_leg(out_ref, 1, 2, by_row(far, other_ref[...]))

    @pl.when(info[0, CORE] == 0)
    def as_first():
        half = halved(info[0, ROW], far)
        put_leg(out_ref, 0, 1, by_row(half, mixed_ref[...]))
        put_leg(out_ref, 0, 2, by_row(half, other_ref[:rows]))


def inner_call(info, own, mate, squares):
    rows, bond = squares.shape[1:3]
    return pl.pallas_call(
        inner_kernel,
        in_specs=[vmem(), vmem(), vmem(), vmem()],
        out_specs=[vmem(), vmem(), vmem()],
        out_shape=[
            jax.ShapeDtypeStruct((8, bond), F32),
            jax.ShapeDtypeStruct((rows, bond), F32),
            jax.ShapeDtypeStruct((bond, bond), F32),
        ],
        scratch_shapes=[pltpu.VMEM((bond, bond), F32), pltpu.VMEM((rows, 8, bond), F32)],
        compiler_params=params(8),
        cost_estimate=cost(4 * squares.size, 2 * squares.size),
        name="inner_round",
    )(info, own, mate, squares)


def outer_call(info, side, part, mixed, other):
    return pl.pallas_call(
        outer_kernel,
        in_specs=[vmem(), vmem(), vmem(), vmem(), vmem()],
        out_specs=vmem(),
        out_shape=jax.ShapeDtypeStruct(part.shape, F32),
        compiler_params=params(8),
        cost_estimate=cost(8 * mixed.size, 8 * mixed.size),
        name="outer_round",
    )(info, side, part, mixed, other)


def add_gram(info, member, weights, d_ref, out_ref, first_ref, gram):
    rows, bond = d_ref.shape[1:3]
    block = 64
    start = info[0, ROW] * rows
    first_ref[...] = down(jnp.sqrt(weights[0]))
    second = down(jnp.sqrt(weights[1]))
    gram[...] = jnp.zeros(gram.shape, F32)

    def body(step, carry):
        parts = []
        for place in range(block):
            index = step * block + place
            scale = first_ref[pl.ds(start + index, 1), :] * second
            piece = d_ref[member, index].astype(F32) * jnp.concatenate([scale, scale], axis=1)
            parts.append(piece.astype(BF16))
        weighted = jnp.concatenate(parts, axis=0)
        gram[...] += dot_of(weighted, weighted, ((0,), (0,)))
        return carry

    lax.fori_loop(0, rows // block, body, 0)
    out_ref[0] = gram[:bond, :bond]
    out_ref[1] = gram[:bond, bond:]
    out_ref[2] = gram[bond:, bond:]


def gram_weights(info, member, own_ref, mate_ref, side_ref):
    own, mate, side = (normalized(own_ref), normalized(mate_ref), normalized(side_ref))
    inner = inner_incoming(info, own, mate)
    outer = outer_incoming(info, own, mate, side)
    return [jnp.where(member == info[0, CORE], outer[leg], inner[leg]) for leg in range(2)]


def send_kernel(info, own_ref, mate_ref, side_ref, d_ref, out_ref, first_ref, gram):
    member = 1 - info[0, KEPT]
    weights = gram_weights(info, member, own_ref, mate_ref, side_ref)
    add_gram(info, member, weights, d_ref, out_ref, first_ref, gram)


def keep_kernel(info, own_ref, mate_ref, side_ref, d_ref, after, out_ref, msg_ref, first_ref, gram):
    member = info[0, KEPT]
    weights = gram_weights(info, member, own_ref, mate_ref, side_ref)
    own = normalized(own_ref)
    for place in range(2):
        for leg in range(3):
            msg_ref[leg, pl.ds(place, 1), :] = pick(own, place, leg)
    add_gram(info, member, weights, d_ref, out_ref, first_ref, gram)


def gram_call(kernel, name, extra_specs, out_specs, out_shape, flat, operands):
    rows, bond, wide = flat.shape[1:]
    return pl.pallas_call(
        kernel,
        in_specs=[vmem()] + [vmem()] * 4 + extra_specs,
        out_specs=out_specs,
        out_shape=out_shape,
        scratch_shapes=[pltpu.VMEM((bond, bond), F32), pltpu.VMEM((wide, wide), F32)],
        compiler_params=params(20),
        cost_estimate=cost(wide * flat.size, flat.size),
        name=name,
    )(*operands)


def send_call(info, own, mate, side, flat):
    bond = flat.shape[2]
    shape = jax.ShapeDtypeStruct((3, bond, bond), F32)
    operands = (info, own, mate, side, flat)
    return gram_call(send_kernel, "gram_to_send", [], vmem(), shape, flat, operands)


def keep_call(info, own, mate, side, flat, after):
    members, _, bond, _ = flat.shape
    shapes = [
        jax.ShapeDtypeStruct((3, bond, bond), F32),
        jax.ShapeDtypeStruct((3, members, bond), F32),
    ]
    operands = (info, own, mate, side, flat, after)
    return gram_call(keep_kernel, "gram_to_keep", [anywhere()], [vmem(), vmem()], shapes, flat, operands)


def eye_mask(size):
    down_index = lax.broadcasted_iota(jnp.int32, (size, size), 0)
    across_index = lax.broadcasted_iota(jnp.int32, (size, size), 1)
    return down_index == across_index


def root_sweeps(matrix):
    size = matrix.shape[0]
    diagonal = eye_mask(size)
    lift = jnp.where(diagonal, 1.5, 0.0).astype(F32)
    scale = jnp.sum(jnp.where(diagonal, matrix, 0.0), keepdims=True)
    current = matrix / scale
    poly = lift - 0.5 * current
    poly_parts = halves(poly)
    current = dot3(halves(current), poly_parts)
    partner = poly
    yield None
    for _ in range(SWEEPS - 1):
        current_parts, partner_parts = (halves(current), halves(partner))
        poly_parts = halves(lift - 0.5 * dot3(partner_parts, current_parts))
        current = dot3(current_parts, poly_parts)
        partner = dot3(poly_parts, partner_parts)
        yield None
    root_scale = jnp.sqrt(scale)
    yield (current * root_scale, partner / root_scale)


def root_pair(matrix):
    for result in root_sweeps(matrix):
        pass
    return result


def root_kernel(keep_ref, got_ref, upper_ref, inverse_ref):
    corner = keep_ref[0] + got_ref[0]
    above = keep_ref[1] + got_ref[1]
    below = keep_ref[2] + got_ref[2]
    matrix = jnp.concatenate(
        [
            jnp.concatenate([corner, above], axis=1),
            jnp.concatenate([jnp.transpose(above), below], axis=1),
        ],
        axis=0,
    )
    upper_ref[...], inverse_ref[...] = root_pair(matrix)


def root_call(keep, got):
    wide = 2 * keep.shape[1]
    full = jax.ShapeDtypeStruct((wide, wide), F32)
    return pl.pallas_call(
        root_kernel,
        in_specs=[vmem(), vmem()],
        out_specs=[vmem(), vmem()],
        out_shape=[full, full],
        compiler_params=params(16),
        cost_estimate=cost(66 * 2 * wide**3, 16 * wide * wide),
        name="root",
    )(keep, got)


def truncate_kernel(info, gate, own_ref, mate_ref, upper_ref, inverse_ref, other_ref, probes_ref, out_ref):
    wide, bond = (upper_ref.shape[0], probes_ref.shape[1])
    odd = info[0, CORE] == 1
    kept = info[0, KEPT]
    mate_place = jnp.maximum(jnp.where(kept == 0, info[0, MATE0], info[0, MATE1]), 0)
    own_msg = own_ref[pl.ds(3 * kept + 2, 1), :]
    mate_msg = mate_ref[pl.ds(3 * mate_place + 2, 1), :]
    own_msg = own_msg / jnp.sum(own_msg, axis=1, keepdims=True)
    mate_msg = mate_msg / jnp.sum(mate_msg, axis=1, keepdims=True)
    strength = bond * jnp.sqrt(own_msg * mate_msg)
    own_upper, other_upper = (upper_ref[...], other_ref[...])
    left = jnp.where(odd, other_upper, own_upper)
    right = jnp.where(odd, own_upper, other_upper)
    left_parts, right_parts = (halves(left), halves(right))

    def block(value, down_half, across_half):
        return value[
            down_half * bond : (down_half + 1) * bond, across_half * bond : (across_half + 1) * bond
        ]

    def combined(value, entry):
        block_rows = []
        for out_down in range(2):
            blocks = []
            for out_across in range(2):
                total = None
                for first in range(2):
                    for second in range(2):
                        term = entry(out_down, out_across, first, second) * block(value, first, second)
                        total = term if total is None else total + term
                blocks.append(total * strength_down)
            block_rows.append(jnp.concatenate(blocks, axis=1))
        return jnp.concatenate(block_rows, axis=0)

    across = lax.broadcasted_iota(jnp.int32, (1, bond), 1)
    mask = (across < info[0, RANK]).astype(F32)
    strength_down = down(strength)
    probes = jnp.concatenate(
        [probes_ref[pl.ds(0, wide, 2), :] * mask, probes_ref[pl.ds(1, wide, 2), :] * mask], axis=1
    )
    probed = combined(
        dot3(right_parts, halves(probes)),
        lambda s, s_out, t, t_out: gate[2 * s_out + t_out, 2 * s + t],
    )
    sampled = dot3(left_parts, halves(probed))
    sampled_parts = halves(jnp.concatenate([sampled[:, :bond], sampled[:, bond:]], axis=0))
    inner = dot3(sampled_parts, sampled_parts, ((0,), (0,)))
    inner = inner + jnp.where(eye_mask(bond), 1.0 - mask, 0.0)
    sweeps = root_sweeps(inner)
    next(sweeps)
    based = dot3(left_parts, halves(sampled))
    next(sweeps)
    based = combined(based, lambda t, t_out, s, s_out: gate[2 * s_out + t_out, 2 * s + t])
    next(sweeps)
    next(sweeps)
    coeffs = dot3(right_parts, halves(based))
    next(sweeps)
    next(sweeps)
    target = dot3(halves(inverse_ref[...]), halves(jnp.where(odd, coeffs, sampled)))
    for result in sweeps:
        pass
    inner_inverse = result[1]
    inner_parts = halves(inner_inverse)

    def rooted(value):
        return [dot3(halves(value[:, :bond]), inner_parts), dot3(halves(value[:, bond:]), inner_parts)]

    squares = sum(jnp.sum(part * part, axis=0, keepdims=True) for part in rooted(coeffs))
    new_bond = jnp.sqrt(squares / (2 * wide) + 1e-06)
    divisor = jnp.where(odd, new_bond, 1.0)
    change = jnp.concatenate([part / divisor for part in rooted(target)], axis=1)
    gated = info[0, GATED] == 1
    identity = eye_mask(wide).astype(F32)
    out_ref[:wide] = jnp.where(gated, change, identity).astype(BF16)
    bond_parts = halves(jnp.where(gated, new_bond, 0.0))
    out_ref[wide:] = jnp.broadcast_to(jnp.concatenate(bond_parts, axis=1), (16, wide))


def truncate_call(info, gate, own, mate, upper, inverse, other, probes):
    wide = upper.shape[0]
    return pl.pallas_call(
        truncate_kernel,
        in_specs=[vmem()] * 8,
        out_specs=vmem(),
        out_shape=jax.ShapeDtypeStruct((wide + 16, wide), BF16),
        compiler_params=params(32),
        cost_estimate=cost(40 * 2 * wide**3, 24 * wide * wide),
        name="truncate",
    )(info, gate, own, mate, upper, inverse, other, probes)


def update_member(member, pack_ref, d_ref, out_hbm, held, scratch, sems):
    rows, bond, wide = d_ref.shape[1:]
    slots, block = held.shape[:2]
    steps = rows // block

    def put(step):
        slot = lax.rem(step, slots)
        target = out_hbm.at[member, pl.ds(step * block, block)]
        return pltpu.make_async_copy(held.at[slot], target, sems.at[slot])

    def body(step, carry):
        start = step * block
        slot = lax.rem(step, slots)

        @pl.when(step >= slots)
        def free():
            put(step).wait()

        change = pack_ref[:wide]
        for index in range(block):
            if index % 4 == 0:
                rows_in = d_ref[member, pl.ds(start + index, 4)].reshape(4 * bond, wide)
                result = dot_of(rows_in, change)
            lane = scratch.at[index % scratch.shape[0]]
            piece = result[index % 4 * bond : (index % 4 + 1) * bond]
            lane[pl.ds(0, bond, 2), :] = piece[:, :bond]
            lane[pl.ds(1, bond, 2), :] = piece[:, bond:]
            held[slot, index] = lane[...].astype(BF16)
        put(step).start()
        return carry

    lax.fori_loop(0, steps, body, 0)
    for step in range(steps - slots, steps):
        put(step).wait()


def own_kernel(info, pack_ref, d_ref, after, out_hbm, held, scratch, sems):
    update_member(info[0, KEPT], pack_ref, d_ref, out_hbm, held, scratch, sems)


def other_kernel(info, pack_ref, got_ref, d_ref, begun_hbm, out_hbm, bond_hbm, held, scratch, sems, bond_ref, bond_sem):
    bond, wide = d_ref.shape[2:]
    kept = info[0, KEPT]
    tail = pack_ref[wide:].astype(F32)
    got = got_ref[wide:].astype(F32)
    mine = tail[:1, :bond] + tail[:1, bond:]
    other = got[:1, :bond] + got[:1, bond:]
    bond_ref[pl.ds(0, 1), :] = jnp.where(kept == 0, mine, other)
    bond_ref[pl.ds(1, 1), :] = jnp.where(kept == 0, other, mine)
    bond_copy = pltpu.make_async_copy(bond_ref, bond_hbm, bond_sem)
    bond_copy.start()
    update_member(1 - kept, got_ref, d_ref, out_hbm, held, scratch, sems)
    bond_copy.wait()


def update_call(kernel, name, in_specs, aliases, with_bonds, flat, operands):
    members, rows, bond, wide = flat.shape
    block, slots = (16, 4)
    tensor = jax.ShapeDtypeStruct((members, rows, wide, bond), BF16)
    bonds = jax.ShapeDtypeStruct((members, bond), F32)
    return pl.pallas_call(
        kernel,
        in_specs=in_specs,
        out_specs=[hbm(), hbm()] if with_bonds else hbm(),
        out_shape=[tensor, bonds] if with_bonds else tensor,
        input_output_aliases=aliases,
        scratch_shapes=[
            pltpu.VMEM((slots, block, wide, bond), BF16),
            pltpu.VMEM((4, wide, bond), F32),
            pltpu.SemaphoreType.DMA((slots,)),
        ]
        + ([pltpu.VMEM((members, bond), F32), pltpu.SemaphoreType.DMA(())] if with_bonds else []),
        compiler_params=params(24),
        cost_estimate=cost(wide * flat.size, 2 * flat.size),
        name=name,
    )(*operands)


def own_call(info, pack, flat, after):
    specs = [vmem(), vmem(), vmem(), anywhere()]
    return update_call(own_kernel, "update_own", specs, {}, False, flat, (info, pack, flat, after))


def other_call(info, pack, got, flat, begun):
    specs = [vmem(), vmem(), vmem(), vmem(), hbm()]
    operands = (info, pack, got, flat, begun)
    return update_call(other_kernel, "update_other", specs, {4: 0}, True, flat, operands)


def shards(tensors, neighbours, edge_ranks, gate_matrix, probes):
    members, rows, bond, phys = tensors.shape[:4]
    sites = lax.axis_size("site")
    row_swap = [(0, 1), (1, 0)]
    core_swap = [(i, i ^ 1) for i in range(sites)]
    side_swap = [(i, i + 1) for i in range(1, sites - 1, 2)]
    side_swap += [(j, i) for i, j in side_swap]
    x = tensors.reshape(members, rows, bond * phys, bond)
    x, squares, part = open_call(x)
    info = scalars_call(part, neighbours.T, edge_ranks)
    for index in range(ROUNDS):
        if index > 0:
            begun = inner_call(info, own, mate, squares)
            part = outer_call(info, side, *begun)
        got = lax.ppermute(part, "row", row_swap)
        own = part + got if index > 0 else add_call(part, got, info)
        side = lax.ppermute(own, "site", side_swap)
        mate = lax.ppermute(own, "site", core_swap)
    flat = flatten_call(own, x)
    send = send_call(info, own, mate, side, flat)
    got = lax.ppermute(send, "row", row_swap)
    keep, messages = keep_call(info, own, mate, side, flat, send)
    upper, inverse = root_call(keep, got)
    other = lax.ppermute(upper, "site", core_swap)
    pack = truncate_call(info, gate_matrix, own, mate, upper, inverse, other, probes)
    got_pack = lax.ppermute(pack, "row", row_swap)
    begun = own_call(info, pack, flat, pack)
    updated, bonds = other_call(info, pack, got_pack, flat, begun)
    return (updated.reshape(tensors.shape), messages.transpose(1, 0, 2), bonds)


def solution(mesh):
    return jax.shard_map(
        shards,
        mesh=mesh,
        in_specs=(P("site", "row", None, None, None), P(), P(), P(), P()),
        out_specs=(P("site", "row", None, None, None), P("site", None, None), P("site", None)),
        check_vma=False,
    )
```

```python
import functools

import jax
import jax.numpy as jnp
from jax import lax
from jax.experimental import pallas as pl
from jax.experimental.pallas import tpu as pltpu
from jax.sharding import PartitionSpec as P

ROUNDS = 4
SWEEPS = 8
F32 = jnp.float32
BF16 = jnp.bfloat16
MB = 1 << 20

CORE, ROW, MATE0, MATE1, FIRST, LAST, KEPT, RANK, GATED = range(9)


def smem():
    return pl.BlockSpec(memory_space=pltpu.SMEM)


def vmem():
    return pl.BlockSpec(memory_space=pltpu.VMEM)


def params(mib):
    return pltpu.CompilerParams(vmem_limit_bytes=mib * MB)


def cost(flops, moved):
    return pl.CostEstimate(flops=int(flops), bytes_accessed=int(moved), transcendentals=0)


def halves(value):
    high = value.astype(BF16)
    low = (value - high.astype(F32)).astype(BF16)
    return (high, low)


def dot_of(left, right, dims=((1,), (0,))):
    return lax.dot_general(left, right, (dims, ((), ())), preferred_element_type=F32)


def dot3(left, right, dims=((1,), (0,))):
    return dot_of(left[0], right[0], dims) + (
        dot_of(left[0], right[1], dims) + dot_of(left[1], right[0], dims)
    )


def down(row):
    size = row.shape[-1]
    return jnp.transpose(jnp.broadcast_to(row, (size, size)))


def normalized(ref):
    rows = ref[...]
    return rows / jnp.sum(rows, axis=1, keepdims=True)


def pick(rows, member, leg):
    return rows[3 * member + leg : 3 * member + leg + 1]


def level(rows):
    return jnp.full((1, rows.shape[-1]), 1.0 / rows.shape[-1], F32)


def from_mate(mate, place):
    return jnp.where(place == 0, pick(mate, 0, 2), pick(mate, 1, 2))


def inner_incoming(info, own, mate):
    odd = info[0, CORE] == 1
    place = jnp.where(odd, info[0, MATE0], info[0, MATE1])
    joined = place == info[0, CORE]
    chain = jnp.where(odd, pick(mate, 1, 1), pick(mate, 0, 0))
    gated = jnp.where(odd, pick(mate, 1, 2), pick(mate, 0, 2))
    near = chain + jnp.where(joined, gated, 0.0)
    home = jnp.where(odd, pick(own, 1, 0), pick(own, 0, 1))
    third = from_mate(mate, place) + jnp.where(joined, chain, 0.0)
    return (
        jnp.where(odd, near, home),
        jnp.where(odd, home, near),
        jnp.where(place < 0, level(own), third),
    )


def outer_known(info, own, mate):
    odd = info[0, CORE] == 1
    place = jnp.where(odd, info[0, MATE1], info[0, MATE0])
    home = jnp.where(odd, pick(own, 0, 1), pick(own, 1, 0))
    return (home, jnp.where(place < 0, level(own), from_mate(mate, place)))


def outer_far(info, side):
    far = jnp.where(info[0, CORE] == 1, pick(side, 0, 0), pick(side, 1, 1))
    return jnp.where(info[0, FIRST] + info[0, LAST] > 0, level(side), far)


def outer_incoming(info, own, mate, side):
    odd = info[0, CORE] == 1
    home, third = outer_known(info, own, mate)
    far = outer_far(info, side)
    return (jnp.where(odd, home, far), jnp.where(odd, far, home), third)


def hbm():
    return pl.BlockSpec(memory_space=pltpu.HBM)


def anywhere():
    return pl.BlockSpec(memory_space=pl.ANY)


def scalars_kernel(after, near, ranks, out_ref):
    device, row = (lax.axis_index("site"), lax.axis_index("row"))
    core = lax.rem(device, 2)
    base = 2 * (device - core)
    even0, even1 = (near[2, base] - base, near[2, base + 1] - base)
    odd0, odd1 = (near[2, base + 2], near[2, base + 3])
    odd = core == 1
    crossed = jnp.logical_or(even0 == 3, even1 == 2)
    kept = jnp.where(jnp.logical_and(odd, crossed), 1 - row, row)
    site = 2 * device + kept
    values = {
        CORE: core,
        ROW: row,
        MATE0: jnp.where(odd, jnp.where(odd0 < 0, -1, odd0 - base), jnp.maximum(even0 - 2, -1)),
        MATE1: jnp.where(odd, jnp.where(odd1 < 0, -1, odd1 - base), jnp.maximum(even1 - 2, -1)),
        FIRST: (device == 0).astype(jnp.int32),
        LAST: (device == lax.axis_size("site") - 1).astype(jnp.int32),
        KEPT: kept,
        RANK: ranks[site],
        GATED: (near[2, site] >= 0).astype(jnp.int32),
    }
    lanes = lax.broadcasted_iota(jnp.int32, out_ref.shape, 1)
    total = jnp.zeros(out_ref.shape, jnp.int32)
    for place, value in values.items():
        total = jnp.where(lanes == place, value, total)
    out_ref[...] = total


def scalars_call(after, near, ranks):
    return pl.pallas_call(
        scalars_kernel,
        in_specs=[anywhere(), smem(), smem()],
        out_specs=vmem(),
        out_shape=jax.ShapeDtypeStruct((8, 128), jnp.int32),
        compiler_params=params(4),
        cost_estimate=cost(1024, 1 << 20),
        name="scalars",
    )(after, near, ranks)


def add_kernel(one_ref, two_ref, after, out_ref):
    out_ref[...] = one_ref[...] + two_ref[...]


def add_call(one, two, after):
    return pl.pallas_call(
        add_kernel,
        in_specs=[vmem(), vmem(), anywhere()],
        out_specs=vmem(),
        out_shape=jax.ShapeDtypeStruct(one.shape, F32),
        compiler_params=params(4),
        cost_estimate=cost(one.size, 12 * one.size),
        name="add",
    )(one, two, after)


def open_kernel(x_hbm, x_ref, s_ref, out_ref, scratch, sums_ref, total_ref, sems):
    members, rows, wide, bond = x_hbm.shape
    steps = sems.shape[0]
    per = steps // members
    block = rows // per

    def fetch(step):
        place = (step // per, pl.ds(lax.rem(step, per) * block, block))
        return pltpu.make_async_copy(x_hbm.at[place], x_ref.at[place], sems.at[step])

    for step in range(steps):
        fetch(step).start()
    total_ref[...] = jnp.zeros(total_ref.shape, F32)

    def body(step, carry):
        fetch(step).wait()
        member, start = (step // per, lax.rem(step, per) * block)
        total = total_ref[member]
        for index in range(block):
            lane = scratch.at[index % scratch.shape[0]]
            lane[...] = x_ref[member, start + index].astype(F32)
            even = lane[pl.ds(0, bond, 2), :]
            odd = lane[pl.ds(1, bond, 2), :]
            square = even * even + odd * odd
            s_ref[member, start + index] = square.astype(BF16)
            sums_ref[member, start + index] = jnp.sum(square.reshape(bond // 8, 8, bond), axis=0)
            total = total + square
        total_ref[member] = total
        return carry

    lax.fori_loop(0, steps, body, 0)
    row = lax.axis_index("row")
    flat_weight = jnp.ones((1, bond), F32)
    out_ref[...] = jnp.ones(out_ref.shape, F32)
    for member in range(members):
        finish(row, out_ref, member, sums_ref[member], total_ref[member], flat_weight, None)


def open_call(x):
    members, rows, wide, bond = x.shape
    block = 16
    steps = members * rows // block
    return pl.pallas_call(
        open_kernel,
        in_specs=[hbm()],
        out_specs=[vmem(), vmem(), vmem()],
        out_shape=[
            jax.ShapeDtypeStruct(x.shape, BF16),
            jax.ShapeDtypeStruct((members, rows, bond, bond), BF16),
            jax.ShapeDtypeStruct((8, bond), F32),
        ],
        scratch_shapes=[
            pltpu.VMEM((4, wide, bond), F32),
            pltpu.VMEM((members, rows, 8, bond), F32),
            pltpu.VMEM((members, bond, bond), F32),
            pltpu.SemaphoreType.DMA((steps,)),
        ],
        compiler_params=params(38),
        cost_estimate=cost(4 * x.size, 5 * x.size),
        name="open",
    )(x)


def flatten_kernel(after, x_ref, flat_ref, scratch):
    members, rows, bond = flat_ref.shape[:3]
    for member in range(members):

        def body(index, carry):
            lane = scratch.at[lax.rem(index, scratch.shape[0])]
            lane[...] = x_ref[member, index].astype(F32)
            parts = [lane[pl.ds(place, bond, 2), :] for place in range(2)]
            flat_ref[member, index] = jnp.concatenate(parts, axis=1).astype(BF16)
            return carry

        lax.fori_loop(0, rows, body, 0, unroll=8)


def flatten_call(after, x):
    members, rows, wide, bond = x.shape
    return pl.pallas_call(
        flatten_kernel,
        in_specs=[anywhere(), vmem()],
        out_specs=vmem(),
        out_shape=jax.ShapeDtypeStruct((members, rows, bond, wide), BF16),
        scratch_shapes=[pltpu.VMEM((8, wide, bond), F32)],
        compiler_params=params(8),
        cost_estimate=cost(2 * x.size, 4 * x.size),
        name="flatten",
    )(after, x)


def halved(row_index, row):
    half = row.shape[1] // 2
    return jnp.where(row_index == 0, row[:, :half], row[:, half:])


def placed(row_index, half):
    empty = jnp.zeros_like(half)
    return jnp.where(
        row_index == 0,
        jnp.concatenate([half, empty], axis=1),
        jnp.concatenate([empty, half], axis=1),
    )


def by_row(row, matrix):
    return dot3(halves(jnp.broadcast_to(row, (16, row.shape[1]))), halves(matrix))[:1]


def by_column(row, matrix):
    return dot3(halves(jnp.broadcast_to(row, (16, row.shape[1]))), halves(matrix), ((1,), (1,)))[:1]


def put_leg(out_ref, member, leg, row):
    out_ref[pl.ds(3 * member + leg, 1), :] = row


def finish(row_index, out_ref, member, sums, total, third, second_down):
    bond = total.shape[0]
    half = by_column(jnp.ones((1, bond), F32), jnp.sum(sums, axis=1))
    weighted = total if second_down is None else total * second_down
    put_leg(out_ref, member, 0, placed(row_index, half))
    put_leg(out_ref, member, 1, by_column(third, total))
    put_leg(out_ref, member, 2, jnp.sum(weighted, axis=0, keepdims=True))


GROUP = 4


def scaled_sum(s_ref, member, step, first_ref, start):
    bond = s_ref.shape[2]
    joined = None
    for place in range(GROUP):
        index = step * GROUP + place
        scale = jnp.broadcast_to(first_ref[pl.ds(start + index, 1), :], (16, bond)).astype(BF16)
        term = jnp.concatenate([scale] * (bond // 16), axis=0) * s_ref[member, index]
        joined = term if joined is None else joined + term
    return joined.astype(F32)


def contract_inner(info, weights, s_ref, out_ref, first_ref, sums_ref):
    rows, bond = s_ref.shape[1:3]
    member = 1 - info[0, CORE]
    start = info[0, ROW] * rows
    first, second, third = weights
    third = third.astype(BF16).astype(F32)
    first_ref[...] = down(first)
    second_down = down(second)
    outer = (second_down * third).astype(BF16)

    def body(step, total):
        for place in range(GROUP):
            index = step * GROUP + place
            piece = s_ref[member, index] * outer
            piece = piece[:64] + piece[64:]
            piece = (piece[:32] + piece[32:]).astype(F32)
            sums_ref[index] = (piece[:8] + piece[8:16]) + (piece[16:24] + piece[24:])
        return total + scaled_sum(s_ref, member, step, first_ref, start)

    total = lax.fori_loop(0, rows // GROUP, body, jnp.zeros((bond, bond), F32), unroll=2)
    finish(info[0, ROW], out_ref, member, sums_ref[...], total, third, second_down)


def contract_outer(info, home, third, s_ref, out_ref, mixed_ref, other_ref, first_ref):
    rows, bond = s_ref.shape[1:3]
    member = info[0, CORE]
    odd = info[0, CORE] == 1
    start = info[0, ROW] * rows
    third_rows = jnp.broadcast_to(third.astype(BF16), (8, bond))

    def mix(step, carry):
        pair = s_ref[member, pl.ds(2 * step, 2)].reshape(2 * bond, bond)
        product = dot_of(third_rows, pair, ((1,), (1,)))
        mixed_ref[pl.ds(2 * step, 1), :] = product[:1, :bond]
        mixed_ref[pl.ds(2 * step + 1, 1), :] = product[:1, bond:]
        return carry

    lax.fori_loop(0, rows // 2, mix, 0, unroll=8)

    @pl.when(odd)
    def over_first():
        first_ref[...] = down(home)

        def body(step, total):
            return total + scaled_sum(s_ref, member, step, first_ref, start)

        zero = jnp.zeros((bond, bond), F32)
        other_ref[...] = lax.fori_loop(0, rows // GROUP, body, zero, unroll=2)
        put_leg(out_ref, member, 1, by_row(halved(info[0, ROW], home), mixed_ref[...]))

    @pl.when(jnp.logical_not(odd))
    def over_second():
        second_rows = jnp.concatenate(halves(home) + (jnp.zeros((6, bond), BF16),), axis=0)

        def body(step, carry):
            pair = jnp.concatenate([s_ref[member, 2 * step], s_ref[member, 2 * step + 1]], axis=1)
            product = dot_of(second_rows, pair)
            product = product[:1] + product[1:2]
            other_ref[pl.ds(2 * step, 1), :] = product[:, :bond]
            other_ref[pl.ds(2 * step + 1, 1), :] = product[:, bond:]
            return carry

        lax.fori_loop(0, rows // 2, body, 0, unroll=8)
        put_leg(out_ref, member, 0, placed(info[0, ROW], by_column(home, mixed_ref[...])))


def inner_kernel(info, own_ref, mate_ref, s_ref, out_ref, mixed_ref, other_ref, first_ref, sums_ref):
    own, mate = (normalized(own_ref), normalized(mate_ref))
    out_ref[...] = jnp.ones(out_ref.shape, F32)
    contract_inner(info, inner_incoming(info, own, mate), s_ref, out_ref, first_ref, sums_ref)
    home, third = outer_known(info, own, mate)
    contract_outer(info, home, third, s_ref, out_ref, mixed_ref, other_ref, first_ref)


def outer_kernel(info, side_ref, part_ref, mixed_ref, other_ref, out_ref):
    rows = mixed_ref.shape[0]
    far = outer_far(info, normalized(side_ref))
    out_ref[...] = part_ref[...]

    @pl.when(info[0, CORE] == 1)
    def as_second():
        put_leg(out_ref, 1, 0, placed(info[0, ROW], by_column(far, mixed_ref[...])))
        put_leg(out_ref, 1, 2, by_row(far, other_ref[...]))

    @pl.when(info[0, CORE] == 0)
    def as_first():
        half = halved(info[0, ROW], far)
        put_leg(out_ref, 0, 1, by_row(half, mixed_ref[...]))
        put_leg(out_ref, 0, 2, by_row(half, other_ref[:rows]))


def inner_call(info, own, mate, squares):
    rows, bond = squares.shape[1:3]
    return pl.pallas_call(
        inner_kernel,
        in_specs=[vmem(), vmem(), vmem(), vmem()],
        out_specs=[vmem(), vmem(), vmem()],
        out_shape=[
            jax.ShapeDtypeStruct((8, bond), F32),
            jax.ShapeDtypeStruct((rows, bond), F32),
            jax.ShapeDtypeStruct((bond, bond), F32),
        ],
        scratch_shapes=[pltpu.VMEM((bond, bond), F32), pltpu.VMEM((rows, 8, bond), F32)],
        compiler_params=params(8),
        cost_estimate=cost(4 * squares.size, 2 * squares.size),
        name="inner_round",
    )(info, own, mate, squares)


def outer_call(info, side, part, mixed, other):
    return pl.pallas_call(
        outer_kernel,
        in_specs=[vmem(), vmem(), vmem(), vmem(), vmem()],
        out_specs=vmem(),
        out_shape=jax.ShapeDtypeStruct(part.shape, F32),
        compiler_params=params(8),
        cost_estimate=cost(8 * mixed.size, 8 * mixed.size),
        name="outer_round",
    )(info, side, part, mixed, other)


def add_gram(info, member, weights, d_ref, first_ref, gram):
    rows, bond = d_ref.shape[1:3]
    block = 64
    start = info[0, ROW] * rows
    first_ref[...] = down(jnp.sqrt(weights[0]))
    second = down(jnp.sqrt(weights[1]))
    gram[...] = jnp.zeros(gram.shape, F32)

    def body(step, carry):
        parts = []
        for place in range(block):
            index = step * block + place
            scale = first_ref[pl.ds(start + index, 1), :] * second
            piece = d_ref[member, index].astype(F32) * jnp.concatenate([scale, scale], axis=1)
            parts.append(piece.astype(BF16))
        weighted = jnp.concatenate(parts, axis=0)
        gram[...] += dot_of(weighted, weighted, ((0,), (0,)))
        return carry

    lax.fori_loop(0, rows // block, body, 0)


def gram_weights(info, member, own_ref, mate_ref, side_ref):
    own, mate, side = (normalized(own_ref), normalized(mate_ref), normalized(side_ref))
    inner = inner_incoming(info, own, mate)
    outer = outer_incoming(info, own, mate, side)
    return [jnp.where(member == info[0, CORE], outer[leg], inner[leg]) for leg in range(2)]


def send_kernel(info, own_ref, mate_ref, side_ref, d_ref, out_ref, first_ref, gram):
    bond = d_ref.shape[2]
    member = 1 - info[0, KEPT]
    weights = gram_weights(info, member, own_ref, mate_ref, side_ref)
    add_gram(info, member, weights, d_ref, first_ref, gram)
    corner, above, below = (gram[:bond, :bond], gram[:bond, bond:], gram[bond:, bond:])
    out_ref[:bond] = jnp.where(below_diagonal(bond), below, corner)
    out_ref[bond : 2 * bond] = above
    diagonal = jnp.sum(jnp.where(eye_mask(bond), below, 0.0), axis=0, keepdims=True)
    out_ref[2 * bond :] = jnp.broadcast_to(diagonal, (8, bond))


def keep_kernel(info, own_ref, mate_ref, side_ref, d_ref, after, out_ref, msg_ref, first_ref, gram):
    bond = d_ref.shape[2]
    member = info[0, KEPT]
    weights = gram_weights(info, member, own_ref, mate_ref, side_ref)
    own = normalized(own_ref)
    for place in range(2):
        for leg in range(3):
            msg_ref[leg, pl.ds(place, 1), :] = pick(own, place, leg)
    add_gram(info, member, weights, d_ref, first_ref, gram)
    out_ref[0] = gram[:bond, :bond]
    out_ref[1] = gram[:bond, bond:]
    out_ref[2] = gram[bond:, bond:]


def gram_call(kernel, name, extra_specs, out_specs, out_shape, flat, operands):
    rows, bond, wide = flat.shape[1:]
    return pl.pallas_call(
        kernel,
        in_specs=[vmem()] + [vmem()] * 4 + extra_specs,
        out_specs=out_specs,
        out_shape=out_shape,
        scratch_shapes=[pltpu.VMEM((bond, bond), F32), pltpu.VMEM((wide, wide), F32)],
        compiler_params=params(20),
        cost_estimate=cost(wide * flat.size, flat.size),
        name=name,
    )(*operands)


def send_call(info, own, mate, side, flat):
    bond = flat.shape[2]
    shape = jax.ShapeDtypeStruct((2 * bond + 8, bond), F32)
    operands = (info, own, mate, side, flat)
    return gram_call(send_kernel, "gram_to_send", [], vmem(), shape, flat, operands)


def keep_call(info, own, mate, side, flat, after):
    members, _, bond, _ = flat.shape
    shapes = [
        jax.ShapeDtypeStruct((3, bond, bond), F32),
        jax.ShapeDtypeStruct((3, members, bond), F32),
    ]
    operands = (info, own, mate, side, flat, after)
    return gram_call(keep_kernel, "gram_to_keep", [anywhere()], [vmem(), vmem()], shapes, flat, operands)


def eye_mask(size):
    down_index = lax.broadcasted_iota(jnp.int32, (size, size), 0)
    across_index = lax.broadcasted_iota(jnp.int32, (size, size), 1)
    return down_index == across_index


def below_diagonal(size):
    down_index = lax.broadcasted_iota(jnp.int32, (size, size), 0)
    return down_index > lax.broadcasted_iota(jnp.int32, (size, size), 1)


def root_sweeps(matrix):
    size = matrix.shape[0]
    diagonal = eye_mask(size)
    lift = jnp.where(diagonal, 1.5, 0.0).astype(F32)
    scale = jnp.sum(jnp.where(diagonal, matrix, 0.0), keepdims=True)
    current = matrix / scale
    poly = lift - 0.5 * current
    poly_parts = halves(poly)
    current = dot3(halves(current), poly_parts)
    partner = poly
    yield None
    for _ in range(SWEEPS - 1):
        current_parts, partner_parts = (halves(current), halves(partner))
        poly_parts = halves(lift - 0.5 * dot3(partner_parts, current_parts))
        current = dot3(current_parts, poly_parts)
        partner = dot3(poly_parts, partner_parts)
        yield None
    root_scale = jnp.sqrt(scale)
    yield (current * root_scale, partner / root_scale)


def root_pair(matrix):
    for result in root_sweeps(matrix):
        pass
    return result


def root_kernel(keep_ref, got_ref, upper_ref, inverse_ref):
    bond = keep_ref.shape[1]
    merged = got_ref[:bond]
    flipped = jnp.transpose(merged)
    lower = below_diagonal(bond)
    got_below = jnp.where(eye_mask(bond), got_ref[2 * bond : 2 * bond + 1], jnp.where(lower, merged, flipped))
    corner = keep_ref[0] + jnp.where(lower, flipped, merged)
    above = keep_ref[1] + got_ref[bond : 2 * bond]
    below = keep_ref[2] + got_below
    matrix = jnp.concatenate(
        [
            jnp.concatenate([corner, above], axis=1),
            jnp.concatenate([jnp.transpose(above), below], axis=1),
        ],
        axis=0,
    )
    upper_ref[...], inverse_ref[...] = root_pair(matrix)


def root_call(keep, got):
    wide = 2 * keep.shape[1]
    full = jax.ShapeDtypeStruct((wide, wide), F32)
    return pl.pallas_call(
        root_kernel,
        in_specs=[vmem(), vmem()],
        out_specs=[vmem(), vmem()],
        out_shape=[full, full],
        compiler_params=params(16),
        cost_estimate=cost(66 * 2 * wide**3, 16 * wide * wide),
        name="root",
    )(keep, got)


def truncate_kernel(info, gate, own_ref, mate_ref, upper_ref, inverse_ref, other_ref, probes_ref, out_ref):
    wide, bond = (upper_ref.shape[0], probes_ref.shape[1])
    odd = info[0, CORE] == 1
    kept = info[0, KEPT]
    mate_place = jnp.maximum(jnp.where(kept == 0, info[0, MATE0], info[0, MATE1]), 0)
    own_msg = own_ref[pl.ds(3 * kept + 2, 1), :]
    mate_msg = mate_ref[pl.ds(3 * mate_place + 2, 1), :]
    own_msg = own_msg / jnp.sum(own_msg, axis=1, keepdims=True)
    mate_msg = mate_msg / jnp.sum(mate_msg, axis=1, keepdims=True)
    strength = bond * jnp.sqrt(own_msg * mate_msg)
    own_upper, other_upper = (upper_ref[...], other_ref[...])
    left = jnp.where(odd, other_upper, own_upper)
    right = jnp.where(odd, own_upper, other_upper)
    left_parts, right_parts = (halves(left), halves(right))

    def block(value, down_half, across_half):
        return value[
            down_half * bond : (down_half + 1) * bond, across_half * bond : (across_half + 1) * bond
        ]

    def combined(value, entry):
        block_rows = []
        for out_down in range(2):
            blocks = []
            for out_across in range(2):
                total = None
                for first in range(2):
                    for second in range(2):
                        term = entry(out_down, out_across, first, second) * block(value, first, second)
                        total = term if total is None else total + term
                blocks.append(total * strength_down)
            block_rows.append(jnp.concatenate(blocks, axis=1))
        return jnp.concatenate(block_rows, axis=0)

    across = lax.broadcasted_iota(jnp.int32, (1, bond), 1)
    mask = (across < info[0, RANK]).astype(F32)
    strength_down = down(strength)
    probes = jnp.concatenate(
        [probes_ref[pl.ds(0, wide, 2), :] * mask, probes_ref[pl.ds(1, wide, 2), :] * mask], axis=1
    )
    probed = combined(
        dot3(right_parts, halves(probes)),
        lambda s, s_out, t, t_out: gate[2 * s_out + t_out, 2 * s + t],
    )
    sampled = dot3(left_parts, halves(probed))
    sampled_parts = halves(jnp.concatenate([sampled[:, :bond], sampled[:, bond:]], axis=0))
    inner = dot3(sampled_parts, sampled_parts, ((0,), (0,)))
    inner = inner + jnp.where(eye_mask(bond), 1.0 - mask, 0.0)
    sweeps = root_sweeps(inner)
    next(sweeps)
    based = dot3(left_parts, halves(sampled))
    next(sweeps)
    based = combined(based, lambda t, t_out, s, s_out: gate[2 * s_out + t_out, 2 * s + t])
    next(sweeps)
    next(sweeps)
    coeffs = dot3(right_parts, halves(based))
    next(sweeps)
    next(sweeps)
    target = dot3(halves(inverse_ref[...]), halves(jnp.where(odd, coeffs, sampled)))
    for result in sweeps:
        pass
    inner_inverse = result[1]
    inner_parts = halves(inner_inverse)

    def rooted(value):
        return [dot3(halves(value[:, :bond]), inner_parts), dot3(halves(value[:, bond:]), inner_parts)]

    squares = sum(jnp.sum(part * part, axis=0, keepdims=True) for part in rooted(coeffs))
    new_bond = jnp.sqrt(squares / (2 * wide) + 1e-06)
    divisor = jnp.where(odd, new_bond, 1.0)
    change = jnp.concatenate([part / divisor for part in rooted(target)], axis=1)
    gated = info[0, GATED] == 1
    identity = eye_mask(wide).astype(F32)
    out_ref[:wide] = jnp.where(gated, change, identity).astype(BF16)
    bond_parts = halves(jnp.where(gated, new_bond, 0.0))
    out_ref[wide:] = jnp.broadcast_to(jnp.concatenate(bond_parts, axis=1), (16, wide))


def truncate_call(info, gate, own, mate, upper, inverse, other, probes):
    wide = upper.shape[0]
    return pl.pallas_call(
        truncate_kernel,
        in_specs=[vmem()] * 8,
        out_specs=vmem(),
        out_shape=jax.ShapeDtypeStruct((wide + 16, wide), BF16),
        compiler_params=params(32),
        cost_estimate=cost(40 * 2 * wide**3, 24 * wide * wide),
        name="truncate",
    )(info, gate, own, mate, upper, inverse, other, probes)


def update_member(member, pack_ref, d_ref, out_hbm, held, scratch, sems):
    rows, bond, wide = d_ref.shape[1:]
    slots, block = held.shape[:2]
    steps = rows // block

    def put(step):
        slot = lax.rem(step, slots)
        target = out_hbm.at[member, pl.ds(step * block, block)]
        return pltpu.make_async_copy(held.at[slot], target, sems.at[slot])

    def body(step, carry):
        start = step * block
        slot = lax.rem(step, slots)

        @pl.when(step >= slots)
        def free():
            put(step).wait()

        change = pack_ref[:wide]
        for index in range(block):
            if index % 4 == 0:
                rows_in = d_ref[member, pl.ds(start + index, 4)].reshape(4 * bond, wide)
                result = dot_of(rows_in, change)
            lane = scratch.at[index % scratch.shape[0]]
            piece = result[index % 4 * bond : (index % 4 + 1) * bond]
            lane[pl.ds(0, bond, 2), :] = piece[:, :bond]
            lane[pl.ds(1, bond, 2), :] = piece[:, bond:]
            held[slot, index] = lane[...].astype(BF16)
        put(step).start()
        return carry

    lax.fori_loop(0, steps, body, 0)
    for step in range(steps - slots, steps):
        put(step).wait()


def own_kernel(info, pack_ref, d_ref, after, out_hbm, held, scratch, sems):
    update_member(info[0, KEPT], pack_ref, d_ref, out_hbm, held, scratch, sems)


def other_kernel(info, pack_ref, got_ref, d_ref, begun_hbm, out_hbm, bond_hbm, held, scratch, sems, bond_ref, bond_sem):
    bond, wide = d_ref.shape[2:]
    kept = info[0, KEPT]
    tail = pack_ref[wide:].astype(F32)
    got = got_ref[wide:].astype(F32)
    mine = tail[:1, :bond] + tail[:1, bond:]
    other = got[:1, :bond] + got[:1, bond:]
    bond_ref[pl.ds(0, 1), :] = jnp.where(kept == 0, mine, other)
    bond_ref[pl.ds(1, 1), :] = jnp.where(kept == 0, other, mine)
    bond_copy = pltpu.make_async_copy(bond_ref, bond_hbm, bond_sem)
    bond_copy.start()
    update_member(1 - kept, got_ref, d_ref, out_hbm, held, scratch, sems)
    bond_copy.wait()


def update_call(kernel, name, in_specs, aliases, with_bonds, flat, operands):
    members, rows, bond, wide = flat.shape
    block, slots = (16, 4)
    tensor = jax.ShapeDtypeStruct((members, rows, wide, bond), BF16)
    bonds = jax.ShapeDtypeStruct((members, bond), F32)
    return pl.pallas_call(
        kernel,
        in_specs=in_specs,
        out_specs=[hbm(), hbm()] if with_bonds else hbm(),
        out_shape=[tensor, bonds] if with_bonds else tensor,
        input_output_aliases=aliases,
        scratch_shapes=[
            pltpu.VMEM((slots, block, wide, bond), BF16),
            pltpu.VMEM((4, wide, bond), F32),
            pltpu.SemaphoreType.DMA((slots,)),
        ]
        + ([pltpu.VMEM((members, bond), F32), pltpu.SemaphoreType.DMA(())] if with_bonds else []),
        compiler_params=params(24),
        cost_estimate=cost(wide * flat.size, 2 * flat.size),
        name=name,
    )(*operands)


def own_call(info, pack, flat, after):
    specs = [vmem(), vmem(), vmem(), anywhere()]
    return update_call(own_kernel, "update_own", specs, {}, False, flat, (info, pack, flat, after))


def other_call(info, pack, got, flat, begun):
    specs = [vmem(), vmem(), vmem(), vmem(), hbm()]
    operands = (info, pack, got, flat, begun)
    return update_call(other_kernel, "update_other", specs, {4: 0}, True, flat, operands)


def shards(tensors, neighbours, edge_ranks, gate_matrix, probes):
    members, rows, bond, phys = tensors.shape[:4]
    sites = lax.axis_size("site")
    row_swap = [(0, 1), (1, 0)]
    core_swap = [(i, i ^ 1) for i in range(sites)]
    side_swap = [(i, i + 1) for i in range(1, sites - 1, 2)]
    side_swap += [(j, i) for i, j in side_swap]
    x = tensors.reshape(members, rows, bond * phys, bond)
    x, squares, part = open_call(x)
    info = scalars_call(part, neighbours.T, edge_ranks)
    for index in range(ROUNDS):
        if index > 0:
            begun = inner_call(info, own, mate, squares)
            part = outer_call(info, side, *begun)
        got = lax.ppermute(part, "row", row_swap)
        own = part + got if index > 0 else add_call(part, got, info)
        side = lax.ppermute(own, "site", side_swap)
        mate = lax.ppermute(own, "site", core_swap)
    flat = flatten_call(own, x)
    send = send_call(info, own, mate, side, flat)
    got = lax.ppermute(send, "row", row_swap)
    keep, messages = keep_call(info, own, mate, side, flat, send)
    upper, inverse = root_call(keep, got)
    other = lax.ppermute(upper, "site", core_swap)
    pack = truncate_call(info, gate_matrix, own, mate, upper, inverse, other, probes)
    got_pack = lax.ppermute(pack, "row", row_swap)
    begun = own_call(info, pack, flat, pack)
    updated, bonds = other_call(info, pack, got_pack, flat, begun)
    return (updated.reshape(tensors.shape), messages.transpose(1, 0, 2), bonds)


def solution(mesh):
    return jax.shard_map(
        shards,
        mesh=mesh,
        in_specs=(P("site", "row", None, None, None), P(), P(), P(), P()),
        out_specs=(P("site", "row", None, None, None), P("site", None, None), P("site", None)),
        check_vma=False,
    )
```

```python
import functools

import jax
import jax.numpy as jnp
from jax import lax
from jax.experimental import pallas as pl
from jax.experimental.pallas import tpu as pltpu
from jax.sharding import PartitionSpec as P

ROUNDS = 4
SWEEPS = 8
F32 = jnp.float32
BF16 = jnp.bfloat16
MB = 1 << 20

CORE, ROW, MATE0, MATE1, FIRST, LAST, KEPT, RANK, GATED = range(9)


def smem():
    return pl.BlockSpec(memory_space=pltpu.SMEM)


def vmem():
    return pl.BlockSpec(memory_space=pltpu.VMEM)


def params(mib):
    return pltpu.CompilerParams(vmem_limit_bytes=mib * MB)


def cost(flops, moved):
    return pl.CostEstimate(flops=int(flops), bytes_accessed=int(moved), transcendentals=0)


def halves(value):
    high = value.astype(BF16)
    low = (value - high.astype(F32)).astype(BF16)
    return (high, low)


def dot_of(left, right, dims=((1,), (0,))):
    return lax.dot_general(left, right, (dims, ((), ())), preferred_element_type=F32)


def dot3(left, right, dims=((1,), (0,))):
    return dot_of(left[0], right[0], dims) + (
        dot_of(left[0], right[1], dims) + dot_of(left[1], right[0], dims)
    )


def down(row):
    size = row.shape[-1]
    return jnp.transpose(jnp.broadcast_to(row, (size, size)))


def normalized(ref):
    rows = ref[...]
    return rows / jnp.sum(rows, axis=1, keepdims=True)


def pick(rows, member, leg):
    return rows[3 * member + leg : 3 * member + leg + 1]


def level(rows):
    return jnp.full((1, rows.shape[-1]), 1.0 / rows.shape[-1], F32)


def from_mate(mate, place):
    return jnp.where(place == 0, pick(mate, 0, 2), pick(mate, 1, 2))


def inner_incoming(info, own, mate):
    odd = info[0, CORE] == 1
    place = jnp.where(odd, info[0, MATE0], info[0, MATE1])
    joined = place == info[0, CORE]
    chain = jnp.where(odd, pick(mate, 1, 1), pick(mate, 0, 0))
    gated = jnp.where(odd, pick(mate, 1, 2), pick(mate, 0, 2))
    near = chain + jnp.where(joined, gated, 0.0)
    home = jnp.where(odd, pick(own, 1, 0), pick(own, 0, 1))
    third = from_mate(mate, place) + jnp.where(joined, chain, 0.0)
    return (
        jnp.where(odd, near, home),
        jnp.where(odd, home, near),
        jnp.where(place < 0, level(own), third),
    )


def outer_known(info, own, mate):
    odd = info[0, CORE] == 1
    place = jnp.where(odd, info[0, MATE1], info[0, MATE0])
    home = jnp.where(odd, pick(own, 0, 1), pick(own, 1, 0))
    return (home, jnp.where(place < 0, level(own), from_mate(mate, place)))


def outer_far(info, side):
    far = jnp.where(info[0, CORE] == 1, pick(side, 0, 0), pick(side, 1, 1))
    return jnp.where(info[0, FIRST] + info[0, LAST] > 0, level(side), far)


def outer_incoming(info, own, mate, side):
    odd = info[0, CORE] == 1
    home, third = outer_known(info, own, mate)
    far = outer_far(info, side)
    return (jnp.where(odd, home, far), jnp.where(odd, far, home), third)


def hbm():
    return pl.BlockSpec(memory_space=pltpu.HBM)


def anywhere():
    return pl.BlockSpec(memory_space=pl.ANY)


def scalars_kernel(after, near, ranks, out_ref):
    device, row = (lax.axis_index("site"), lax.axis_index("row"))
    core = lax.rem(device, 2)
    base = 2 * (device - core)
    even0, even1 = (near[2, base] - base, near[2, base + 1] - base)
    odd0, odd1 = (near[2, base + 2], near[2, base + 3])
    odd = core == 1
    crossed = jnp.logical_or(even0 == 3, even1 == 2)
    kept = jnp.where(jnp.logical_and(odd, crossed), 1 - row, row)
    site = 2 * device + kept
    values = {
        CORE: core,
        ROW: row,
        MATE0: jnp.where(odd, jnp.where(odd0 < 0, -1, odd0 - base), jnp.maximum(even0 - 2, -1)),
        MATE1: jnp.where(odd, jnp.where(odd1 < 0, -1, odd1 - base), jnp.maximum(even1 - 2, -1)),
        FIRST: (device == 0).astype(jnp.int32),
        LAST: (device == lax.axis_size("site") - 1).astype(jnp.int32),
        KEPT: kept,
        RANK: ranks[site],
        GATED: (near[2, site] >= 0).astype(jnp.int32),
    }
    lanes = lax.broadcasted_iota(jnp.int32, out_ref.shape, 1)
    total = jnp.zeros(out_ref.shape, jnp.int32)
    for place, value in values.items():
        total = jnp.where(lanes == place, value, total)
    out_ref[...] = total


def scalars_call(after, near, ranks):
    return pl.pallas_call(
        scalars_kernel,
        in_specs=[anywhere(), smem(), smem()],
        out_specs=vmem(),
        out_shape=jax.ShapeDtypeStruct((8, 128), jnp.int32),
        compiler_params=params(4),
        cost_estimate=cost(1024, 1 << 20),
        name="scalars",
    )(after, near, ranks)


def add_kernel(one_ref, two_ref, after, out_ref):
    out_ref[...] = one_ref[...] + two_ref[...]


def add_call(one, two, after):
    return pl.pallas_call(
        add_kernel,
        in_specs=[vmem(), vmem(), anywhere()],
        out_specs=vmem(),
        out_shape=jax.ShapeDtypeStruct(one.shape, F32),
        compiler_params=params(4),
        cost_estimate=cost(one.size, 12 * one.size),
        name="add",
    )(one, two, after)


def open_kernel(x_hbm, x_ref, s_ref, out_ref, scratch, sums_ref, total_ref, sems):
    members, rows, wide, bond = x_hbm.shape
    steps = sems.shape[0]
    per = steps // members
    block = rows // per

    def fetch(step):
        place = (step // per, pl.ds(lax.rem(step, per) * block, block))
        return pltpu.make_async_copy(x_hbm.at[place], x_ref.at[place], sems.at[step])

    for step in range(steps):
        fetch(step).start()
    total_ref[...] = jnp.zeros(total_ref.shape, F32)

    def body(step, carry):
        fetch(step).wait()
        member, start = (step // per, lax.rem(step, per) * block)
        total = total_ref[member]
        for index in range(block):
            lane = scratch.at[index % scratch.shape[0]]
            lane[...] = x_ref[member, start + index].astype(F32)
            even = lane[pl.ds(0, bond, 2), :]
            odd = lane[pl.ds(1, bond, 2), :]
            square = even * even + odd * odd
            s_ref[member, start + index] = square.astype(BF16)
            sums_ref[member, start + index] = jnp.sum(square.reshape(bond // 8, 8, bond), axis=0)
            total = total + square
        total_ref[member] = total
        return carry

    lax.fori_loop(0, steps, body, 0)
    row = lax.axis_index("row")
    flat_weight = jnp.ones((1, bond), F32)
    out_ref[...] = jnp.ones(out_ref.shape, F32)
    for member in range(members):
        finish(row, out_ref, member, sums_ref[member], total_ref[member], flat_weight, None)


def open_call(x):
    members, rows, wide, bond = x.shape
    block = 16
    steps = members * rows // block
    return pl.pallas_call(
        open_kernel,
        in_specs=[hbm()],
        out_specs=[vmem(), vmem(), vmem()],
        out_shape=[
            jax.ShapeDtypeStruct(x.shape, BF16),
            jax.ShapeDtypeStruct((members, rows, bond, bond), BF16),
            jax.ShapeDtypeStruct((8, bond), F32),
        ],
        scratch_shapes=[
            pltpu.VMEM((4, wide, bond), F32),
            pltpu.VMEM((members, rows, 8, bond), F32),
            pltpu.VMEM((members, bond, bond), F32),
            pltpu.SemaphoreType.DMA((steps,)),
        ],
        compiler_params=params(38),
        cost_estimate=cost(4 * x.size, 5 * x.size),
        name="open",
    )(x)


def flatten_kernel(after, x_ref, flat_ref, scratch):
    members, rows, bond = flat_ref.shape[:3]
    for member in range(members):

        def body(index, carry):
            lane = scratch.at[lax.rem(index, scratch.shape[0])]
            lane[...] = x_ref[member, index].astype(F32)
            parts = [lane[pl.ds(place, bond, 2), :] for place in range(2)]
            flat_ref[member, index] = jnp.concatenate(parts, axis=1).astype(BF16)
            return carry

        lax.fori_loop(0, rows, body, 0, unroll=8)


def flatten_call(after, x):
    members, rows, wide, bond = x.shape
    return pl.pallas_call(
        flatten_kernel,
        in_specs=[anywhere(), vmem()],
        out_specs=vmem(),
        out_shape=jax.ShapeDtypeStruct((members, rows, bond, wide), BF16),
        scratch_shapes=[pltpu.VMEM((8, wide, bond), F32)],
        compiler_params=params(8),
        cost_estimate=cost(2 * x.size, 4 * x.size),
        name="flatten",
    )(after, x)


def halved(row_index, row):
    half = row.shape[1] // 2
    return jnp.where(row_index == 0, row[:, :half], row[:, half:])


def placed(row_index, half):
    empty = jnp.zeros_like(half)
    return jnp.where(
        row_index == 0,
        jnp.concatenate([half, empty], axis=1),
        jnp.concatenate([empty, half], axis=1),
    )


def by_row(row, matrix):
    return dot3(halves(jnp.broadcast_to(row, (16, row.shape[1]))), halves(matrix))[:1]


def by_column(row, matrix):
    return dot3(halves(jnp.broadcast_to(row, (16, row.shape[1]))), halves(matrix), ((1,), (1,)))[:1]


def put_leg(out_ref, member, leg, row):
    out_ref[pl.ds(3 * member + leg, 1), :] = row


def finish(row_index, out_ref, member, sums, total, third, second_down):
    bond = total.shape[0]
    half = by_column(jnp.ones((1, bond), F32), jnp.sum(sums, axis=1))
    weighted = total if second_down is None else total * second_down
    put_leg(out_ref, member, 0, placed(row_index, half))
    put_leg(out_ref, member, 1, by_column(third, total))
    put_leg(out_ref, member, 2, jnp.sum(weighted, axis=0, keepdims=True))


GROUP = 4


def scaled_sum(s_ref, member, step, first_ref, start):
    bond = s_ref.shape[2]
    joined = None
    for place in range(GROUP):
        index = step * GROUP + place
        scale = jnp.broadcast_to(first_ref[pl.ds(start + index, 1), :], (16, bond)).astype(BF16)
        term = jnp.concatenate([scale] * (bond // 16), axis=0) * s_ref[member, index]
        joined = term if joined is None else joined + term
    return joined.astype(F32)


def contract_inner(info, weights, s_ref, out_ref, first_ref, sums_ref):
    rows, bond = s_ref.shape[1:3]
    member = 1 - info[0, CORE]
    start = info[0, ROW] * rows
    first, second, third = weights
    third = third.astype(BF16).astype(F32)
    first_ref[...] = down(first)
    second_down = down(second)
    outer = (second_down * third).astype(BF16)

    def body(step, total):
        for place in range(GROUP):
            index = step * GROUP + place
            piece = s_ref[member, index] * outer
            piece = piece[:64] + piece[64:]
            piece = (piece[:32] + piece[32:]).astype(F32)
            sums_ref[index] = (piece[:8] + piece[8:16]) + (piece[16:24] + piece[24:])
        return total + scaled_sum(s_ref, member, step, first_ref, start)

    total = lax.fori_loop(0, rows // GROUP, body, jnp.zeros((bond, bond), F32), unroll=2)
    finish(info[0, ROW], out_ref, member, sums_ref[...], total, third, second_down)


def contract_outer(info, home, third, s_ref, out_ref, mixed_ref, other_ref, first_ref):
    rows, bond = s_ref.shape[1:3]
    member = info[0, CORE]
    odd = info[0, CORE] == 1
    start = info[0, ROW] * rows
    third_rows = jnp.broadcast_to(third.astype(BF16), (8, bond))

    def mix(step, carry):
        pair = s_ref[member, pl.ds(2 * step, 2)].reshape(2 * bond, bond)
        product = dot_of(third_rows, pair, ((1,), (1,)))
        mixed_ref[pl.ds(2 * step, 1), :] = product[:1, :bond]
        mixed_ref[pl.ds(2 * step + 1, 1), :] = product[:1, bond:]
        return carry

    lax.fori_loop(0, rows // 2, mix, 0, unroll=8)

    @pl.when(odd)
    def over_first():
        first_ref[...] = down(home)

        def body(step, total):
            return total + scaled_sum(s_ref, member, step, first_ref, start)

        zero = jnp.zeros((bond, bond), F32)
        other_ref[...] = lax.fori_loop(0, rows // GROUP, body, zero, unroll=2)
        put_leg(out_ref, member, 1, by_row(halved(info[0, ROW], home), mixed_ref[...]))

    @pl.when(jnp.logical_not(odd))
    def over_second():
        second_rows = jnp.concatenate(halves(home) + (jnp.zeros((6, bond), BF16),), axis=0)

        def body(step, carry):
            pair = jnp.concatenate([s_ref[member, 2 * step], s_ref[member, 2 * step + 1]], axis=1)
            product = dot_of(second_rows, pair)
            product = product[:1] + product[1:2]
            other_ref[pl.ds(2 * step, 1), :] = product[:, :bond]
            other_ref[pl.ds(2 * step + 1, 1), :] = product[:, bond:]
            return carry

        lax.fori_loop(0, rows // 2, body, 0, unroll=8)
        put_leg(out_ref, member, 0, placed(info[0, ROW], by_column(home, mixed_ref[...])))


def inner_kernel(info, own_ref, mate_ref, s_ref, out_ref, mixed_ref, other_ref, first_ref, sums_ref):
    own, mate = (normalized(own_ref), normalized(mate_ref))
    out_ref[...] = jnp.ones(out_ref.shape, F32)
    contract_inner(info, inner_incoming(info, own, mate), s_ref, out_ref, first_ref, sums_ref)
    home, third = outer_known(info, own, mate)
    contract_outer(info, home, third, s_ref, out_ref, mixed_ref, other_ref, first_ref)


def outer_kernel(info, side_ref, part_ref, mixed_ref, other_ref, out_ref):
    rows = mixed_ref.shape[0]
    far = outer_far(info, normalized(side_ref))
    out_ref[...] = part_ref[...]

    @pl.when(info[0, CORE] == 1)
    def as_second():
        put_leg(out_ref, 1, 0, placed(info[0, ROW], by_column(far, mixed_ref[...])))
        put_leg(out_ref, 1, 2, by_row(far, other_ref[...]))

    @pl.when(info[0, CORE] == 0)
    def as_first():
        half = halved(info[0, ROW], far)
        put_leg(out_ref, 0, 1, by_row(half, mixed_ref[...]))
        put_leg(out_ref, 0, 2, by_row(half, other_ref[:rows]))


def inner_call(info, own, mate, squares):
    rows, bond = squares.shape[1:3]
    return pl.pallas_call(
        inner_kernel,
        in_specs=[vmem(), vmem(), vmem(), vmem()],
        out_specs=[vmem(), vmem(), vmem()],
        out_shape=[
            jax.ShapeDtypeStruct((8, bond), F32),
            jax.ShapeDtypeStruct((rows, bond), F32),
            jax.ShapeDtypeStruct((bond, bond), F32),
        ],
        scratch_shapes=[pltpu.VMEM((bond, bond), F32), pltpu.VMEM((rows, 8, bond), F32)],
        compiler_params=params(8),
        cost_estimate=cost(4 * squares.size, 2 * squares.size),
        name="inner_round",
    )(info, own, mate, squares)


def outer_call(info, side, part, mixed, other):
    return pl.pallas_call(
        outer_kernel,
        in_specs=[vmem(), vmem(), vmem(), vmem(), vmem()],
        out_specs=vmem(),
        out_shape=jax.ShapeDtypeStruct(part.shape, F32),
        compiler_params=params(8),
        cost_estimate=cost(8 * mixed.size, 8 * mixed.size),
        name="outer_round",
    )(info, side, part, mixed, other)


def add_gram(info, member, weights, d_ref, first_ref, gram):
    rows, bond = d_ref.shape[1:3]
    block = 64
    start = info[0, ROW] * rows
    first_ref[...] = down(jnp.sqrt(weights[0]))
    second = down(jnp.sqrt(weights[1]))
    gram[...] = jnp.zeros(gram.shape, F32)

    def body(step, carry):
        parts = []
        for place in range(block):
            index = step * block + place
            scale = first_ref[pl.ds(start + index, 1), :] * second
            piece = d_ref[member, index].astype(F32) * jnp.concatenate([scale, scale], axis=1)
            parts.append(piece.astype(BF16))
        weighted = jnp.concatenate(parts, axis=0)
        gram[...] += dot_of(weighted, weighted, ((0,), (0,)))
        return carry

    lax.fori_loop(0, rows // block, body, 0)


def gram_weights(info, member, own_ref, mate_ref, side_ref):
    own, mate, side = (normalized(own_ref), normalized(mate_ref), normalized(side_ref))
    inner = inner_incoming(info, own, mate)
    outer = outer_incoming(info, own, mate, side)
    return [jnp.where(member == info[0, CORE], outer[leg], inner[leg]) for leg in range(2)]


def send_kernel(info, own_ref, mate_ref, side_ref, d_ref, out_ref, first_ref, gram):
    bond = d_ref.shape[2]
    member = 1 - info[0, KEPT]
    weights = gram_weights(info, member, own_ref, mate_ref, side_ref)
    add_gram(info, member, weights, d_ref, first_ref, gram)
    corner, above, below = (gram[:bond, :bond], gram[:bond, bond:], gram[bond:, bond:])
    out_ref[:bond] = jnp.where(below_diagonal(bond), below, corner)
    out_ref[bond : 2 * bond] = above
    diagonal = jnp.sum(jnp.where(eye_mask(bond), below, 0.0), axis=0, keepdims=True)
    out_ref[2 * bond :] = jnp.broadcast_to(diagonal, (8, bond))


def keep_kernel(info, own_ref, mate_ref, side_ref, d_ref, after, out_ref, msg_ref, first_ref, gram):
    bond = d_ref.shape[2]
    member = info[0, KEPT]
    weights = gram_weights(info, member, own_ref, mate_ref, side_ref)
    own = normalized(own_ref)
    for place in range(2):
        for leg in range(3):
            msg_ref[leg, pl.ds(place, 1), :] = pick(own, place, leg)
    add_gram(info, member, weights, d_ref, first_ref, gram)
    out_ref[0] = gram[:bond, :bond]
    out_ref[1] = gram[:bond, bond:]
    out_ref[2] = gram[bond:, bond:]


def gram_call(kernel, name, extra_specs, out_specs, out_shape, flat, operands):
    rows, bond, wide = flat.shape[1:]
    return pl.pallas_call(
        kernel,
        in_specs=[vmem()] + [vmem()] * 4 + extra_specs,
        out_specs=out_specs,
        out_shape=out_shape,
        scratch_shapes=[pltpu.VMEM((bond, bond), F32), pltpu.VMEM((wide, wide), F32)],
        compiler_params=params(20),
        cost_estimate=cost(wide * flat.size, flat.size),
        name=name,
    )(*operands)


def send_call(info, own, mate, side, flat):
    bond = flat.shape[2]
    shape = jax.ShapeDtypeStruct((2 * bond + 8, bond), F32)
    operands = (info, own, mate, side, flat)
    return gram_call(send_kernel, "gram_to_send", [], vmem(), shape, flat, operands)


def keep_call(info, own, mate, side, flat, after):
    members, _, bond, _ = flat.shape
    shapes = [
        jax.ShapeDtypeStruct((3, bond, bond), F32),
        jax.ShapeDtypeStruct((3, members, bond), F32),
    ]
    operands = (info, own, mate, side, flat, after)
    return gram_call(keep_kernel, "gram_to_keep", [anywhere()], [vmem(), vmem()], shapes, flat, operands)


def eye_mask(size):
    down_index = lax.broadcasted_iota(jnp.int32, (size, size), 0)
    across_index = lax.broadcasted_iota(jnp.int32, (size, size), 1)
    return down_index == across_index


def below_diagonal(size):
    down_index = lax.broadcasted_iota(jnp.int32, (size, size), 0)
    return down_index > lax.broadcasted_iota(jnp.int32, (size, size), 1)


def root_sweeps(matrix):
    size = matrix.shape[0]
    diagonal = eye_mask(size)
    lift = jnp.where(diagonal, 1.5, 0.0).astype(F32)
    scale = jnp.sum(jnp.where(diagonal, matrix, 0.0), keepdims=True)
    current = matrix / scale
    poly = lift - 0.5 * current
    poly_parts = halves(poly)
    current = dot3(halves(current), poly_parts)
    partner = poly
    yield None
    for _ in range(SWEEPS - 1):
        current_parts, partner_parts = (halves(current), halves(partner))
        poly_parts = halves(lift - 0.5 * dot3(partner_parts, current_parts))
        current = dot3(current_parts, poly_parts)
        partner = dot3(poly_parts, partner_parts)
        yield None
    root_scale = jnp.sqrt(scale)
    yield (current * root_scale, partner / root_scale)


def root_pair(matrix):
    for result in root_sweeps(matrix):
        pass
    return result


def root_kernel(keep_ref, got_ref, upper_ref, inverse_ref):
    bond = keep_ref.shape[1]
    merged = got_ref[:bond]
    flipped = jnp.transpose(merged)
    lower = below_diagonal(bond)
    got_below = jnp.where(eye_mask(bond), got_ref[2 * bond : 2 * bond + 1], jnp.where(lower, merged, flipped))
    corner = keep_ref[0] + jnp.where(lower, flipped, merged)
    above = keep_ref[1] + got_ref[bond : 2 * bond]
    below = keep_ref[2] + got_below
    matrix = jnp.concatenate(
        [
            jnp.concatenate([corner, above], axis=1),
            jnp.concatenate([jnp.transpose(above), below], axis=1),
        ],
        axis=0,
    )
    upper_ref[...], inverse_ref[...] = root_pair(matrix)


def root_call(keep, got):
    wide = 2 * keep.shape[1]
    full = jax.ShapeDtypeStruct((wide, wide), F32)
    return pl.pallas_call(
        root_kernel,
        in_specs=[vmem(), vmem()],
        out_specs=[vmem(), vmem()],
        out_shape=[full, full],
        compiler_params=params(16),
        cost_estimate=cost(66 * 2 * wide**3, 16 * wide * wide),
        name="root",
    )(keep, got)


def truncate_kernel(info, gate, own_ref, mate_ref, upper_ref, inverse_ref, other_ref, probes_ref, out_ref):
    wide, bond = (upper_ref.shape[0], probes_ref.shape[1])
    odd = info[0, CORE] == 1
    kept = info[0, KEPT]
    mate_place = jnp.maximum(jnp.where(kept == 0, info[0, MATE0], info[0, MATE1]), 0)
    own_msg = own_ref[pl.ds(3 * kept + 2, 1), :]
    mate_msg = mate_ref[pl.ds(3 * mate_place + 2, 1), :]
    own_msg = own_msg / jnp.sum(own_msg, axis=1, keepdims=True)
    mate_msg = mate_msg / jnp.sum(mate_msg, axis=1, keepdims=True)
    strength = bond * jnp.sqrt(own_msg * mate_msg)
    own_upper, other_upper = (upper_ref[...], other_ref[...])
    left = jnp.where(odd, other_upper, own_upper)
    right = jnp.where(odd, own_upper, other_upper)
    left_parts, right_parts = (halves(left), halves(right))

    def block(value, down_half, across_half):
        return value[
            down_half * bond : (down_half + 1) * bond, across_half * bond : (across_half + 1) * bond
        ]

    def combined(value, entry):
        block_rows = []
        for out_down in range(2):
            blocks = []
            for out_across in range(2):
                total = None
                for first in range(2):
                    for second in range(2):
                        term = entry(out_down, out_across, first, second) * block(value, first, second)
                        total = term if total is None else total + term
                blocks.append(total * strength_down)
            block_rows.append(jnp.concatenate(blocks, axis=1))
        return jnp.concatenate(block_rows, axis=0)

    across = lax.broadcasted_iota(jnp.int32, (1, bond), 1)
    mask = (across < info[0, RANK]).astype(F32)
    strength_down = down(strength)
    probes = jnp.concatenate(
        [probes_ref[pl.ds(0, wide, 2), :] * mask, probes_ref[pl.ds(1, wide, 2), :] * mask], axis=1
    )
    probed = combined(
        dot3(right_parts, halves(probes)),
        lambda s, s_out, t, t_out: gate[2 * s_out + t_out, 2 * s + t],
    )
    sampled = dot3(left_parts, halves(probed))
    sampled_parts = halves(jnp.concatenate([sampled[:, :bond], sampled[:, bond:]], axis=0))
    inner = dot3(sampled_parts, sampled_parts, ((0,), (0,)))
    inner = inner + jnp.where(eye_mask(bond), 1.0 - mask, 0.0)
    sweeps = root_sweeps(inner)
    next(sweeps)
    based = dot3(left_parts, halves(sampled))
    next(sweeps)
    based = combined(based, lambda t, t_out, s, s_out: gate[2 * s_out + t_out, 2 * s + t])
    next(sweeps)
    next(sweeps)
    coeffs = dot3(right_parts, halves(based))
    next(sweeps)
    next(sweeps)
    target = dot3(halves(inverse_ref[...]), halves(jnp.where(odd, coeffs, sampled)))
    for result in sweeps:
        pass
    inner_inverse = result[1]
    inner_parts = halves(inner_inverse)

    def rooted(value):
        return [dot3(halves(value[:, :bond]), inner_parts), dot3(halves(value[:, bond:]), inner_parts)]

    squares = sum(jnp.sum(part * part, axis=0, keepdims=True) for part in rooted(coeffs))
    new_bond = jnp.sqrt(squares / (2 * wide) + 1e-06)
    divisor = jnp.where(odd, new_bond, 1.0)
    change = jnp.concatenate([part / divisor for part in rooted(target)], axis=1)
    gated = info[0, GATED] == 1
    identity = eye_mask(wide).astype(F32)
    out_ref[:wide] = jnp.where(gated, change, identity).astype(BF16)
    bond_parts = halves(jnp.where(gated, new_bond, 0.0))
    out_ref[wide:] = jnp.broadcast_to(jnp.concatenate(bond_parts, axis=1), (16, wide))


def truncate_call(info, gate, own, mate, upper, inverse, other, probes):
    wide = upper.shape[0]
    return pl.pallas_call(
        truncate_kernel,
        in_specs=[vmem()] * 8,
        out_specs=vmem(),
        out_shape=jax.ShapeDtypeStruct((wide + 16, wide), BF16),
        compiler_params=params(32),
        cost_estimate=cost(40 * 2 * wide**3, 24 * wide * wide),
        name="truncate",
    )(info, gate, own, mate, upper, inverse, other, probes)


def update_member(member, pack_ref, d_ref, out_hbm, held, scratch, sems):
    rows, bond, wide = d_ref.shape[1:]
    slots, block = held.shape[:2]
    steps = rows // block

    def put(step):
        slot = step % slots
        target = out_hbm.at[member, pl.ds(step * block, block)]
        return pltpu.make_async_copy(held.at[slot], target, sems.at[slot])

    change = pack_ref[:wide]
    for step in range(steps):
        slot = step % slots
        if step >= slots:
            put(step - slots).wait()
        for index in range(block):
            if index % 4 == 0:
                rows_in = d_ref[member, pl.ds(step * block + index, 4)].reshape(4 * bond, wide)
                result = dot_of(rows_in, change)
            lane = scratch.at[index % scratch.shape[0]]
            piece = result[index % 4 * bond : (index % 4 + 1) * bond]
            lane[pl.ds(0, bond, 2), :] = piece[:, :bond]
            lane[pl.ds(1, bond, 2), :] = piece[:, bond:]
            held[slot, index] = lane[...].astype(BF16)
        put(step).start()
    for step in range(steps - slots, steps):
        put(step).wait()


def own_kernel(info, pack_ref, d_ref, after, out_hbm, held, scratch, sems):
    update_member(info[0, KEPT], pack_ref, d_ref, out_hbm, held, scratch, sems)


def other_kernel(info, pack_ref, got_ref, d_ref, begun_hbm, out_hbm, bond_hbm, held, scratch, sems, bond_ref, bond_sem):
    bond, wide = d_ref.shape[2:]
    kept = info[0, KEPT]
    tail = pack_ref[wide:].astype(F32)
    got = got_ref[wide:].astype(F32)
    mine = tail[:1, :bond] + tail[:1, bond:]
    other = got[:1, :bond] + got[:1, bond:]
    bond_ref[pl.ds(0, 1), :] = jnp.where(kept == 0, mine, other)
    bond_ref[pl.ds(1, 1), :] = jnp.where(kept == 0, other, mine)
    bond_copy = pltpu.make_async_copy(bond_ref, bond_hbm, bond_sem)
    bond_copy.start()
    update_member(1 - kept, got_ref, d_ref, out_hbm, held, scratch, sems)
    bond_copy.wait()


def update_call(kernel, name, in_specs, aliases, with_bonds, flat, operands):
    members, rows, bond, wide = flat.shape
    block, slots = (8, 8)
    tensor = jax.ShapeDtypeStruct((members, rows, wide, bond), BF16)
    bonds = jax.ShapeDtypeStruct((members, bond), F32)
    return pl.pallas_call(
        kernel,
        in_specs=in_specs,
        out_specs=[hbm(), hbm()] if with_bonds else hbm(),
        out_shape=[tensor, bonds] if with_bonds else tensor,
        input_output_aliases=aliases,
        scratch_shapes=[
            pltpu.VMEM((slots, block, wide, bond), BF16),
            pltpu.VMEM((4, wide, bond), F32),
            pltpu.SemaphoreType.DMA((slots,)),
        ]
        + ([pltpu.VMEM((members, bond), F32), pltpu.SemaphoreType.DMA(())] if with_bonds else []),
        compiler_params=params(24),
        cost_estimate=cost(wide * flat.size, 2 * flat.size),
        name=name,
    )(*operands)


def own_call(info, pack, flat, after):
    specs = [vmem(), vmem(), vmem(), anywhere()]
    return update_call(own_kernel, "update_own", specs, {}, False, flat, (info, pack, flat, after))


def other_call(info, pack, got, flat, begun):
    specs = [vmem(), vmem(), vmem(), vmem(), hbm()]
    operands = (info, pack, got, flat, begun)
    return update_call(other_kernel, "update_other", specs, {4: 0}, True, flat, operands)


def shards(tensors, neighbours, edge_ranks, gate_matrix, probes):
    members, rows, bond, phys = tensors.shape[:4]
    sites = lax.axis_size("site")
    row_swap = [(0, 1), (1, 0)]
    core_swap = [(i, i ^ 1) for i in range(sites)]
    side_swap = [(i, i + 1) for i in range(1, sites - 1, 2)]
    side_swap += [(j, i) for i, j in side_swap]
    x = tensors.reshape(members, rows, bond * phys, bond)
    x, squares, part = open_call(x)
    info = scalars_call(part, neighbours.T, edge_ranks)
    for index in range(ROUNDS):
        if index > 0:
            begun = inner_call(info, own, mate, squares)
            part = outer_call(info, side, *begun)
        got = lax.ppermute(part, "row", row_swap)
        own = part + got if index > 0 else add_call(part, got, info)
        side = lax.ppermute(own, "site", side_swap)
        mate = lax.ppermute(own, "site", core_swap)
    flat = flatten_call(own, x)
    send = send_call(info, own, mate, side, flat)
    got = lax.ppermute(send, "row", row_swap)
    keep, messages = keep_call(info, own, mate, side, flat, send)
    upper, inverse = root_call(keep, got)
    other = lax.ppermute(upper, "site", core_swap)
    pack = truncate_call(info, gate_matrix, own, mate, upper, inverse, other, probes)
    got_pack = lax.ppermute(pack, "row", row_swap)
    begun = own_call(info, pack, flat, pack)
    updated, bonds = other_call(info, pack, got_pack, flat, begun)
    return (updated.reshape(tensors.shape), messages.transpose(1, 0, 2), bonds)


def solution(mesh):
    return jax.shard_map(
        shards,
        mesh=mesh,
        in_specs=(P("site", "row", None, None, None), P(), P(), P(), P()),
        out_specs=(P("site", "row", None, None, None), P("site", None, None), P("site", None)),
        check_vma=False,
    )
```

```python
import functools

import jax
import jax.numpy as jnp
from jax import lax
from jax.experimental import pallas as pl
from jax.experimental.pallas import tpu as pltpu
from jax.sharding import PartitionSpec as P

ROUNDS = 4
SWEEPS = 8
F32 = jnp.float32
BF16 = jnp.bfloat16
MB = 1 << 20

CORE, ROW, MATE0, MATE1, FIRST, LAST, KEPT, RANK, GATED = range(9)


def smem():
    return pl.BlockSpec(memory_space=pltpu.SMEM)


def vmem():
    return pl.BlockSpec(memory_space=pltpu.VMEM)


def params(mib):
    return pltpu.CompilerParams(vmem_limit_bytes=mib * MB)


def cost(flops, moved):
    return pl.CostEstimate(flops=int(flops), bytes_accessed=int(moved), transcendentals=0)


def halves(value):
    high = value.astype(BF16)
    low = (value - high.astype(F32)).astype(BF16)
    return (high, low)


def dot_of(left, right, dims=((1,), (0,))):
    return lax.dot_general(left, right, (dims, ((), ())), preferred_element_type=F32)


def dot3(left, right, dims=((1,), (0,))):
    return dot_of(left[0], right[0], dims) + (
        dot_of(left[0], right[1], dims) + dot_of(left[1], right[0], dims)
    )


def down(row):
    size = row.shape[-1]
    return jnp.transpose(jnp.broadcast_to(row, (size, size)))


def normalized(ref):
    rows = ref[...]
    return rows / jnp.sum(rows, axis=1, keepdims=True)


def pick(rows, member, leg):
    return rows[3 * member + leg : 3 * member + leg + 1]


def level(rows):
    return jnp.full((1, rows.shape[-1]), 1.0 / rows.shape[-1], F32)


def from_mate(mate, place):
    return jnp.where(place == 0, pick(mate, 0, 2), pick(mate, 1, 2))


def inner_incoming(info, own, mate):
    odd = info[0, CORE] == 1
    place = jnp.where(odd, info[0, MATE0], info[0, MATE1])
    joined = place == info[0, CORE]
    chain = jnp.where(odd, pick(mate, 1, 1), pick(mate, 0, 0))
    gated = jnp.where(odd, pick(mate, 1, 2), pick(mate, 0, 2))
    near = chain + jnp.where(joined, gated, 0.0)
    home = jnp.where(odd, pick(own, 1, 0), pick(own, 0, 1))
    third = from_mate(mate, place) + jnp.where(joined, chain, 0.0)
    return (
        jnp.where(odd, near, home),
        jnp.where(odd, home, near),
        jnp.where(place < 0, level(own), third),
    )


def outer_known(info, own, mate):
    odd = info[0, CORE] == 1
    place = jnp.where(odd, info[0, MATE1], info[0, MATE0])
    home = jnp.where(odd, pick(own, 0, 1), pick(own, 1, 0))
    return (home, jnp.where(place < 0, level(own), from_mate(mate, place)))


def outer_far(info, side):
    far = jnp.where(info[0, CORE] == 1, pick(side, 0, 0), pick(side, 1, 1))
    return jnp.where(info[0, FIRST] + info[0, LAST] > 0, level(side), far)


def outer_incoming(info, own, mate, side):
    odd = info[0, CORE] == 1
    home, third = outer_known(info, own, mate)
    far = outer_far(info, side)
    return (jnp.where(odd, home, far), jnp.where(odd, far, home), third)


def hbm():
    return pl.BlockSpec(memory_space=pltpu.HBM)


def anywhere():
    return pl.BlockSpec(memory_space=pl.ANY)


def scalars_kernel(after, near, ranks, out_ref):
    device, row = (lax.axis_index("site"), lax.axis_index("row"))
    core = lax.rem(device, 2)
    base = 2 * (device - core)
    even0, even1 = (near[2, base] - base, near[2, base + 1] - base)
    odd0, odd1 = (near[2, base + 2], near[2, base + 3])
    odd = core == 1
    crossed = jnp.logical_or(even0 == 3, even1 == 2)
    kept = jnp.where(jnp.logical_and(odd, crossed), 1 - row, row)
    site = 2 * device + kept
    values = {
        CORE: core,
        ROW: row,
        MATE0: jnp.where(odd, jnp.where(odd0 < 0, -1, odd0 - base), jnp.maximum(even0 - 2, -1)),
        MATE1: jnp.where(odd, jnp.where(odd1 < 0, -1, odd1 - base), jnp.maximum(even1 - 2, -1)),
        FIRST: (device == 0).astype(jnp.int32),
        LAST: (device == lax.axis_size("site") - 1).astype(jnp.int32),
        KEPT: kept,
        RANK: ranks[site],
        GATED: (near[2, site] >= 0).astype(jnp.int32),
    }
    lanes = lax.broadcasted_iota(jnp.int32, out_ref.shape, 1)
    total = jnp.zeros(out_ref.shape, jnp.int32)
    for place, value in values.items():
        total = jnp.where(lanes == place, value, total)
    out_ref[...] = total


def scalars_call(after, near, ranks):
    return pl.pallas_call(
        scalars_kernel,
        in_specs=[anywhere(), smem(), smem()],
        out_specs=vmem(),
        out_shape=jax.ShapeDtypeStruct((8, 128), jnp.int32),
        compiler_params=params(4),
        cost_estimate=cost(1024, 1 << 20),
        name="scalars",
    )(after, near, ranks)


def add_kernel(one_ref, two_ref, after, out_ref):
    out_ref[...] = one_ref[...] + two_ref[...]


def add_call(one, two, after):
    return pl.pallas_call(
        add_kernel,
        in_specs=[vmem(), vmem(), anywhere()],
        out_specs=vmem(),
        out_shape=jax.ShapeDtypeStruct(one.shape, F32),
        compiler_params=params(4),
        cost_estimate=cost(one.size, 12 * one.size),
        name="add",
    )(one, two, after)


def open_kernel(x_hbm, x_ref, s_ref, out_ref, pairs_ref, sums_ref, total_ref, sems):
    members, rows, wide, bond = x_hbm.shape
    steps = sems.shape[0]
    per = steps // members
    block = rows // per

    def fetch(step):
        place = (step // per, pl.ds(lax.rem(step, per) * block, block))
        return pltpu.make_async_copy(x_hbm.at[place], x_ref.at[place], sems.at[step])

    for step in range(steps):
        fetch(step).start()
    total_ref[...] = jnp.zeros(total_ref.shape, F32)
    down_index = lax.broadcasted_iota(jnp.int32, (bond, wide), 0)
    across_index = lax.broadcasted_iota(jnp.int32, (bond, wide), 1)
    pairs_ref[...] = (across_index // 2 == down_index).astype(F32).astype(BF16)

    def body(step, carry):
        fetch(step).wait()
        member, start = (step // per, lax.rem(step, per) * block)
        total = total_ref[member]
        for index in range(0, block, 2):
            places = [start + index, start + index + 1]
            both = jnp.concatenate([x_ref[member, place] for place in places], axis=1)
            both = dot_of(pairs_ref[...], both * both)
            for place, square in zip(places, (both[:, :bond], both[:, bond:])):
                s_ref[member, place] = square.astype(BF16)
                sums_ref[member, place] = jnp.sum(square.reshape(bond // 8, 8, bond), axis=0)
                total = total + square
        total_ref[member] = total
        return carry

    lax.fori_loop(0, steps, body, 0)
    row = lax.axis_index("row")
    flat_weight = jnp.ones((1, bond), F32)
    out_ref[...] = jnp.ones(out_ref.shape, F32)
    for member in range(members):
        finish(row, out_ref, member, sums_ref[member], total_ref[member], flat_weight, None)


def open_call(x):
    members, rows, wide, bond = x.shape
    block = 16
    steps = members * rows // block
    return pl.pallas_call(
        open_kernel,
        in_specs=[hbm()],
        out_specs=[vmem(), vmem(), vmem()],
        out_shape=[
            jax.ShapeDtypeStruct(x.shape, BF16),
            jax.ShapeDtypeStruct((members, rows, bond, bond), BF16),
            jax.ShapeDtypeStruct((8, bond), F32),
        ],
        scratch_shapes=[
            pltpu.VMEM((bond, wide), BF16),
            pltpu.VMEM((members, rows, 8, bond), F32),
            pltpu.VMEM((members, bond, bond), F32),
            pltpu.SemaphoreType.DMA((steps,)),
        ],
        compiler_params=params(38),
        cost_estimate=cost(4 * x.size, 5 * x.size),
        name="open",
    )(x)


def flatten_kernel(after, x_ref, flat_ref, scratch):
    members, rows, bond = flat_ref.shape[:3]
    for member in range(members):

        def body(index, carry):
            lane = scratch.at[lax.rem(index, scratch.shape[0])]
            lane[...] = x_ref[member, index].astype(F32)
            parts = [lane[pl.ds(place, bond, 2), :] for place in range(2)]
            flat_ref[member, index] = jnp.concatenate(parts, axis=1).astype(BF16)
            return carry

        lax.fori_loop(0, rows, body, 0, unroll=8)


def flatten_call(after, x):
    members, rows, wide, bond = x.shape
    return pl.pallas_call(
        flatten_kernel,
        in_specs=[anywhere(), vmem()],
        out_specs=vmem(),
        out_shape=jax.ShapeDtypeStruct((members, rows, bond, wide), BF16),
        scratch_shapes=[pltpu.VMEM((8, wide, bond), F32)],
        compiler_params=params(8),
        cost_estimate=cost(2 * x.size, 4 * x.size),
        name="flatten",
    )(after, x)


def halved(row_index, row):
    half = row.shape[1] // 2
    return jnp.where(row_index == 0, row[:, :half], row[:, half:])


def placed(row_index, half):
    empty = jnp.zeros_like(half)
    return jnp.where(
        row_index == 0,
        jnp.concatenate([half, empty], axis=1),
        jnp.concatenate([empty, half], axis=1),
    )


def by_row(row, matrix):
    return dot3(halves(jnp.broadcast_to(row, (16, row.shape[1]))), halves(matrix))[:1]


def by_column(row, matrix):
    return dot3(halves(jnp.broadcast_to(row, (16, row.shape[1]))), halves(matrix), ((1,), (1,)))[:1]


def put_leg(out_ref, member, leg, row):
    out_ref[pl.ds(3 * member + leg, 1), :] = row


def finish(row_index, out_ref, member, sums, total, third, second_down):
    bond = total.shape[0]
    half = by_column(jnp.ones((1, bond), F32), jnp.sum(sums, axis=1))
    weighted = total if second_down is None else total * second_down
    put_leg(out_ref, member, 0, placed(row_index, half))
    put_leg(out_ref, member, 1, by_column(third, total))
    put_leg(out_ref, member, 2, jnp.sum(weighted, axis=0, keepdims=True))


GROUP = 4


def scaled_sum(s_ref, member, step, first_ref, start):
    bond = s_ref.shape[2]
    joined = None
    for place in range(GROUP):
        index = step * GROUP + place
        scale = jnp.broadcast_to(first_ref[pl.ds(start + index, 1), :], (16, bond)).astype(BF16)
        term = jnp.concatenate([scale] * (bond // 16), axis=0) * s_ref[member, index]
        joined = term if joined is None else joined + term
    return joined.astype(F32)


def contract_inner(info, weights, s_ref, out_ref, first_ref, sums_ref):
    rows, bond = s_ref.shape[1:3]
    member = 1 - info[0, CORE]
    start = info[0, ROW] * rows
    first, second, third = weights
    third = third.astype(BF16).astype(F32)
    first_ref[...] = down(first)
    second_down = down(second)
    outer = (second_down * third).astype(BF16)

    def body(step, total):
        for place in range(GROUP):
            index = step * GROUP + place
            piece = s_ref[member, index] * outer
            piece = piece[:64] + piece[64:]
            piece = (piece[:32] + piece[32:]).astype(F32)
            sums_ref[index] = (piece[:8] + piece[8:16]) + (piece[16:24] + piece[24:])
        return total + scaled_sum(s_ref, member, step, first_ref, start)

    total = lax.fori_loop(0, rows // GROUP, body, jnp.zeros((bond, bond), F32), unroll=2)
    finish(info[0, ROW], out_ref, member, sums_ref[...], total, third, second_down)


def contract_outer(info, home, third, s_ref, out_ref, mixed_ref, other_ref, first_ref):
    rows, bond = s_ref.shape[1:3]
    member = info[0, CORE]
    odd = info[0, CORE] == 1
    start = info[0, ROW] * rows
    third_rows = jnp.broadcast_to(third.astype(BF16), (8, bond))

    def mix(step, carry):
        pair = s_ref[member, pl.ds(2 * step, 2)].reshape(2 * bond, bond)
        product = dot_of(third_rows, pair, ((1,), (1,)))
        mixed_ref[pl.ds(2 * step, 1), :] = product[:1, :bond]
        mixed_ref[pl.ds(2 * step + 1, 1), :] = product[:1, bond:]
        return carry

    lax.fori_loop(0, rows // 2, mix, 0, unroll=8)

    @pl.when(odd)
    def over_first():
        first_ref[...] = down(home)

        def body(step, total):
            return total + scaled_sum(s_ref, member, step, first_ref, start)

        zero = jnp.zeros((bond, bond), F32)
        other_ref[...] = lax.fori_loop(0, rows // GROUP, body, zero, unroll=2)
        put_leg(out_ref, member, 1, by_row(halved(info[0, ROW], home), mixed_ref[...]))

    @pl.when(jnp.logical_not(odd))
    def over_second():
        second_rows = jnp.concatenate(halves(home) + (jnp.zeros((6, bond), BF16),), axis=0)

        def body(step, carry):
            pair = jnp.concatenate([s_ref[member, 2 * step], s_ref[member, 2 * step + 1]], axis=1)
            product = dot_of(second_rows, pair)
            product = product[:1] + product[1:2]
            other_ref[pl.ds(2 * step, 1), :] = product[:, :bond]
            other_ref[pl.ds(2 * step + 1, 1), :] = product[:, bond:]
            return carry

        lax.fori_loop(0, rows // 2, body, 0, unroll=8)
        put_leg(out_ref, member, 0, placed(info[0, ROW], by_column(home, mixed_ref[...])))


def inner_kernel(info, own_ref, mate_ref, s_ref, out_ref, mixed_ref, other_ref, first_ref, sums_ref):
    own, mate = (normalized(own_ref), normalized(mate_ref))
    out_ref[...] = jnp.ones(out_ref.shape, F32)
    contract_inner(info, inner_incoming(info, own, mate), s_ref, out_ref, first_ref, sums_ref)
    home, third = outer_known(info, own, mate)
    contract_outer(info, home, third, s_ref, out_ref, mixed_ref, other_ref, first_ref)


def outer_kernel(info, side_ref, part_ref, mixed_ref, other_ref, out_ref):
    rows = mixed_ref.shape[0]
    far = outer_far(info, normalized(side_ref))
    out_ref[...] = part_ref[...]

    @pl.when(info[0, CORE] == 1)
    def as_second():
        put_leg(out_ref, 1, 0, placed(info[0, ROW], by_column(far, mixed_ref[...])))
        put_leg(out_ref, 1, 2, by_row(far, other_ref[...]))

    @pl.when(info[0, CORE] == 0)
    def as_first():
        half = halved(info[0, ROW], far)
        both = by_row(half, jnp.concatenate([mixed_ref[...], other_ref[:rows]], axis=1))
        bond = mixed_ref.shape[1]
        put_leg(out_ref, 0, 1, both[:, :bond])
        put_leg(out_ref, 0, 2, both[:, bond:])


def inner_call(info, own, mate, squares):
    rows, bond = squares.shape[1:3]
    return pl.pallas_call(
        inner_kernel,
        in_specs=[vmem(), vmem(), vmem(), vmem()],
        out_specs=[vmem(), vmem(), vmem()],
        out_shape=[
            jax.ShapeDtypeStruct((8, bond), F32),
            jax.ShapeDtypeStruct((rows, bond), F32),
            jax.ShapeDtypeStruct((bond, bond), F32),
        ],
        scratch_shapes=[pltpu.VMEM((bond, bond), F32), pltpu.VMEM((rows, 8, bond), F32)],
        compiler_params=params(8),
        cost_estimate=cost(4 * squares.size, 2 * squares.size),
        name="inner_round",
    )(info, own, mate, squares)


def outer_call(info, side, part, mixed, other):
    return pl.pallas_call(
        outer_kernel,
        in_specs=[vmem(), vmem(), vmem(), vmem(), vmem()],
        out_specs=vmem(),
        out_shape=jax.ShapeDtypeStruct(part.shape, F32),
        compiler_params=params(8),
        cost_estimate=cost(8 * mixed.size, 8 * mixed.size),
        name="outer_round",
    )(info, side, part, mixed, other)


def add_gram(info, member, weights, d_ref, first_ref, gram):
    rows, bond = d_ref.shape[1:3]
    block = 64
    start = info[0, ROW] * rows
    first_ref[...] = down(jnp.sqrt(weights[0]))
    second = down(jnp.sqrt(weights[1]))
    gram[...] = jnp.zeros(gram.shape, F32)

    def body(step, carry):
        parts = []
        for place in range(block):
            index = step * block + place
            scale = first_ref[pl.ds(start + index, 1), :] * second
            piece = d_ref[member, index].astype(F32) * jnp.concatenate([scale, scale], axis=1)
            parts.append(piece.astype(BF16))
        weighted = jnp.concatenate(parts, axis=0)
        gram[...] += dot_of(weighted, weighted, ((0,), (0,)))
        return carry

    lax.fori_loop(0, rows // block, body, 0)


def gram_weights(info, member, own_ref, mate_ref, side_ref):
    own, mate, side = (normalized(own_ref), normalized(mate_ref), normalized(side_ref))
    inner = inner_incoming(info, own, mate)
    outer = outer_incoming(info, own, mate, side)
    return [jnp.where(member == info[0, CORE], outer[leg], inner[leg]) for leg in range(2)]


def send_kernel(info, own_ref, mate_ref, side_ref, d_ref, out_ref, first_ref, gram):
    bond = d_ref.shape[2]
    member = 1 - info[0, KEPT]
    weights = gram_weights(info, member, own_ref, mate_ref, side_ref)
    add_gram(info, member, weights, d_ref, first_ref, gram)
    corner, above, below = (gram[:bond, :bond], gram[:bond, bond:], gram[bond:, bond:])
    out_ref[:bond] = jnp.where(below_diagonal(bond), below, corner)
    out_ref[bond : 2 * bond] = above
    diagonal = jnp.sum(jnp.where(eye_mask(bond), below, 0.0), axis=0, keepdims=True)
    out_ref[2 * bond :] = jnp.broadcast_to(diagonal, (8, bond))


def keep_kernel(info, own_ref, mate_ref, side_ref, d_ref, after, out_ref, msg_ref, first_ref, gram):
    bond = d_ref.shape[2]
    member = info[0, KEPT]
    weights = gram_weights(info, member, own_ref, mate_ref, side_ref)
    own = normalized(own_ref)
    for place in range(2):
        for leg in range(3):
            msg_ref[leg, pl.ds(place, 1), :] = pick(own, place, leg)
    add_gram(info, member, weights, d_ref, first_ref, gram)
    out_ref[0] = gram[:bond, :bond]
    out_ref[1] = gram[:bond, bond:]
    out_ref[2] = gram[bond:, bond:]


def gram_call(kernel, name, extra_specs, out_specs, out_shape, flat, operands):
    rows, bond, wide = flat.shape[1:]
    return pl.pallas_call(
        kernel,
        in_specs=[vmem()] + [vmem()] * 4 + extra_specs,
        out_specs=out_specs,
        out_shape=out_shape,
        scratch_shapes=[pltpu.VMEM((bond, bond), F32), pltpu.VMEM((wide, wide), F32)],
        compiler_params=params(20),
        cost_estimate=cost(wide * flat.size, flat.size),
        name=name,
    )(*operands)


def send_call(info, own, mate, side, flat):
    bond = flat.shape[2]
    shape = jax.ShapeDtypeStruct((2 * bond + 8, bond), F32)
    operands = (info, own, mate, side, flat)
    return gram_call(send_kernel, "gram_to_send", [], vmem(), shape, flat, operands)


def keep_call(info, own, mate, side, flat, after):
    members, _, bond, _ = flat.shape
    shapes = [
        jax.ShapeDtypeStruct((3, bond, bond), F32),
        jax.ShapeDtypeStruct((3, members, bond), F32),
    ]
    operands = (info, own, mate, side, flat, after)
    return gram_call(keep_kernel, "gram_to_keep", [anywhere()], [vmem(), vmem()], shapes, flat, operands)


def eye_mask(size):
    down_index = lax.broadcasted_iota(jnp.int32, (size, size), 0)
    across_index = lax.broadcasted_iota(jnp.int32, (size, size), 1)
    return down_index == across_index


def below_diagonal(size):
    down_index = lax.broadcasted_iota(jnp.int32, (size, size), 0)
    return down_index > lax.broadcasted_iota(jnp.int32, (size, size), 1)


def root_sweeps(matrix):
    size = matrix.shape[0]
    diagonal = eye_mask(size)
    lift = jnp.where(diagonal, 1.5, 0.0).astype(F32)
    scale = jnp.sum(jnp.where(diagonal, matrix, 0.0), keepdims=True)
    current = matrix / scale
    poly = lift - 0.5 * current
    poly_parts = halves(poly)
    current = dot3(halves(current), poly_parts)
    partner = poly
    yield None
    for _ in range(SWEEPS - 1):
        current_parts, partner_parts = (halves(current), halves(partner))
        poly_parts = halves(lift - 0.5 * dot3(partner_parts, current_parts))
        current = dot3(current_parts, poly_parts)
        partner = dot3(poly_parts, partner_parts)
        yield None
    root_scale = jnp.sqrt(scale)
    yield (current * root_scale, partner / root_scale)


def root_pair(matrix):
    for result in root_sweeps(matrix):
        pass
    return result


def root_kernel(keep_ref, got_ref, upper_ref, inverse_ref):
    bond = keep_ref.shape[1]
    merged = got_ref[:bond]
    flipped = jnp.transpose(merged)
    lower = below_diagonal(bond)
    got_below = jnp.where(eye_mask(bond), got_ref[2 * bond : 2 * bond + 1], jnp.where(lower, merged, flipped))
    corner = keep_ref[0] + jnp.where(lower, flipped, merged)
    above = keep_ref[1] + got_ref[bond : 2 * bond]
    below = keep_ref[2] + got_below
    matrix = jnp.concatenate(
        [
            jnp.concatenate([corner, above], axis=1),
            jnp.concatenate([jnp.transpose(above), below], axis=1),
        ],
        axis=0,
    )
    upper_ref[...], inverse_ref[...] = root_pair(matrix)


def root_call(keep, got):
    wide = 2 * keep.shape[1]
    full = jax.ShapeDtypeStruct((wide, wide), F32)
    return pl.pallas_call(
        root_kernel,
        in_specs=[vmem(), vmem()],
        out_specs=[vmem(), vmem()],
        out_shape=[full, full],
        compiler_params=params(16),
        cost_estimate=cost(66 * 2 * wide**3, 16 * wide * wide),
        name="root",
    )(keep, got)


def truncate_kernel(info, gate, own_ref, mate_ref, upper_ref, inverse_ref, other_ref, probes_ref, out_ref):
    wide, bond = (upper_ref.shape[0], probes_ref.shape[1])
    odd = info[0, CORE] == 1
    kept = info[0, KEPT]
    mate_place = jnp.maximum(jnp.where(kept == 0, info[0, MATE0], info[0, MATE1]), 0)
    own_msg = own_ref[pl.ds(3 * kept + 2, 1), :]
    mate_msg = mate_ref[pl.ds(3 * mate_place + 2, 1), :]
    own_msg = own_msg / jnp.sum(own_msg, axis=1, keepdims=True)
    mate_msg = mate_msg / jnp.sum(mate_msg, axis=1, keepdims=True)
    strength = bond * jnp.sqrt(own_msg * mate_msg)
    own_upper, other_upper = (upper_ref[...], other_ref[...])
    left = jnp.where(odd, other_upper, own_upper)
    right = jnp.where(odd, own_upper, other_upper)
    left_parts, right_parts = (halves(left), halves(right))

    def block(value, down_half, across_half):
        return value[
            down_half * bond : (down_half + 1) * bond, across_half * bond : (across_half + 1) * bond
        ]

    def combined(value, entry):
        block_rows = []
        for out_down in range(2):
            blocks = []
            for out_across in range(2):
                total = None
                for first in range(2):
                    for second in range(2):
                        term = entry(out_down, out_across, first, second) * block(value, first, second)
                        total = term if total is None else total + term
                blocks.append(total * strength_down)
            block_rows.append(jnp.concatenate(blocks, axis=1))
        return jnp.concatenate(block_rows, axis=0)

    across = lax.broadcasted_iota(jnp.int32, (1, bond), 1)
    mask = (across < info[0, RANK]).astype(F32)
    strength_down = down(strength)
    probes = jnp.concatenate(
        [probes_ref[pl.ds(0, wide, 2), :] * mask, probes_ref[pl.ds(1, wide, 2), :] * mask], axis=1
    )
    probed = combined(
        dot3(right_parts, halves(probes)),
        lambda s, s_out, t, t_out: gate[2 * s_out + t_out, 2 * s + t],
    )
    sampled = dot3(left_parts, halves(probed))
    sampled_parts = halves(jnp.concatenate([sampled[:, :bond], sampled[:, bond:]], axis=0))
    inner = dot3(sampled_parts, sampled_parts, ((0,), (0,)))
    inner = inner + jnp.where(eye_mask(bond), 1.0 - mask, 0.0)
    sweeps = root_sweeps(inner)
    next(sweeps)
    based = dot3(left_parts, halves(sampled))
    next(sweeps)
    based = combined(based, lambda t, t_out, s, s_out: gate[2 * s_out + t_out, 2 * s + t])
    next(sweeps)
    next(sweeps)
    coeffs = dot3(right_parts, halves(based))
    next(sweeps)
    next(sweeps)
    target = dot3(halves(inverse_ref[...]), halves(jnp.where(odd, coeffs, sampled)))
    for result in sweeps:
        pass
    inner_inverse = result[1]
    inner_parts = halves(inner_inverse)

    def rooted(value):
        return [dot3(halves(value[:, :bond]), inner_parts), dot3(halves(value[:, bond:]), inner_parts)]

    squares = sum(jnp.sum(part * part, axis=0, keepdims=True) for part in rooted(coeffs))
    new_bond = jnp.sqrt(squares / (2 * wide) + 1e-06)
    divisor = jnp.where(odd, new_bond, 1.0)
    change = jnp.concatenate([part / divisor for part in rooted(target)], axis=1)
    gated = info[0, GATED] == 1
    identity = eye_mask(wide).astype(F32)
    out_ref[:wide] = jnp.where(gated, change, identity).astype(BF16)
    bond_parts = halves(jnp.where(gated, new_bond, 0.0))
    out_ref[wide:] = jnp.broadcast_to(jnp.concatenate(bond_parts, axis=1), (16, wide))


def truncate_call(info, gate, own, mate, upper, inverse, other, probes):
    wide = upper.shape[0]
    return pl.pallas_call(
        truncate_kernel,
        in_specs=[vmem()] * 8,
        out_specs=vmem(),
        out_shape=jax.ShapeDtypeStruct((wide + 16, wide), BF16),
        compiler_params=params(32),
        cost_estimate=cost(40 * 2 * wide**3, 24 * wide * wide),
        name="truncate",
    )(info, gate, own, mate, upper, inverse, other, probes)


def update_member(member, pack_ref, d_ref, out_hbm, held, scratch, sems):
    rows, bond, wide = d_ref.shape[1:]
    slots, block = held.shape[:2]
    steps = rows // block

    def put(step):
        slot = step % slots
        target = out_hbm.at[member, pl.ds(step * block, block)]
        return pltpu.make_async_copy(held.at[slot], target, sems.at[slot])

    change = pack_ref[:wide]
    for step in range(steps):
        slot = step % slots
        if step >= slots:
            put(step - slots).wait()
        for index in range(block):
            if index % 4 == 0:
                rows_in = d_ref[member, pl.ds(step * block + index, 4)].reshape(4 * bond, wide)
                result = dot_of(rows_in, change)
            lane = scratch.at[index % scratch.shape[0]]
            piece = result[index % 4 * bond : (index % 4 + 1) * bond]
            lane[pl.ds(0, bond, 2), :] = piece[:, :bond]
            lane[pl.ds(1, bond, 2), :] = piece[:, bond:]
            held[slot, index] = lane[...].astype(BF16)
        put(step).start()
    for step in range(steps - slots, steps):
        put(step).wait()


def own_kernel(info, pack_ref, d_ref, after, out_hbm, held, scratch, sems):
    update_member(info[0, KEPT], pack_ref, d_ref, out_hbm, held, scratch, sems)


def other_kernel(info, pack_ref, got_ref, d_ref, begun_hbm, out_hbm, bond_hbm, held, scratch, sems, bond_ref, bond_sem):
    bond, wide = d_ref.shape[2:]
    kept = info[0, KEPT]
    tail = pack_ref[wide:].astype(F32)
    got = got_ref[wide:].astype(F32)
    mine = tail[:1, :bond] + tail[:1, bond:]
    other = got[:1, :bond] + got[:1, bond:]
    bond_ref[pl.ds(0, 1), :] = jnp.where(kept == 0, mine, other)
    bond_ref[pl.ds(1, 1), :] = jnp.where(kept == 0, other, mine)
    bond_copy = pltpu.make_async_copy(bond_ref, bond_hbm, bond_sem)
    bond_copy.start()
    update_member(1 - kept, got_ref, d_ref, out_hbm, held, scratch, sems)
    bond_copy.wait()


def update_call(kernel, name, in_specs, aliases, with_bonds, flat, operands):
    members, rows, bond, wide = flat.shape
    block, slots = (8, 8)
    tensor = jax.ShapeDtypeStruct((members, rows, wide, bond), BF16)
    bonds = jax.ShapeDtypeStruct((members, bond), F32)
    return pl.pallas_call(
        kernel,
        in_specs=in_specs,
        out_specs=[hbm(), hbm()] if with_bonds else hbm(),
        out_shape=[tensor, bonds] if with_bonds else tensor,
        input_output_aliases=aliases,
        scratch_shapes=[
            pltpu.VMEM((slots, block, wide, bond), BF16),
            pltpu.VMEM((4, wide, bond), F32),
            pltpu.SemaphoreType.DMA((slots,)),
        ]
        + ([pltpu.VMEM((members, bond), F32), pltpu.SemaphoreType.DMA(())] if with_bonds else []),
        compiler_params=params(24),
        cost_estimate=cost(wide * flat.size, 2 * flat.size),
        name=name,
    )(*operands)


def own_call(info, pack, flat, after):
    specs = [vmem(), vmem(), vmem(), anywhere()]
    return update_call(own_kernel, "update_own", specs, {}, False, flat, (info, pack, flat, after))


def other_call(info, pack, got, flat, begun):
    specs = [vmem(), vmem(), vmem(), vmem(), hbm()]
    operands = (info, pack, got, flat, begun)
    return update_call(other_kernel, "update_other", specs, {4: 0}, True, flat, operands)


def shards(tensors, neighbours, edge_ranks, gate_matrix, probes):
    members, rows, bond, phys = tensors.shape[:4]
    sites = lax.axis_size("site")
    row_swap = [(0, 1), (1, 0)]
    core_swap = [(i, i ^ 1) for i in range(sites)]
    side_swap = [(i, i + 1) for i in range(1, sites - 1, 2)]
    side_swap += [(j, i) for i, j in side_swap]
    x = tensors.reshape(members, rows, bond * phys, bond)
    x, squares, part = open_call(x)
    info = scalars_call(part, neighbours.T, edge_ranks)
    for index in range(ROUNDS):
        if index > 0:
            begun = inner_call(info, own, mate, squares)
            part = outer_call(info, side, *begun)
        got = lax.ppermute(part, "row", row_swap)
        own = part + got if index > 0 else add_call(part, got, info)
        side = lax.ppermute(own, "site", side_swap)
        mate = lax.ppermute(own, "site", core_swap)
    flat = flatten_call(own, x)
    send = send_call(info, own, mate, side, flat)
    got = lax.ppermute(send, "row", row_swap)
    keep, messages = keep_call(info, own, mate, side, flat, send)
    upper, inverse = root_call(keep, got)
    other = lax.ppermute(upper, "site", core_swap)
    pack = truncate_call(info, gate_matrix, own, mate, upper, inverse, other, probes)
    got_pack = lax.ppermute(pack, "row", row_swap)
    begun = own_call(info, pack, flat, pack)
    updated, bonds = other_call(info, pack, got_pack, flat, begun)
    return (updated.reshape(tensors.shape), messages.transpose(1, 0, 2), bonds)


def solution(mesh):
    return jax.shard_map(
        shards,
        mesh=mesh,
        in_specs=(P("site", "row", None, None, None), P(), P(), P(), P()),
        out_specs=(P("site", "row", None, None, None), P("site", None, None), P("site", None)),
        check_vma=False,
    )
```
